256 devices in a mesh: ctx: 16 (over z_hi, x), head: 16 (over y, z_lo, core).
Axes of the slice: x: 4, y: 4, z: 8 (z_hi: 4, z_lo: 2; z = z_hi * 2 + z_lo), core: 2. Of those that a mesh axis runs over, the one named last changes fastest.
Arguments:
- queries: bfloat16 [2048, 12288], P('ctx', 'head'), may hold values from -12 to 12
- latent: bfloat16 [2048, 512], P('ctx'), may hold values from -6 to 6
- rope_key: bfloat16 [2048, 64], P('ctx'), may hold values from -12 to 12
- key_weight: bfloat16 [512, 8192], P(None, 'head'), may hold values from -0.25 to 0.25
- value_weight: bfloat16 [512, 8192], P(None, 'head'), may hold values from -0.25 to 0.25
- lambda_pair: float32 [32], P('head'), may hold values from 0.2 to 0.8
- norm_gain: float32 [8192], P('head'), may hold values from 0.1 to 1.9
- out_grad: bfloat16 [2048, 8192], P('ctx', 'head'), may hold values from -6 to 6
- block_order: int32 [32], replicated, may hold values from 0 to 31, as said below
Outputs:
- query_grad: bfloat16 [2048, 12288], P('ctx', 'head')
- latent_grad: bfloat16 [2048, 512], P('ctx')
- rope_grad: bfloat16 [2048, 64], P('ctx')
The draws below stay inside these ranges and needn't reach their ends.
Inputs may be any that keep to these rules, and one draw needn't show every extreme that they name: `block_order`: slots 2d and 2d + 1 hold blocks b and 31 - b with b < 16; every block appears once.
All inputs are finite; a program needn't handle non-finite values.
Results may differ from the reference program's by a relative error of at most 0.03.
Values may be sent and summed in bfloat16 or wider, within the bound.
A program may use at most 64 MiB of HBM per device.

```python
import jax
import jax.numpy as jnp
from jax import lax

D_LAT = 512
D_NOPE = 128
D_ROPE = 64
VALUE_WIDTH = 128
TOKENS_PER_SHARD = 128
PAIRS = 32
HEADS = 64
SEQUENCE_TOKENS = 2048
HALF = 64
N_CTX = 16


def draw_queries(key, part):
    key = jax.random.fold_in(key, 3)
    shape_full = (SEQUENCE_TOKENS // 8, 8, HEADS, D_NOPE + D_ROPE)
    values_drawn = jnp.clip(jax.random.normal(key, shape_full, jnp.float32), -6.0, 6.0)
    return values_drawn.reshape(SEQUENCE_TOKENS, HEADS * (D_NOPE + D_ROPE)).astype(jnp.bfloat16)


def draw_rope_key(key, part):
    key = jax.random.fold_in(key, 5)
    shape_full = (SEQUENCE_TOKENS // 8, 8, D_ROPE)
    values_drawn = jnp.clip(jax.random.normal(key, shape_full, jnp.float32), -6.0, 6.0)
    return values_drawn.reshape(SEQUENCE_TOKENS, D_ROPE).astype(jnp.bfloat16)


def draw_block_order(key, part):
    key = jax.random.fold_in(key, 7)
    first_blocks = jax.random.permutation(key, N_CTX).astype(jnp.int32)
    return jnp.stack([first_blocks, 2 * N_CTX - 1 - first_blocks], axis=1).reshape(2 * N_CTX)


def steps_of(key, shape, pieces, least, high):
    def one(position, parts):
        draws = jax.random.uniform(jax.random.fold_in(jax.random.fold_in(key, 6), position), (parts,), jnp.float32, least / len(pieces), high / len(pieces))
        return jnp.repeat(jnp.exp(draws), shape[position] // parts).reshape((-1,) + (1,) * (len(shape) - position - 1))

    factor_of = one(*pieces[0])
    for cut in pieces[1:]:
        factor_of = factor_of * one(*cut)
    return factor_of


def scatter_about(key, shape, width, limit, cuts=(), kind=jnp.bfloat16):
    result = jax.random.normal(key, shape, jnp.float32) * width
    if len(cuts) > 0:
        result = steps_of(key, shape, cuts, -0.22, 0.18) * result
    return jnp.clip(result, min=-limit, max=limit).astype(kind)


def setup_inputs(seed: int = 0) -> dict:
    seeds = jax.random.split(jax.random.key(seed), 10)
    return {
        "queries": draw_queries(jax.random.fold_in(seeds[9], 71), 0),
        "latent": scatter_about(seeds[1], (SEQUENCE_TOKENS, D_LAT), 1.0, 6.0, ((0, 16),)),
        "rope_key": draw_rope_key(jax.random.fold_in(seeds[9], 71), 0),
        "key_weight": scatter_about(seeds[3], (D_LAT, HEADS * D_NOPE), D_LAT ** -0.5, 0.25, ((1, 16),)),
        "value_weight": scatter_about(seeds[4], (D_LAT, HEADS * VALUE_WIDTH), D_LAT ** -0.5, 0.25, ((1, 16),)),
        "lambda_pair": jnp.clip(0.2 + 0.6 * jax.random.uniform(seeds[5], (PAIRS,), jnp.float32) ** steps_of(seeds[5], (PAIRS,), ((0, 16),), -0.2, 0.2), 0.2, 0.8),
        "norm_gain": jnp.clip(1.0 + 0.18 * jax.random.normal(seeds[6], (HEADS * VALUE_WIDTH,), jnp.float32), 0.1, 1.9),
        "out_grad": scatter_about(seeds[7], (SEQUENCE_TOKENS, HEADS * VALUE_WIDTH), 1.0, 6.0, ((0, 16), (1, 16))),
        "block_order": draw_block_order(jax.random.fold_in(seeds[9], 71), 0),
    }


eps = 1e-06

def positions_of(block_order):
    row_index = jnp.arange(SEQUENCE_TOKENS, dtype=jnp.int32)
    return block_order[row_index // HALF] * HALF + row_index % HALF

def kept_rounding(member):
    return lax.optimization_barrier(member.astype(jnp.bfloat16)).astype(jnp.float32)

def reference(queries, latent, rope_key, key_weight, value_weight, lambda_pair, norm_gain, out_grad, block_order):
    logit_scale = (D_NOPE + D_ROPE) ** (-0.5)
    query_key_width = D_NOPE + D_ROPE
    token_pos = positions_of(block_order)
    visible = token_pos[None, :] <= token_pos[:, None]
    key_nope = jnp.dot(latent, key_weight, preferred_element_type=jnp.float32).astype(jnp.bfloat16)
    key_values = jnp.dot(latent, value_weight, preferred_element_type=jnp.float32).astype(jnp.bfloat16)
    query_pairs = queries.reshape(SEQUENCE_TOKENS, PAIRS, 2, query_key_width).transpose(1, 2, 0, 3)
    nope_pairs = key_nope.reshape(SEQUENCE_TOKENS, PAIRS, 2, D_NOPE).transpose(1, 2, 0, 3)
    value_pairs = key_values.reshape(SEQUENCE_TOKENS, PAIRS, 2 * VALUE_WIDTH).transpose(1, 0, 2)
    grad_pairs = out_grad.reshape(SEQUENCE_TOKENS, PAIRS, 2 * VALUE_WIDTH).transpose(1, 0, 2)
    gain_pairs = norm_gain.reshape(PAIRS, 2 * VALUE_WIDTH)
    kweight_pairs = key_weight.reshape(D_LAT, PAIRS, 2 * D_NOPE).transpose(1, 0, 2)
    vweight_pairs = value_weight.reshape(D_LAT, PAIRS, 2 * VALUE_WIDTH).transpose(1, 0, 2)

    def one_pair(running, inputs):
        latent_sum, rope_sum = running
        query_couple, nope_pair, value_pair, grad_pair, gain_row, lambda_one, kweight_pair, vweight_pair = inputs
        maps_out = []
        probabilities = []
        keys_cat = []
        for mapped_position in range(2):
            keys_joined = jnp.concatenate([nope_pair[mapped_position], rope_key], axis=1)
            keys_cat.append(keys_joined)
            scores = logit_scale * jnp.dot(query_couple[mapped_position], keys_joined.T, preferred_element_type=jnp.float32)
            scores = jnp.where(visible, scores, -jnp.inf)
            row_top = lax.optimization_barrier(jnp.max(scores, axis=1, keepdims=True))
            weights = jnp.exp(scores - row_top)
            row_total = lax.optimization_barrier(jnp.sum(weights, axis=1, keepdims=True))
            maps_out.append(jnp.dot(weights.astype(jnp.bfloat16), value_pair, preferred_element_type=jnp.float32) / row_total)
            log_total = row_top + jnp.log(row_total)
            probabilities.append(jnp.exp(scores - log_total))
        factor = [1.0, -lambda_one]
        mixed_out = maps_out[0] - lambda_one * maps_out[1]
        root_mean = jnp.sqrt(lax.optimization_barrier(jnp.mean(mixed_out * mixed_out, axis=1, keepdims=True)) + eps)
        normed = mixed_out / root_mean
        scaled = grad_pair.astype(jnp.float32) * gain_row[None, :]
        d_mixed = (scaled - normed * lax.optimization_barrier(jnp.mean(scaled * normed, axis=1, keepdims=True))) / root_mean
        gradient_lowered = d_mixed.astype(jnp.bfloat16)
        through_values = jnp.dot(gradient_lowered, value_pair.T, preferred_element_type=jnp.float32)
        merged_scores = (probabilities[0] - lambda_one * probabilities[1]).astype(jnp.bfloat16)
        value_pieces_list = jnp.einsum('tfl,tfu->tlu', merged_scores.reshape(N_CTX, TOKENS_PER_SHARD, SEQUENCE_TOKENS).astype(jnp.float32), gradient_lowered.reshape(N_CTX, TOKENS_PER_SHARD, 2 * VALUE_WIDTH).astype(jnp.float32))
        value_sum = lax.optimization_barrier(jnp.sum(kept_rounding(value_pieces_list), axis=0))
        latent_term = jnp.dot(value_sum, vweight_pair.T.astype(jnp.float32), precision=lax.Precision.HIGHEST)
        query_out = []
        for mapped_position in range(2):
            delta_rows = factor[mapped_position] * lax.optimization_barrier(jnp.sum(d_mixed * maps_out[mapped_position], axis=1, keepdims=True))
            scores_gradient = (probabilities[mapped_position] * (factor[mapped_position] * through_values - delta_rows)).astype(jnp.bfloat16)
            query_out.append(logit_scale * jnp.dot(scores_gradient, keys_cat[mapped_position], preferred_element_type=jnp.float32))
            key_pieces_list = logit_scale * jnp.einsum('mzx,mzs->mxs', scores_gradient.reshape(N_CTX, TOKENS_PER_SHARD, SEQUENCE_TOKENS).astype(jnp.float32), query_couple[mapped_position].reshape(N_CTX, TOKENS_PER_SHARD, query_key_width).astype(jnp.float32))
            nope_sum = lax.optimization_barrier(jnp.sum(kept_rounding(key_pieces_list[:, :, :D_NOPE]), axis=0))
            weight_part = kweight_pair[:, mapped_position * D_NOPE:(mapped_position + 1) * D_NOPE]
            latent_term = latent_term + jnp.dot(nope_sum, weight_part.T.astype(jnp.float32), precision=lax.Precision.HIGHEST)
            rope_sum = rope_sum + lax.optimization_barrier(jnp.sum(key_pieces_list[:, :, D_NOPE:], axis=0))
        return ((latent_sum + latent_term, rope_sum), jnp.stack(query_out))
    start_sums = (jnp.zeros((SEQUENCE_TOKENS, D_LAT), jnp.float32), jnp.zeros((SEQUENCE_TOKENS, D_ROPE), jnp.float32))
    inputs = (query_pairs, nope_pairs, value_pairs, grad_pairs, gain_pairs, lambda_pair, kweight_pairs, vweight_pairs)
    (latent_sum, rope_sum), query_stack = lax.scan(one_pair, start_sums, inputs)
    query_grad = query_stack.transpose(2, 0, 1, 3).reshape(SEQUENCE_TOKENS, HEADS * query_key_width).astype(jnp.bfloat16)
    return (query_grad, latent_sum.astype(jnp.bfloat16), rope_sum.astype(jnp.bfloat16))
```

```python
import functools

import jax
import jax.numpy as jnp
from jax import lax
from jax.experimental import pallas as pl
from jax.experimental.pallas import tpu as pltpu
from jax.sharding import PartitionSpec as P

MESH = pl.DeviceIdType.MESH
D_LAT = 512
D_NOPE = 128
D_ROPE = 64
D_QK = D_NOPE + D_ROPE
PAIR_WIDTH = 256
ROWS = 128
WIDE = 640
HALF = 64
CHUNKS = 8
CHUNK = 256
PIECE = 16
MAPS = 4
PAIRS_DEV = 2
LOGIT_SCALE = D_QK**-0.5
LOG2E = 1.4426950408889634
EPS = 1e-6
F32 = jnp.float32
BF16 = jnp.bfloat16


class Place:
    def __init__(self):
        ctx, head = lax.axis_index("ctx"), lax.axis_index("head")
        self.x, self.zh = lax.rem(ctx, 4), lax.div(ctx, 4)
        self.y = lax.div(head, 4)
        self.zl = lax.rem(lax.div(head, 2), 2)
        self.c = lax.rem(head, 2)
        self.o = 1 - self.c
        self.first = self.y * self.o + self.x * self.c
        self.last = self.x * self.o + self.y * self.c

    def at(self, x=None, y=None, zh=None, zl=None, c=None):
        x = self.x if x is None else x
        y = self.y if y is None else y
        zh = self.zh if zh is None else zh
        zl = self.zl if zl is None else zl
        c = self.c if c is None else c
        return (zh * 4 + x, y * 4 + zl * 2 + c)

    def first_peer(self, d):
        return self.at(x=lax.rem(self.x + d * self.c, 4), y=lax.rem(self.y + d * self.o, 4))

    def last_peer(self, d):
        return self.at(x=lax.rem(self.x + d * self.o, 4), y=lax.rem(self.y + d * self.c, 4))

    def sibling(self):
        return self.at(c=self.o)


def remote(src, dst, send, recv, device):
    return pltpu.make_async_remote_copy(
        src_ref=src, dst_ref=dst, send_sem=send, recv_sem=recv, device_id=device, device_id_type=MESH
    )


def greet(devices, count):
    barrier = pltpu.get_barrier_semaphore()
    for device in devices:
        pl.semaphore_signal(barrier, inc=1, device_id=device, device_id_type=MESH)
    pl.semaphore_wait(barrier, count)


def gather_kernel(latent, rope, out, z_send, z_recv, f_send, f_recv, l_send, l_recv, s_send, s_recv):
    me = Place()
    base = me.c * 4
    row = pl.multiple_of(me.c * HALF + me.y * PIECE, PIECE)
    mine = out.at[base + me.last]
    mine[me.zh, me.first, :, 0:D_LAT] = latent[pl.ds(row, PIECE), :]
    mine[me.zh, me.first, :, D_LAT:WIDE] = jnp.concatenate(
        [rope[pl.ds(row, PIECE), :], jnp.zeros((PIECE, D_ROPE), BF16)], axis=1
    )
    step = 2 * me.zl - 1
    ahead = lax.rem(me.zh + step + 4, 4)
    behind = lax.rem(me.zh - step + 4, 4)
    across = lax.rem(me.zh + 2, 4)
    z_to = [me.at(zh=ahead, zl=0), me.at(zh=ahead, zl=1), me.at(zh=across, zl=1 - me.zl)]
    z_from = [
        me.at(zh=lax.rem(me.zh + 3, 4), zl=1),
        me.at(zh=lax.rem(me.zh + 1, 4), zl=0),
        me.at(zh=across, zl=1 - me.zl),
    ]
    firsts = [me.first_peer(d) for d in (1, 2, 3)]
    lasts = [me.last_peer(d) for d in (1, 2, 3)]
    greet(z_from + firsts + lasts + [me.sibling()], 10)

    sent = []
    for i, device in enumerate(z_to):
        piece = mine.at[me.zh, me.first]
        copy = remote(piece, piece, z_send.at[i], z_recv.at[me.zh], device)
        copy.start()
        sent.append(copy)
    for d in (1, 2, 3):
        other = lax.rem(me.zh + d, 4)
        piece = mine.at[other, me.first]
        remote(piece, piece, z_send.at[0], z_recv.at[other], z_to[0]).wait_recv()
    for i, device in enumerate(firsts):
        piece = mine.at[:, me.first]
        copy = remote(piece, piece, f_send.at[i], f_recv.at[me.first], device)
        copy.start()
        sent.append(copy)
    for d in (1, 2, 3):
        other = lax.rem(me.first + d, 4)
        piece = mine.at[:, other]
        remote(piece, piece, f_send.at[0], f_recv.at[other], firsts[0]).wait_recv()
    for i, device in enumerate(lasts):
        copy = remote(mine, mine, l_send.at[i], l_recv.at[me.last], device)
        copy.start()
        sent.append(copy)
    for d in (0, 1, 3, 2):
        other = lax.rem(me.last + d, 4)
        piece = out.at[base + other]
        if d:
            remote(piece, piece, l_send.at[0], l_recv.at[other], lasts[0]).wait_recv()
        copy = remote(piece, piece, s_send.at[d], s_recv.at[other], me.sibling())
        copy.start()
        sent.append(copy)
    for d in range(4):
        piece = out.at[me.o * 4 + d]
        remote(piece, piece, s_send.at[0], s_recv.at[d], me.sibling()).wait_recv()
    for copy in sent:
        copy.wait_send()


def total_of(parts):
    total = parts[0].astype(F32)
    for part in parts[1:]:
        total = total + part.astype(F32)
    return total


def scatter_kernel(
    part, latent_out, rope_out,
    from_s, own, from_l, middle, from_f, small, from_z, result,
    s_send, s_recv, l_send, l_recv, f_send, f_recv, z_send, z_recv, e_send, e_recv,
):
    me = Place()
    base = me.c * 4
    firsts = [me.first_peer(d) for d in (1, 2, 3)]
    lasts = [me.last_peer(d) for d in (1, 2, 3)]
    zs = []
    for d in range(1, 8):
        z = lax.rem(me.zh * 2 + me.zl + d, 8)
        zs.append((lax.div(z, 2), lax.rem(z, 2)))
    z_devices = [me.at(zh=zh, zl=zl) for zh, zl in zs]
    others = [me.at(y=lax.rem(me.y + d, 4), c=c) for d in (1, 2, 3) for c in (0, 1)]
    x_line = [me.at(x=lax.rem(me.x + d, 4)) for d in (1, 2, 3)]
    greet(x_line + others + z_devices + [me.sibling()], 17)

    sent = []
    for d in (1, 3, 2, 0):
        chunk = lax.rem(me.first + d, 4)
        copy = remote(
            part.at[me.o * 4 + chunk], from_s.at[chunk], s_send.at[d], s_recv.at[chunk], me.sibling()
        )
        copy.start()
        sent.append(copy)
    for d in (1, 3, 2, 0):
        chunk = lax.rem(me.last + d, 4)
        there = from_s.at[chunk]
        remote(there, there, s_send.at[0], s_recv.at[chunk], me.sibling()).wait_recv()
        own[chunk] = total_of([part[base + chunk], from_s[chunk]]).astype(BF16)
        if d:
            copy = remote(own.at[chunk], from_l.at[d - 1], l_send.at[d - 1], l_recv.at[d - 1], lasts[d - 1])
            copy.start()
            sent.append(copy)
    for d in range(3):
        there = from_l.at[d]
        remote(there, there, l_send.at[0], l_recv.at[d], lasts[0]).wait_recv()
    middle[...] = total_of([own[me.last], from_l[0], from_l[1], from_l[2]]).astype(BF16)
    for d in (1, 2, 3):
        other = lax.rem(me.first + d, 4)
        copy = remote(
            middle.at[:, other], from_f.at[d - 1], f_send.at[d - 1], f_recv.at[d - 1], firsts[d - 1]
        )
        copy.start()
        sent.append(copy)
    for d in range(3):
        there = from_f.at[d]
        remote(there, there, f_send.at[0], f_recv.at[d], firsts[0]).wait_recv()
    small[...] = total_of([middle[:, me.first], from_f[0], from_f[1], from_f[2]]).astype(BF16)
    z_mine = me.zh * 2 + me.zl
    for i, (zh, zl) in enumerate(zs):
        copy = remote(small.at[zh], from_z.at[z_mine], z_send.at[i], z_recv.at[z_mine], z_devices[i])
        copy.start()
        sent.append(copy)
    from_z[z_mine] = small[me.zh]
    for d in range(1, 8):
        z = lax.rem(z_mine + d, 8)
        there = from_z.at[z]
        remote(there, there, z_send.at[0], z_recv.at[z], z_devices[0]).wait_recv()
    place = me.c * 4 + me.y
    result[place] = total_of([from_z[z] for z in range(8)]).astype(BF16)
    ends = others + [me.sibling()]
    for i, device in enumerate(ends):
        copy = remote(result.at[place], result.at[place], e_send.at[i], e_recv.at[place], device)
        copy.start()
        sent.append(copy)
    for d in range(1, 8):
        other = lax.rem(place + d, 8)
        there = result.at[other]
        remote(there, there, e_send.at[0], e_recv.at[other], ends[0]).wait_recv()
    for i in range(8):
        latent_out[i * PIECE : (i + 1) * PIECE, :] = result[i, :, 0:D_LAT]
        rope_out[i * PIECE : (i + 1) * PIECE, :] = result[i, :, D_LAT : D_LAT + D_ROPE]
    for copy in sent:
        copy.wait_send()


NT = (((1,), (1,)), ((), ()))
TN = (((0,), (0,)), ((), ()))


def dot(a, b, dims=None):
    if dims is None:
        return jnp.dot(a, b, preferred_element_type=F32)
    return lax.dot_general(a, b, dims, preferred_element_type=F32)


def compute_kernel(
    lam, queries, keys, key_weight, value_weight, gain, out_grad, query_pos, key_pos,
    query_grad, part,
    q_cat, k_cat, values, scores, tops, outs, totals, lowered, deltas, q_acc,
):
    for h in range(MAPS):
        q_cat[h] = jnp.concatenate(
            [queries[:, h * D_QK : (h + 1) * D_QK], jnp.zeros((ROWS, 256 - D_QK), BF16)], axis=1
        )
    tops[...] = jnp.full(tops.shape, -jnp.inf, F32)
    outs[...] = jnp.zeros(outs.shape, F32)
    totals[...] = jnp.zeros(totals.shape, F32)
    q_acc[...] = jnp.zeros(q_acc.shape, F32)

    def expand(i, carry):
        latent = keys[i, :, 0:D_LAT]
        rope = keys[i, :, D_LAT:WIDE]
        nope = dot(latent, key_weight[...]).astype(BF16)
        value = dot(latent, value_weight[...]).astype(BF16)
        seen = key_pos[i] <= query_pos[...]
        for p in range(PAIRS_DEV):
            values[i, p] = value[:, p * PAIR_WIDTH : (p + 1) * PAIR_WIDTH]
        for h in range(MAPS):
            k_cat[i, h, :, 0:D_NOPE] = nope[:, h * D_NOPE : (h + 1) * D_NOPE]
            k_cat[i, h, :, D_NOPE:256] = rope
            tile = jnp.where(seen, dot(q_cat[h], k_cat[i, h], NT), -jnp.inf)
            scores[i, h] = tile
            tops[h] = jnp.maximum(tops[h], jnp.maximum(tile[:, 0:128], tile[:, 128:256]))
        return carry

    lax.fori_loop(0, CHUNKS, expand, 0)

    for h in range(MAPS):
        tops[h] = jnp.broadcast_to(jnp.max(tops[h], axis=1, keepdims=True), (ROWS, 128))

    def forward(i, carry):
        for p in range(PAIRS_DEV):
            both = []
            for m in range(2):
                h = 2 * p + m
                top = jnp.concatenate([tops[h], tops[h]], axis=1)
                weight = jnp.exp2((scores[i, h] - top) * (LOGIT_SCALE * LOG2E))
                scores[i, h] = weight
                totals[h] += weight[:, 0:128] + weight[:, 128:256]
                both.append(weight.astype(BF16))
            outs[p] += dot(jnp.concatenate(both, axis=0), values[i, p])
        return carry

    lax.fori_loop(0, CHUNKS, forward, 0)

    for p in range(PAIRS_DEV):
        lam_p = lam[p]
        maps = []
        for m in range(2):
            h = 2 * p + m
            inverse = 1.0 / jnp.sum(totals[h], axis=1, keepdims=True)
            totals[h] = jnp.broadcast_to(inverse, (ROWS, 128))
            maps.append(outs[p, m * ROWS : (m + 1) * ROWS] * inverse)
        mixed = maps[0] - lam_p * maps[1]
        inv_root = lax.rsqrt(jnp.mean(mixed * mixed, axis=1, keepdims=True) + EPS)
        normed = mixed * inv_root
        scaled = out_grad[:, p * PAIR_WIDTH : (p + 1) * PAIR_WIDTH].astype(F32) * gain[
            :, p * PAIR_WIDTH : (p + 1) * PAIR_WIDTH
        ]
        d_mixed = (scaled - normed * jnp.mean(scaled * normed, axis=1, keepdims=True)) * inv_root
        lowered[p] = d_mixed.astype(BF16)
        deltas[2 * p] = jnp.broadcast_to(
            jnp.sum(d_mixed * maps[0], axis=1, keepdims=True), (ROWS, 128)
        )
        deltas[2 * p + 1] = jnp.broadcast_to(
            -lam_p * jnp.sum(d_mixed * maps[1], axis=1, keepdims=True), (ROWS, 128)
        )

    def backward(i, carry):
        d_nope = []
        d_value = []
        d_rope = jnp.zeros((CHUNK, 128), F32)
        for p in range(PAIRS_DEV):
            lam_p = lam[p]
            grad = lowered[p]
            through = dot(grad, values[i, p], NT)
            probs = []
            for m in range(2):
                h = 2 * p + m
                probs.append(scores[i, h] * jnp.concatenate([totals[h], totals[h]], axis=1))
            d_value.append(dot((probs[0] - lam_p * probs[1]).astype(BF16), grad, TN).astype(BF16))
            for m in range(2):
                h = 2 * p + m
                delta = jnp.concatenate([deltas[h], deltas[h]], axis=1)
                inner = through if m == 0 else -lam_p * through
                d_score = (probs[m] * (inner - delta)).astype(BF16)
                q_acc[h] += dot(d_score, k_cat[i, h])
                d_key = dot(d_score, q_cat[h], TN) * LOGIT_SCALE
                d_nope.append(d_key[:, 0:D_NOPE].astype(BF16))
                d_rope = d_rope + d_key[:, D_NOPE:256]
        d_latent = dot(jnp.concatenate(d_nope, axis=1), key_weight[...], NT)
        d_latent = d_latent + dot(jnp.concatenate(d_value, axis=1), value_weight[...], NT)
        part[i, :, 0:D_LAT] = d_latent.astype(BF16)
        part[i, :, D_LAT:WIDE] = d_rope.astype(BF16)
        return carry

    lax.fori_loop(0, CHUNKS, backward, 0)
    for h in range(MAPS):
        query_grad[:, h * D_QK : (h + 1) * D_QK] = (q_acc[h, :, 0:D_QK] * LOGIT_SCALE).astype(BF16)


VMEM = pl.BlockSpec(memory_space=pltpu.VMEM)
SMEM = pl.BlockSpec(memory_space=pltpu.SMEM)
DMA = pltpu.SemaphoreType.DMA


def gather_keys(latent, rope_key):
    return pl.pallas_call(
        gather_kernel,
        out_shape=jax.ShapeDtypeStruct((CHUNKS, 4, 4, PIECE, WIDE), BF16),
        in_specs=[VMEM, VMEM],
        out_specs=VMEM,
        scratch_shapes=[DMA((n,)) for n in (3, 4, 3, 4, 3, 4, 4, 4)],
        compiler_params=pltpu.CompilerParams(
            collective_id=0, has_side_effects=True, vmem_limit_bytes=32 << 20
        ),
        name="gather_keys",
    )(latent, rope_key)


def scatter_grads(part):
    chunk = (4, 4, PIECE, WIDE)
    return pl.pallas_call(
        scatter_kernel,
        out_shape=(
            jax.ShapeDtypeStruct((ROWS, D_LAT), BF16),
            jax.ShapeDtypeStruct((ROWS, D_ROPE), BF16),
        ),
        in_specs=[VMEM],
        out_specs=(VMEM, VMEM),
        scratch_shapes=[
            pltpu.VMEM((4,) + chunk, BF16),
            pltpu.VMEM((4,) + chunk, BF16),
            pltpu.VMEM((3,) + chunk, BF16),
            pltpu.VMEM(chunk, BF16),
            pltpu.VMEM((3, 4, PIECE, WIDE), BF16),
            pltpu.VMEM((4, PIECE, WIDE), BF16),
            pltpu.VMEM((8, PIECE, WIDE), BF16),
            pltpu.VMEM((8, PIECE, WIDE), BF16),
        ]
        + [DMA((n,)) for n in (4, 4, 3, 3, 3, 3, 7, 8, 7, 8)],
        compiler_params=pltpu.CompilerParams(
            collective_id=1, has_side_effects=True, vmem_limit_bytes=32 << 20
        ),
        name="scatter_grads",
    )(part)


def attend(lam, queries, keys, key_weight, value_weight, gain, out_grad, query_pos, key_pos):
    return pl.pallas_call(
        compute_kernel,
        out_shape=(
            jax.ShapeDtypeStruct((ROWS, MAPS * D_QK), BF16),
            jax.ShapeDtypeStruct((CHUNKS, CHUNK, WIDE), BF16),
        ),
        in_specs=[SMEM] + [VMEM] * 8,
        out_specs=(VMEM, VMEM),
        scratch_shapes=[
            pltpu.VMEM((MAPS, ROWS, 256), BF16),
            pltpu.VMEM((CHUNKS, MAPS, CHUNK, 256), BF16),
            pltpu.VMEM((CHUNKS, PAIRS_DEV, CHUNK, PAIR_WIDTH), BF16),
            pltpu.VMEM((CHUNKS, MAPS, ROWS, CHUNK), F32),
            pltpu.VMEM((MAPS, ROWS, 128), F32),
            pltpu.VMEM((PAIRS_DEV, 2 * ROWS, PAIR_WIDTH), F32),
            pltpu.VMEM((MAPS, ROWS, 128), F32),
            pltpu.VMEM((PAIRS_DEV, ROWS, PAIR_WIDTH), BF16),
            pltpu.VMEM((MAPS, ROWS, 128), F32),
            pltpu.VMEM((MAPS, ROWS, 256), F32),
        ],
        compiler_params=pltpu.CompilerParams(vmem_limit_bytes=48 << 20),
        name="attend",
    )(lam, queries, keys, key_weight, value_weight, gain, out_grad, query_pos, key_pos)


def key_tokens():
    last = jnp.arange(4)[:, None, None, None]
    z = jnp.arange(4)[None, :, None, None]
    first = jnp.arange(4)[None, None, :, None]
    r = jnp.arange(PIECE)[None, None, None, :]
    zero = (z * 4 + last) * ROWS + first * PIECE + r
    one = (z * 4 + first) * ROWS + HALF + last * PIECE + r
    return jnp.stack([zero, one]).astype(jnp.int32)


def on_device(
    queries, latent, rope_key, key_weight, value_weight, lambda_pair, norm_gain, out_grad, block_order
):
    me = lax.axis_index("ctx")
    tokens = key_tokens()
    slots = (tokens[..., 0] // HALF).reshape(-1)
    hot = slots[:, None] == jnp.arange(32, dtype=jnp.int32)[None, :]
    blocks = jnp.sum(jnp.where(hot, block_order[None, :], 0), axis=1)
    key_pos = (blocks[:, None] * HALF + (tokens % HALF).reshape(-1, PIECE)).reshape(CHUNKS, 1, CHUNK)
    my_slots = jnp.arange(2, dtype=jnp.int32) + 2 * me
    hot = my_slots[:, None] == jnp.arange(32, dtype=jnp.int32)[None, :]
    mine = jnp.sum(jnp.where(hot, block_order[None, :], 0), axis=1)
    query_pos = (mine[:, None] * HALF + jnp.arange(HALF, dtype=jnp.int32)[None, :]).reshape(ROWS, 1)

    keys = gather_keys(latent, rope_key).reshape(CHUNKS, CHUNK, WIDE)
    query_grad, part = attend(
        lambda_pair, queries, keys, key_weight, value_weight, norm_gain.reshape(1, -1), out_grad,
        query_pos, key_pos,
    )
    latent_grad, rope_grad = scatter_grads(part.reshape(CHUNKS, 4, 4, PIECE, WIDE))
    return (query_grad, latent_grad, rope_grad)


def solution(mesh):
    return jax.shard_map(
        on_device,
        mesh=mesh,
        in_specs=(
            P("ctx", "head"),
            P("ctx", None),
            P("ctx", None),
            P(None, "head"),
            P(None, "head"),
            P("head"),
            P("head"),
            P("ctx", "head"),
            P(),
        ),
        out_specs=(P("ctx", "head"), P("ctx", None), P("ctx", None)),
        check_vma=False,
    )
```

```python
import functools

import jax
import jax.numpy as jnp
from jax import lax
from jax.experimental import pallas as pl
from jax.experimental.pallas import tpu as pltpu
from jax.sharding import PartitionSpec as P

MESH = pl.DeviceIdType.MESH
D_LAT = 512
D_NOPE = 128
D_ROPE = 64
D_QK = D_NOPE + D_ROPE
PAIR_WIDTH = 256
ROWS = 128
WIDE = 640
HALF = 64
CHUNKS = 8
CHUNK = 256
PIECE = 16
MAPS = 4
PAIRS_DEV = 2
LOGIT_SCALE = D_QK**-0.5
LOG2E = 1.4426950408889634
EPS = 1e-6
F32 = jnp.float32
BF16 = jnp.bfloat16


class Place:
    def __init__(self):
        ctx, head = lax.axis_index("ctx"), lax.axis_index("head")
        self.x, self.zh = lax.rem(ctx, 4), lax.div(ctx, 4)
        self.y = lax.div(head, 4)
        self.zl = lax.rem(lax.div(head, 2), 2)
        self.c = lax.rem(head, 2)
        self.o = 1 - self.c
        self.first = self.y * self.o + self.x * self.c
        self.last = self.x * self.o + self.y * self.c

    def at(self, x=None, y=None, zh=None, zl=None, c=None):
        x = self.x if x is None else x
        y = self.y if y is None else y
        zh = self.zh if zh is None else zh
        zl = self.zl if zl is None else zl
        c = self.c if c is None else c
        return (zh * 4 + x, y * 4 + zl * 2 + c)

    def first_peer(self, d):
        return self.at(x=lax.rem(self.x + d * self.c, 4), y=lax.rem(self.y + d * self.o, 4))

    def last_peer(self, d):
        return self.at(x=lax.rem(self.x + d * self.o, 4), y=lax.rem(self.y + d * self.c, 4))

    def z_peer(self, d):
        z = lax.rem(self.zh * 2 + self.zl + d, 8)
        return self.at(zh=lax.div(z, 2), zl=lax.rem(z, 2))

    def sibling(self):
        return self.at(c=self.o)


def remote(src, dst, send, recv, device):
    return pltpu.make_async_remote_copy(
        src_ref=src, dst_ref=dst, send_sem=send, recv_sem=recv, device_id=device, device_id_type=MESH
    )


def greet(devices, count):
    barrier = pltpu.get_barrier_semaphore()
    for device in devices:
        pl.semaphore_signal(barrier, inc=1, device_id=device, device_id_type=MESH)
    pl.semaphore_wait(barrier, count)


NT = (((1,), (1,)), ((), ()))
TN = (((0,), (0,)), ((), ()))


def dot(a, b, dims=None):
    if dims is None:
        return jnp.dot(a, b, preferred_element_type=F32)
    return lax.dot_general(a, b, dims, preferred_element_type=F32)


def total_of(parts):
    total = parts[0].astype(F32)
    for part in parts[1:]:
        total = total + part.astype(F32)
    return total


def pick(step, table):
    value = jnp.int32(table[0])
    for i in range(1, len(table)):
        value = jnp.where(step == i, jnp.int32(table[i]), value)
    return value


EXPAND_SIDE = (0, 1, 0, 1, 0, 1, 0, 1)
EXPAND_FAR = (0, 0, 1, 1, 3, 3, 2, 2)
BACK_SIDE = (1, 1, 0, 1, 0, 0, 1, 0)
BACK_FAR = (2, 3, 2, 1, 3, 1, 0, 0)
BACK_STEP = {(side, far): i for i, (side, far) in enumerate(zip(BACK_SIDE, BACK_FAR))}
REL = (0, 1, 3, 2)
HALVES = (slice(0, 2), slice(2, 4))


def fused_kernel(
    lam, block_order, gain_hbm, queries_hbm, latent_hbm, rope_hbm, key_weight_hbm, value_weight_hbm, out_grad_hbm,
    query_grad, latent_out, rope_out,
    gain, queries, rope_in, rope_rows, key_weight, value_weight, out_grad,
    keys, key_pos, query_pos, q_cat, k_cat, values, scores, d_scores, tops, outs, totals, lowered, deltas, q_acc,
    part, from_s, from_a, from_b, from_plus, from_minus, middle, from_f, small, from_z, result,
    in_sem, z_send, z_recv, f_send, f_recv, l_send, l_recv, w_send, w_recv, s_send, s_recv,
    t_send, t_recv, a_send, a_recv, p_send, p_recv, m_send, m_recv, g_send, g_recv, y_send, y_recv, e_send, e_recv,
):
    me = Place()
    ctx = me.zh * 4 + me.x
    base, other = me.c * 4, me.o * 4
    mine = keys.at[base + me.last]
    row = pl.multiple_of(me.c * HALF + me.y * PIECE, PIECE)
    x_line = [me.at(x=lax.rem(me.x + d, 4)) for d in (1, 2, 3)]
    y_lines = [me.at(y=lax.rem(me.y + d, 4), c=c) for d in (1, 2, 3) for c in (0, 1)]
    z_line = [me.z_peer(d) for d in range(1, 8)]
    firsts = {d: me.first_peer(d) for d in (1, 2, 3)}
    lasts = {d: me.last_peer(d) for d in (1, 3)}
    sibling = me.sibling()
    barrier = pltpu.get_barrier_semaphore()
    for device in x_line + y_lines + z_line + [sibling]:
        pl.semaphore_signal(barrier, inc=1, device_id=device, device_id_type=MESH)

    first_piece = mine.at[me.zh, me.first]
    loads = [
        pltpu.make_async_copy(latent_hbm.at[pl.ds(row, PIECE)], first_piece.at[:, 0:D_LAT], in_sem.at[0]),
        pltpu.make_async_copy(rope_hbm, rope_in, in_sem.at[1]),
        pltpu.make_async_copy(queries_hbm, queries, in_sem.at[2]),
        pltpu.make_async_copy(key_weight_hbm, key_weight, in_sem.at[3]),
        pltpu.make_async_copy(value_weight_hbm, value_weight, in_sem.at[4]),
        pltpu.make_async_copy(out_grad_hbm, out_grad, in_sem.at[5]),
        pltpu.make_async_copy(gain_hbm, gain, in_sem.at[6]),
    ]
    for load in loads:
        load.start()

    chunk = lax.broadcasted_iota(jnp.int32, (CHUNKS, CHUNK), 0)
    lane = lax.broadcasted_iota(jnp.int32, (CHUNKS, CHUNK), 1)
    side, far = chunk // 4, chunk % 4
    k_z, k_first, k_r = lane // 64, (lane // 16) % 4, lane % 16
    slot = 2 * (k_z * 4 + jnp.where(side == 0, far, k_first)) + side
    held = jnp.zeros((CHUNKS, CHUNK), jnp.int32)
    for i in range(32):
        held = jnp.where(slot == i, block_order[i], held)
    key_pos[...] = held * HALF + jnp.where(side == 0, k_first, far) * PIECE + k_r
    token = lax.broadcasted_iota(jnp.int32, (ROWS, CHUNK), 0)
    query_pos[...] = (
        jnp.where(token < HALF, block_order[2 * ctx], block_order[2 * ctx + 1]) * HALF + token % HALF
    )
    tops[...] = jnp.full(tops.shape, -jnp.inf, F32)
    outs[...] = jnp.zeros(outs.shape, F32)
    totals[...] = jnp.zeros(totals.shape, F32)
    q_acc[...] = jnp.zeros(q_acc.shape, F32)

    loads[1].wait()
    rope_rows[:, 0:D_ROPE] = rope_in[...].astype(F32).T.astype(BF16)
    rope_rows[:, D_ROPE:128] = jnp.zeros((ROWS, 128 - D_ROPE), BF16)
    loads[0].wait()
    mine[me.zh, me.first, :, D_LAT:WIDE] = rope_rows[pl.ds(row, PIECE), :]
    pl.semaphore_wait(barrier, 17)

    def z_of(k):
        return lax.rem(me.zh + k, 4)

    forward_z = 2 * me.zl - 1
    ahead, across = lax.rem(me.zh + forward_z + 4, 4), z_of(2)
    z_to = [me.at(zh=ahead, zl=0), me.at(zh=ahead, zl=1), me.at(zh=across, zl=1 - me.zl)]

    def z_copy(i):
        return remote(first_piece, first_piece, z_send.at[i], z_recv.at[me.zh], z_to[i])

    def f_copy(k, d):
        piece = mine.at[z_of(k), me.first]
        i = k * 3 + d - 1
        return remote(piece, piece, f_send.at[i], f_recv.at[i], firsts[d])

    def l_copy(k, d):
        piece = mine.at[z_of(k)]
        i = (d // 2) * 4 + k
        return remote(piece, piece, l_send.at[i], l_recv.at[i], lasts[d])

    def w_copy(k, d):
        piece = keys.at[base + lax.rem(me.last + 4 - d, 4), z_of(k)]
        i = (d // 2) * 4 + k
        return remote(piece, piece, w_send.at[i], w_recv.at[i], lasts[d])

    W_PIECES = ((0, 3), (1, 3), (3, 1), (2, 1))

    def s_copy(d):
        piece = keys.at[base + lax.rem(me.last + d, 4)]
        return remote(piece, piece, s_send.at[d], s_recv.at[d], sibling)

    def f_sends(k):
        for d in (1, 3, 2):
            f_copy(k, d).start()

    def f_done(k):
        for d in (1, 2, 3):
            f_copy(k, d).wait_recv()
        for d in (1, 3):
            l_copy(k, d).start()

    def z_wait(k):
        piece = mine.at[z_of(k), me.first]
        remote(piece, piece, z_send.at[0], z_recv.at[z_of(k)], z_to[0]).wait_recv()

    for i in range(3):
        z_copy(i).start()
    f_sends(0)
    loads[2].wait()
    for h in range(MAPS):
        q_cat[h] = jnp.concatenate(
            [queries[:, h * D_QK : (h + 1) * D_QK], jnp.zeros((ROWS, 256 - D_QK), BF16)], axis=1
        )
    z_wait(1)
    f_sends(1)
    z_wait(3)
    f_sends(3)
    f_done(0)
    z_wait(2)
    f_sends(2)
    f_done(1)
    f_done(3)
    f_done(2)
    s_copy(0).start()
    for load in loads[3:]:
        load.wait()

    def expand(step, carry):
        @pl.when(step == 2)
        def _():
            for k in (0, 1, 3, 2):
                for d in (3, 1):
                    l_copy(k, d).wait_recv()
                    if (k, d) in W_PIECES:
                        w_copy(k, d).start()
            s_copy(1).start()
            s_copy(3).start()

        @pl.when(step == 6)
        def _():
            for k, d in W_PIECES:
                w_copy(k, d).wait_recv()
            s_copy(2).start()

        for i, d in ((1, 0), (3, 1), (5, 3), (7, 2)):

            @pl.when(step == i)
            def _(d=d):
                s_copy(d).wait_recv()

        theirs, distance = lax.rem(step, 2), pick(step, EXPAND_FAR)
        ours = 1 - theirs
        i = (base + lax.rem(me.last + distance, 4)) * ours + (other + lax.rem(me.first + distance, 4)) * theirs
        tokens = keys[i].reshape(CHUNK, WIDE)
        latent = tokens[:, 0:D_LAT]
        rope = tokens[:, D_LAT:WIDE]
        nope = dot(latent, key_weight[...]).astype(BF16)
        value = dot(latent, value_weight[...]).astype(BF16)
        seen = key_pos[pl.ds(i, 1), :] <= query_pos[...]
        for p in range(PAIRS_DEV):
            values[i, p] = value[:, p * PAIR_WIDTH : (p + 1) * PAIR_WIDTH]
        for h in range(MAPS):
            k_cat[i, h, :, 0:D_NOPE] = nope[:, h * D_NOPE : (h + 1) * D_NOPE]
            k_cat[i, h, :, D_NOPE:256] = rope
            tile = jnp.where(seen, dot(q_cat[h], k_cat[i, h], NT), -jnp.inf)
            scores[i, h] = tile
            tops[h] = jnp.maximum(tops[h], jnp.maximum(tile[:, 0:128], tile[:, 128:256]))
        return carry

    lax.fori_loop(0, CHUNKS, expand, 0)

    for h in range(MAPS):
        tops[h] = jnp.broadcast_to(jnp.max(tops[h], axis=1, keepdims=True), (ROWS, 128))

    def forward(i, carry):
        for p in range(PAIRS_DEV):
            both = []
            for m in range(2):
                h = 2 * p + m
                top = jnp.concatenate([tops[h], tops[h]], axis=1)
                weight = jnp.exp2((scores[i, h] - top) * (LOGIT_SCALE * LOG2E))
                scores[i, h] = weight
                totals[h] += weight[:, 0:128] + weight[:, 128:256]
                both.append(weight.astype(BF16))
            outs[p] += dot(jnp.concatenate(both, axis=0), values[i, p])
        return carry

    lax.fori_loop(0, CHUNKS, forward, 0)

    for p in range(PAIRS_DEV):
        lam_p = lam[p]
        maps = []
        for m in range(2):
            h = 2 * p + m
            inverse = 1.0 / jnp.sum(totals[h], axis=1, keepdims=True)
            totals[h] = jnp.broadcast_to(inverse, (ROWS, 128))
            maps.append(outs[p, m * ROWS : (m + 1) * ROWS] * inverse)
        mixed = maps[0] - lam_p * maps[1]
        inv_root = lax.rsqrt(jnp.mean(mixed * mixed, axis=1, keepdims=True) + EPS)
        normed = mixed * inv_root
        scaled = out_grad[:, p * PAIR_WIDTH : (p + 1) * PAIR_WIDTH].astype(F32) * gain[
            :, p * PAIR_WIDTH : (p + 1) * PAIR_WIDTH
        ]
        d_mixed = (scaled - normed * jnp.mean(scaled * normed, axis=1, keepdims=True)) * inv_root
        lowered[p] = d_mixed.astype(BF16)
        deltas[2 * p] = jnp.broadcast_to(jnp.sum(d_mixed * maps[0], axis=1, keepdims=True), (ROWS, 128))
        deltas[2 * p + 1] = jnp.broadcast_to(
            -lam_p * jnp.sum(d_mixed * maps[1], axis=1, keepdims=True), (ROWS, 128)
        )

    def t_copy(d):
        return remote(part.at[BACK_STEP[1, d]], from_s.at[d], t_send.at[d], t_recv.at[d], sibling)

    def a_copy(h):
        piece = part.at[BACK_STEP[0, 2], HALVES[h]]
        return remote(piece, (from_a, from_b)[h], a_send.at[h], a_recv.at[h], lasts[(1, 3)[h]])

    def p_copy(h):
        there = from_minus.at[HALVES[h]]
        return remote(part.at[BACK_STEP[0, 1], HALVES[h]], there, p_send.at[h], p_recv.at[h], lasts[1])

    def m_copy(h):
        there = from_plus.at[HALVES[h]]
        return remote(part.at[BACK_STEP[0, 3], HALVES[h]], there, m_send.at[h], m_recv.at[h], lasts[3])

    def add_up(d, h, extra=None):
        there = part.at[BACK_STEP[0, d], HALVES[h]]
        terms = [there[...], from_s[d, HALVES[h]]]
        if extra is not None:
            terms.append(extra[...])
        there[...] = total_of(terms).astype(BF16)

    def backward(step, carry):
        theirs, distance = pick(step, BACK_SIDE), pick(step, BACK_FAR)
        ours = 1 - theirs
        i = (base + lax.rem(me.last + distance, 4)) * ours + (other + lax.rem(me.first + distance, 4)) * theirs
        d_nope = []
        d_value = []
        d_rope = jnp.zeros((CHUNK, 128), F32)
        for p in range(PAIRS_DEV):
            lam_p = lam[p]
            grad = lowered[p]
            through = dot(grad, values[i, p], NT)
            probs = []
            for m in range(2):
                h = 2 * p + m
                probs.append(scores[i, h] * jnp.concatenate([totals[h], totals[h]], axis=1))
            d_value.append(dot((probs[0] - lam_p * probs[1]).astype(BF16), grad, TN).astype(BF16))
            for m in range(2):
                h = 2 * p + m
                delta = jnp.concatenate([deltas[h], deltas[h]], axis=1)
                inner = through if m == 0 else -lam_p * through
                d_score = (probs[m] * (inner - delta)).astype(BF16)
                d_scores[i, h] = d_score
                d_key = dot(d_score, q_cat[h], TN) * LOGIT_SCALE
                d_nope.append(d_key[:, 0:D_NOPE].astype(BF16))
                d_rope = d_rope + d_key[:, D_NOPE:256]
        d_latent = dot(jnp.concatenate(d_nope, axis=1), key_weight[...], NT)
        d_latent = d_latent + dot(jnp.concatenate(d_value, axis=1), value_weight[...], NT)
        part[step, :, :, :, 0:D_LAT] = d_latent.astype(BF16).reshape(4, 4, PIECE, D_LAT)
        part[step, :, :, :, D_LAT:WIDE] = d_rope.astype(BF16).reshape(4, 4, PIECE, WIDE - D_LAT)

        for d in (2, 3, 1, 0):

            @pl.when(step == BACK_STEP[1, d])
            def _(d=d):
                t_copy(d).start()

        @pl.when(step == BACK_STEP[0, 2])
        def _():
            t_copy(2).wait_recv()
            for h in range(2):
                add_up(2, h)
                a_copy(h).start()

        @pl.when(step == BACK_STEP[0, 3])
        def _():
            t_copy(3).wait_recv()
            add_up(3, 0)
            m_copy(0).start()

        @pl.when(step == BACK_STEP[0, 1])
        def _():
            t_copy(1).wait_recv()
            add_up(1, 1)
            p_copy(1).start()
            a_copy(1).wait_recv()
            add_up(3, 1, from_b)
            m_copy(1).start()
            a_copy(0).wait_recv()
            add_up(1, 0, from_a)
            p_copy(0).start()

        return carry

    lax.fori_loop(0, CHUNKS, backward, 0)

    def to_queries(i, carry):
        for h in range(MAPS):
            q_acc[h] += dot(d_scores[i, h], k_cat[i, h])
        return carry

    lax.fori_loop(0, CHUNKS, to_queries, 0)
    for h in range(MAPS):
        query_grad[:, h * D_QK : (h + 1) * D_QK] = (q_acc[h, :, 0:D_QK] * LOGIT_SCALE).astype(BF16)

    def g_copy(h, d):
        piece = middle.at[HALVES[h], lax.rem(me.first + d, 4)]
        i = h * 3 + d - 1
        return remote(piece, from_f.at[d - 1, HALVES[h]], g_send.at[i], g_recv.at[i], firsts[d])

    t_copy(0).wait_recv()
    for h in (1, 0):
        p_copy(h).wait_recv()
        m_copy(h).wait_recv()
        middle[HALVES[h]] = total_of(
            [part[BACK_STEP[0, 0], HALVES[h]], from_s[0, HALVES[h]], from_minus[HALVES[h]], from_plus[HALVES[h]]]
        ).astype(BF16)
        for d in (2, 1, 3):
            g_copy(h, d).start()
    for h in (1, 0):
        for d in (1, 3, 2):
            g_copy(h, d).wait_recv()
        small[HALVES[h]] = total_of(
            [middle[HALVES[h], me.first]] + [from_f[d, HALVES[h]] for d in range(3)]
        ).astype(BF16)
    z_mine = me.zh * 2 + me.zl

    def y_copy(d):
        source = small.at[lax.div(lax.rem(z_mine + d, 8), 2)]
        return remote(source, from_z.at[z_mine], y_send.at[d - 1], y_recv.at[z_mine], z_line[d - 1])

    for d in (4, 3, 5, 2, 6, 1, 7):
        y_copy(d).start()
    from_z[z_mine] = small[me.zh]
    for d in range(1, 8):
        z = lax.rem(z_mine + d, 8)
        there = from_z.at[z]
        remote(there, there, y_send.at[0], y_recv.at[z], z_line[0]).wait_recv()
    place = me.c * 4 + me.y
    result[place] = total_of([from_z[z] for z in range(8)]).astype(BF16)
    ends = y_lines + [sibling]

    def e_copy(i):
        return remote(result.at[place], result.at[place], e_send.at[i], e_recv.at[place], ends[i])

    for i in (2, 3, 0, 1, 4, 5, 6):
        e_copy(i).start()
    for d in range(1, 8):
        there = result.at[lax.rem(place + d, 8)]
        remote(there, there, e_send.at[0], e_recv.at[lax.rem(place + d, 8)], sibling).wait_recv()
    everything = result[...].reshape(ROWS, WIDE)
    latent_out[...] = everything[:, 0:D_LAT]
    rope_out[...] = everything[:, D_LAT:WIDE].astype(F32).T[0:D_ROPE].astype(BF16)

    sent = [z_copy(i) for i in range(3)] + [s_copy(d) for d in range(4)] + [t_copy(d) for d in range(4)]
    sent += [f_copy(k, d) for k in range(4) for d in (1, 2, 3)] + [l_copy(k, d) for k in range(4) for d in (1, 3)]
    sent += [w_copy(k, d) for k, d in W_PIECES]
    sent += [make(h) for make in (a_copy, p_copy, m_copy) for h in range(2)]
    sent += [g_copy(h, d) for h in range(2) for d in (1, 2, 3)]
    sent += [y_copy(d) for d in range(1, 8)] + [e_copy(i) for i in range(7)]
    for copy in sent:
        copy.wait_send()


VMEM = pl.BlockSpec(memory_space=pltpu.VMEM)
SMEM = pl.BlockSpec(memory_space=pltpu.SMEM)
ANY = pl.BlockSpec(memory_space=pl.ANY)
DMA = pltpu.SemaphoreType.DMA


def fused(lam, block_order, gain, queries, latent, rope_t, key_weight, value_weight, out_grad):
    piece = (PIECE, WIDE)
    return pl.pallas_call(
        fused_kernel,
        out_shape=(
            jax.ShapeDtypeStruct((ROWS, MAPS * D_QK), BF16),
            jax.ShapeDtypeStruct((ROWS, D_LAT), BF16),
            jax.ShapeDtypeStruct((D_ROPE, ROWS), BF16),
        ),
        in_specs=[SMEM, SMEM] + [ANY] * 7,
        out_specs=(VMEM, VMEM, VMEM),
        scratch_shapes=[
            pltpu.VMEM((1, 512), F32),
            pltpu.VMEM((ROWS, MAPS * D_QK), BF16),
            pltpu.VMEM((D_ROPE, ROWS), BF16),
            pltpu.VMEM((ROWS, 128), BF16),
            pltpu.VMEM((D_LAT, 512), BF16),
            pltpu.VMEM((D_LAT, 512), BF16),
            pltpu.VMEM((ROWS, 512), BF16),
            pltpu.VMEM((CHUNKS, 4, 4) + piece, BF16),
            pltpu.VMEM((CHUNKS, CHUNK), jnp.int32),
            pltpu.VMEM((ROWS, CHUNK), jnp.int32),
            pltpu.VMEM((MAPS, ROWS, 256), BF16),
            pltpu.VMEM((CHUNKS, MAPS, CHUNK, 256), BF16),
            pltpu.VMEM((CHUNKS, PAIRS_DEV, CHUNK, PAIR_WIDTH), BF16),
            pltpu.VMEM((CHUNKS, MAPS, ROWS, CHUNK), F32),
            pltpu.VMEM((CHUNKS, MAPS, ROWS, CHUNK), BF16),
            pltpu.VMEM((MAPS, ROWS, 128), F32),
            pltpu.VMEM((PAIRS_DEV, 2 * ROWS, PAIR_WIDTH), F32),
            pltpu.VMEM((MAPS, ROWS, 128), F32),
            pltpu.VMEM((PAIRS_DEV, ROWS, PAIR_WIDTH), BF16),
            pltpu.VMEM((MAPS, ROWS, 128), F32),
            pltpu.VMEM((MAPS, ROWS, 256), F32),
            pltpu.VMEM((CHUNKS, 4, 4) + piece, BF16),
            pltpu.VMEM((4, 4, 4) + piece, BF16),
            pltpu.VMEM((2, 4) + piece, BF16),
            pltpu.VMEM((2, 4) + piece, BF16),
            pltpu.VMEM((4, 4) + piece, BF16),
            pltpu.VMEM((4, 4) + piece, BF16),
            pltpu.VMEM((4, 4) + piece, BF16),
            pltpu.VMEM((3, 4) + piece, BF16),
            pltpu.VMEM((4,) + piece, BF16),
            pltpu.VMEM((8,) + piece, BF16),
            pltpu.VMEM((8,) + piece, BF16),
        ]
        + [
            DMA((n,))
            for n in (7, 3, 4, 12, 12, 8, 8, 8, 8, 4, 4, 4, 4, 2, 2, 2, 2, 2, 2, 6, 6, 7, 8, 7, 8)
        ],
        compiler_params=pltpu.CompilerParams(
            collective_id=0, has_side_effects=True, vmem_limit_bytes=56 << 20
        ),
        name="fused",
    )(lam, block_order, gain, queries, latent, rope_t, key_weight, value_weight, out_grad)


def on_device(
    queries, latent, rope_key, key_weight, value_weight, lambda_pair, norm_gain, out_grad, block_order
):
    query_grad, latent_grad, rope_grad = fused(
        lambda_pair, block_order, norm_gain.reshape(1, -1), queries, latent, rope_key.T,
        key_weight, value_weight, out_grad,
    )
    return (query_grad, latent_grad, rope_grad.T)


def solution(mesh):
    return jax.shard_map(
        on_device,
        mesh=mesh,
        in_specs=(
            P("ctx", "head"),
            P("ctx", None),
            P("ctx", None),
            P(None, "head"),
            P(None, "head"),
            P("head"),
            P("head"),
            P("ctx", "head"),
            P(),
        ),
        out_specs=(P("ctx", "head"), P("ctx", None), P("ctx", None)),
        check_vma=False,
    )
```

```python
import functools

import jax
import jax.numpy as jnp
from jax import lax
from jax.experimental import pallas as pl
from jax.experimental.pallas import tpu as pltpu
from jax.sharding import PartitionSpec as P

MESH = pl.DeviceIdType.MESH
D_LAT = 512
D_NOPE = 128
D_ROPE = 64
D_QK = D_NOPE + D_ROPE
PAIR_WIDTH = 256
ROWS = 128
WIDE = 640
HALF = 64
CHUNKS = 8
CHUNK = 256
PIECE = 16
MAPS = 4
PAIRS_DEV = 2
LOGIT_SCALE = D_QK**-0.5
EXPONENT = LOGIT_SCALE * 1.4426950408889634
EPS = 1e-6
F32 = jnp.float32
BF16 = jnp.bfloat16


class Place:
    def __init__(self):
        ctx, head = lax.axis_index("ctx"), lax.axis_index("head")
        self.x, self.zh = lax.rem(ctx, 4), lax.div(ctx, 4)
        self.y = lax.div(head, 4)
        self.zl = lax.rem(lax.div(head, 2), 2)
        self.c = lax.rem(head, 2)
        self.o = 1 - self.c
        self.first = self.y * self.o + self.x * self.c
        self.last = self.x * self.o + self.y * self.c

    def at(self, x=None, y=None, zh=None, zl=None, c=None):
        x = self.x if x is None else x
        y = self.y if y is None else y
        zh = self.zh if zh is None else zh
        zl = self.zl if zl is None else zl
        c = self.c if c is None else c
        return (zh * 4 + x, y * 4 + zl * 2 + c)

    def first_peer(self, d):
        return self.at(x=lax.rem(self.x + d * self.c, 4), y=lax.rem(self.y + d * self.o, 4))

    def last_peer(self, d):
        return self.at(x=lax.rem(self.x + d * self.o, 4), y=lax.rem(self.y + d * self.c, 4))

    def z_peer(self, d):
        z = lax.rem(self.zh * 2 + self.zl + d, 8)
        return self.at(zh=lax.div(z, 2), zl=lax.rem(z, 2))

    def sibling(self):
        return self.at(c=self.o)


def remote(src, dst, send, recv, device):
    return pltpu.make_async_remote_copy(
        src_ref=src, dst_ref=dst, send_sem=send, recv_sem=recv, device_id=device, device_id_type=MESH
    )


def greet(devices, count):
    barrier = pltpu.get_barrier_semaphore()
    for device in devices:
        pl.semaphore_signal(barrier, inc=1, device_id=device, device_id_type=MESH)
    pl.semaphore_wait(barrier, count)


NT = (((1,), (1,)), ((), ()))
TN = (((0,), (0,)), ((), ()))


def dot(a, b, dims=None):
    if dims is None:
        return jnp.dot(a, b, preferred_element_type=F32)
    return lax.dot_general(a, b, dims, preferred_element_type=F32)


def total_of(parts):
    total = parts[0].astype(F32)
    for part in parts[1:]:
        total = total + part.astype(F32)
    return total


def pick(step, table):
    value = jnp.int32(table[0])
    for i in range(1, len(table)):
        value = jnp.where(step == i, jnp.int32(table[i]), value)
    return value


BACK_SIDE = (1, 1, 0, 0, 1, 1, 0, 0)
BACK_TURN = (3, 2, 3, 2, 1, 0, 1, 0)
BACK_STEP = {(side, turn): i for i, (side, turn) in enumerate(zip(BACK_SIDE, BACK_TURN))}


def fused_kernel(
    lam_hbm, order_hbm, gain_hbm, queries_hbm, latent_hbm, rope_hbm, key_weight_hbm, value_weight_hbm, out_grad_hbm,
    query_hbm, latent_out_hbm, rope_out_hbm,
    query_grad, latent_out, rope_out, lam, block_order, gain, queries, rope_in, rope_rows, key_weight, value_weight, out_grad,
    keys, key_pos, query_pos, q_cat, k_cat, values, scores, d_scores, tops, tops_then, outs, totals, lowered, deltas, q_acc,
    part, from_s, from_l, middle, from_f, small, from_z, result,
    in_sem, out_sem, f_send, f_recv, z_send, z_recv, l_send, l_recv, s_send, s_recv,
    t_send, t_recv, p_send, p_recv, g_send, g_recv, y_send, y_recv, e_send, e_recv,
):
    me = Place()
    ctx = me.zh * 4 + me.x
    base, other = me.c * 4, me.o * 4
    x_line = [me.at(x=lax.rem(me.x + d, 4)) for d in (1, 2, 3)]
    y_lines = [me.at(y=lax.rem(me.y + d, 4), c=c) for d in (1, 2, 3) for c in (0, 1)]
    z_line = [me.z_peer(d) for d in range(1, 8)]
    firsts = {d: me.first_peer(d) for d in (1, 2, 3)}
    lasts = {d: me.last_peer(d) for d in (1, 2, 3)}
    sibling = me.sibling()
    barrier = pltpu.get_barrier_semaphore()
    for device in x_line + y_lines + z_line + [sibling]:
        pl.semaphore_signal(barrier, inc=1, device_id=device, device_id_type=MESH)

    near = lax.rem(me.zh + 3 - 2 * me.zl, 4)
    z_order = [me.zh, near, lax.rem(me.zh + 1 + 2 * me.zl, 4), lax.rem(me.zh + 2, 4)]
    my_rows = keys.at[base + me.zh, me.last]
    my_piece = my_rows.at[me.first]
    loads = [
        pltpu.make_async_copy(order_hbm, block_order, in_sem.at[0]),
        pltpu.make_async_copy(lam_hbm, lam, in_sem.at[1]),
        pltpu.make_async_copy(rope_hbm, rope_in, in_sem.at[2]),
        pltpu.make_async_copy(queries_hbm, queries, in_sem.at[3]),
        pltpu.make_async_copy(key_weight_hbm, key_weight, in_sem.at[4]),
        pltpu.make_async_copy(value_weight_hbm, value_weight, in_sem.at[5]),
        pltpu.make_async_copy(out_grad_hbm, out_grad, in_sem.at[6]),
        pltpu.make_async_copy(gain_hbm, gain, in_sem.at[7]),
    ]
    whole_load = pltpu.make_async_copy(
        latent_hbm.at[pl.ds(0, 4)], my_rows.at[:, :, pl.ds(0, D_LAT)], in_sem.at[8]
    )
    piece_load = pltpu.make_async_copy(
        latent_hbm.at[4 + me.y], my_piece.at[:, pl.ds(0, D_LAT)], in_sem.at[8]
    )

    @pl.when(me.c == 0)
    def _():
        whole_load.start()

    @pl.when(me.c == 1)
    def _():
        piece_load.start()

    loads[2].start()
    loads[0].start()
    loads[1].start()
    for load in loads[3:]:
        load.start()

    loads[2].wait()
    rope_rows[:, :, 0:D_ROPE] = rope_in[...].astype(F32).T.astype(BF16).reshape(8, PIECE, D_ROPE)
    rope_rows[:, :, D_ROPE:128] = jnp.zeros((8, PIECE, 128 - D_ROPE), BF16)

    @pl.when(me.c == 0)
    def _():
        whole_load.wait()
        my_rows[:, :, D_LAT:WIDE] = rope_rows[0:4]

    @pl.when(me.c == 1)
    def _():
        piece_load.wait()
        my_piece[:, D_LAT:WIDE] = rope_rows[4 + me.y]

    pl.semaphore_wait(barrier, 17)

    z_to = [
        me.at(zh=near, zl=1 - me.zl),
        me.at(zh=near, zl=me.zl),
        me.at(zh=z_order[3], zl=1 - me.zl),
    ]

    def f_copy(turn, d):
        piece = keys.at[base + z_order[turn], me.last, me.first]
        i = turn * 3 + d - 1
        return remote(piece, piece, f_send.at[i], f_recv.at[i], firsts[d])

    def rows_copy(i):
        return remote(my_rows, my_rows, z_send.at[i], z_recv.at[me.zh], z_to[i])

    def piece_copy(i):
        return remote(my_piece, my_piece, z_send.at[i], z_recv.at[me.zh], z_to[i])

    def rows_wait(turn):
        rows = keys.at[base + z_order[turn], me.last]
        remote(rows, rows, z_send.at[0], z_recv.at[z_order[turn]], z_to[0]).wait_recv()

    def piece_wait(turn):
        piece = keys.at[base + z_order[turn], me.last, me.first]
        remote(piece, piece, z_send.at[0], z_recv.at[z_order[turn]], z_to[0]).wait_recv()

    def l_copy(turn, d):
        rows = keys.at[base + z_order[turn], me.last]
        i = turn * 3 + d - 1
        return remote(rows, rows, l_send.at[i], l_recv.at[i], lasts[d])

    def s_copy(turn):
        rows = keys.at[base + z_order[turn]]
        return remote(rows, rows, s_send.at[turn], s_recv.at[turn], sibling)

    def l_sends(turn):
        for d in (2, 1, 3):
            l_copy(turn, d).start()

    def f_sends(turn):
        for d in (2, 1, 3):
            f_copy(turn, d).start()

    def f_done(turn):
        for d in (1, 3, 2):
            f_copy(turn, d).wait_recv()
        l_sends(turn)

    @pl.when(me.c == 0)
    def _():
        for i in range(3):
            rows_copy(i).start()
        l_sends(0)

    @pl.when(me.c == 1)
    def _():
        f_sends(0)
        for i in (2, 1, 0):
            piece_copy(i).start()

    loads[0].wait()
    chunk = lax.broadcasted_iota(jnp.int32, (CHUNKS, CHUNK), 0)
    lane = lax.broadcasted_iota(jnp.int32, (CHUNKS, CHUNK), 1)
    side, k_z = chunk // 4, chunk % 4
    k_last, k_first, k_r = lane // 64, (lane // 16) % 4, lane % 16
    slot = 2 * (k_z * 4 + jnp.where(side == 0, k_last, k_first)) + side
    held = jnp.zeros((CHUNKS, CHUNK), jnp.int32)
    for i in range(32):
        held = jnp.where(slot == i, block_order[i], held)
    key_pos[...] = held * HALF + jnp.where(side == 0, k_first, k_last) * PIECE + k_r
    token = lax.broadcasted_iota(jnp.int32, (ROWS, CHUNK), 0)
    query_pos[...] = (
        jnp.where(token < HALF, block_order[2 * ctx], block_order[2 * ctx + 1]) * HALF + token % HALF
    )
    tops[...] = jnp.full(tops.shape, -1e30, F32)
    outs[...] = jnp.zeros(outs.shape, F32)
    totals[...] = jnp.zeros(totals.shape, F32)
    q_acc[...] = jnp.zeros(q_acc.shape, F32)

    for load in loads[1:2] + loads[3:4]:
        load.wait()
    for h in range(MAPS):
        q_cat[h] = jnp.concatenate(
            [queries[:, h * D_QK : (h + 1) * D_QK], jnp.zeros((ROWS, 256 - D_QK), BF16)], axis=1
        )
    for load in loads[4:]:
        load.wait()

    @pl.when(me.c == 0)
    def _():
        for turn in (1, 2, 3):
            rows_wait(turn)
            l_sends(turn)

    @pl.when(me.c == 1)
    def _():
        f_done(0)
        for turn in (1, 2, 3):
            piece_wait(turn)
            f_sends(turn)
        for turn in (1, 2, 3):
            f_done(turn)

    def expand(step, carry):
        for turn in range(4):

            @pl.when(step == 2 * turn)
            def _(turn=turn):
                for d in (1, 3, 2):
                    l_copy(turn, d).wait_recv()
                s_copy(turn).start()

            @pl.when(step == 2 * turn + 1)
            def _(turn=turn):
                s_copy(turn).wait_recv()

        theirs = lax.rem(step, 2)
        i = base * (1 - theirs) + other * theirs + pick(lax.div(step, 2), z_order)
        tokens = keys[i].reshape(CHUNK, WIDE)
        latent = tokens[:, 0:D_LAT]
        rope = tokens[:, D_LAT:WIDE]
        nope = dot(latent, key_weight[...]).astype(BF16)
        value = dot(latent, value_weight[...]).astype(BF16)
        seen = key_pos[pl.ds(i, 1), :] <= query_pos[...]
        for p in range(PAIRS_DEV):
            values[i, p] = value[:, p * PAIR_WIDTH : (p + 1) * PAIR_WIDTH]
        for p in range(PAIRS_DEV):
            both, shrinks = [], []
            for m in range(2):
                h = 2 * p + m
                k_cat[i, h, :, 0:D_NOPE] = nope[:, h * D_NOPE : (h + 1) * D_NOPE]
                k_cat[i, h, :, D_NOPE:256] = rope
                tile = jnp.where(seen, dot(q_cat[h], k_cat[i, h], NT), -jnp.inf)
                top = jnp.maximum(tops[h], jnp.max(tile, axis=1, keepdims=True))
                shrink = jnp.exp2((tops[h] - top) * EXPONENT)
                weight = jnp.exp2((tile - jnp.concatenate([top, top], axis=1)) * EXPONENT)
                tops[h] = top
                tops_then[i, h] = top
                scores[i, h] = weight
                totals[h] = totals[h] * shrink + (weight[:, 0:128] + weight[:, 128:256])
                both.append(weight.astype(BF16))
                shrinks.append(jnp.concatenate([shrink, shrink], axis=1))
            outs[p] = outs[p] * jnp.concatenate(shrinks, axis=0) + dot(
                jnp.concatenate(both, axis=0), values[i, p]
            )
        return carry

    lax.fori_loop(0, CHUNKS, expand, 0)

    for p in range(PAIRS_DEV):
        lam_p = lam[p]
        maps = []
        for m in range(2):
            h = 2 * p + m
            inverse = 1.0 / jnp.sum(totals[h], axis=1, keepdims=True)
            totals[h] = jnp.broadcast_to(inverse, (ROWS, 128))
            maps.append(outs[p, m * ROWS : (m + 1) * ROWS] * inverse)
        mixed = maps[0] - lam_p * maps[1]
        inv_root = lax.rsqrt(jnp.mean(mixed * mixed, axis=1, keepdims=True) + EPS)
        normed = mixed * inv_root
        scaled = out_grad[:, p * PAIR_WIDTH : (p + 1) * PAIR_WIDTH].astype(F32) * gain[
            :, p * PAIR_WIDTH : (p + 1) * PAIR_WIDTH
        ]
        d_mixed = (scaled - normed * jnp.mean(scaled * normed, axis=1, keepdims=True)) * inv_root
        lowered[p] = d_mixed.astype(BF16)
        deltas[2 * p] = jnp.broadcast_to(jnp.sum(d_mixed * maps[0], axis=1, keepdims=True), (ROWS, 128))
        deltas[2 * p + 1] = jnp.broadcast_to(
            -lam_p * jnp.sum(d_mixed * maps[1], axis=1, keepdims=True), (ROWS, 128)
        )

    def t_copy(turn):
        return remote(part.at[BACK_STEP[1, turn]], from_s.at[turn], t_send.at[turn], t_recv.at[turn], sibling)

    def p_copy(turn, d):
        rows = part.at[BACK_STEP[0, turn], lax.rem(me.last + d, 4)]
        i = turn * 3 + d - 1
        return remote(rows, from_l.at[turn, d - 1], p_send.at[i], p_recv.at[i], lasts[d])

    def g_copy(turn, d):
        piece = middle.at[turn, lax.rem(me.first + d, 4)]
        i = turn * 3 + d - 1
        return remote(piece, from_f.at[turn, d - 1], g_send.at[i], g_recv.at[i], firsts[d])

    def add_own(turn):
        t_copy(turn).wait_recv()
        there = part.at[BACK_STEP[0, turn]]
        there[...] = total_of([there[...], from_s[turn]]).astype(BF16)
        for d in (2, 1, 3):
            p_copy(turn, d).start()

    def add_last(turn):
        for d in (1, 3, 2):
            p_copy(turn, d).wait_recv()
        middle[turn] = total_of(
            [part[BACK_STEP[0, turn], me.last]] + [from_l[turn, d] for d in range(3)]
        ).astype(BF16)
        for d in (2, 1, 3):
            g_copy(turn, d).start()

    def backward(step, carry):
        theirs = pick(step, BACK_SIDE)
        i = base * (1 - theirs) + other * theirs + pick(pick(step, BACK_TURN), z_order)
        d_nope = []
        d_value = []
        d_rope = jnp.zeros((CHUNK, 128), F32)
        for p in range(PAIRS_DEV):
            lam_p = lam[p]
            grad = lowered[p]
            through = dot(grad, values[i, p], NT)
            probs = []
            for m in range(2):
                h = 2 * p + m
                share = jnp.exp2((tops_then[i, h] - tops[h]) * EXPONENT) * totals[h]
                probs.append(scores[i, h] * jnp.concatenate([share, share], axis=1))
            d_value.append(dot((probs[0] - lam_p * probs[1]).astype(BF16), grad, TN).astype(BF16))
            for m in range(2):
                h = 2 * p + m
                delta = jnp.concatenate([deltas[h], deltas[h]], axis=1)
                inner = through if m == 0 else -lam_p * through
                d_score = (probs[m] * (inner - delta)).astype(BF16)
                d_scores[i, h] = d_score
                d_key = dot(d_score, q_cat[h], TN) * LOGIT_SCALE
                d_nope.append(d_key[:, 0:D_NOPE].astype(BF16))
                d_rope = d_rope + d_key[:, D_NOPE:256]
        d_latent = dot(jnp.concatenate(d_nope, axis=1), key_weight[...], NT)
        d_latent = d_latent + dot(jnp.concatenate(d_value, axis=1), value_weight[...], NT)
        part[step, :, :, :, 0:D_LAT] = d_latent.astype(BF16).reshape(4, 4, PIECE, D_LAT)
        part[step, :, :, :, D_LAT:WIDE] = d_rope.astype(BF16).reshape(4, 4, PIECE, WIDE - D_LAT)

        for turn in range(4):

            @pl.when(step == BACK_STEP[1, turn])
            def _(turn=turn):
                t_copy(turn).start()

            @pl.when(step == BACK_STEP[0, turn])
            def _(turn=turn):
                add_own(turn)

        return carry

    lax.fori_loop(0, CHUNKS, backward, 0)
    add_last(3)
    add_last(2)

    def to_queries(i, carry):
        for h in range(MAPS):
            q_acc[h] += dot(d_scores[i, h], k_cat[i, h])
        return carry

    lax.fori_loop(0, CHUNKS, to_queries, 0)
    for h in range(MAPS):
        query_grad[:, h * D_QK : (h + 1) * D_QK] = (q_acc[h, :, 0:D_QK] * LOGIT_SCALE).astype(BF16)

    stores = [
        pltpu.make_async_copy(query_grad, query_hbm, out_sem.at[0]),
        pltpu.make_async_copy(latent_out, latent_out_hbm, out_sem.at[1]),
        pltpu.make_async_copy(rope_out, rope_out_hbm, out_sem.at[2]),
    ]
    stores[0].start()
    z_mine = me.zh * 2 + me.zl

    def y_copy(turn, zl):
        i = turn * 2 + zl
        device = me.at(zh=z_order[turn], zl=zl)
        return remote(small.at[turn], from_z.at[z_mine], y_send.at[i], y_recv.at[z_mine], device)

    own_y = remote(
        small.at[0], from_z.at[z_mine], y_send.at[0], y_recv.at[z_mine], me.at(zl=1 - me.zl)
    )

    def add_first(turn):
        for d in (1, 3, 2):
            g_copy(turn, d).wait_recv()
        small[turn] = total_of(
            [middle[turn, me.first]] + [from_f[turn, d] for d in range(3)]
        ).astype(BF16)
        if turn:
            for zl in (0, 1):
                y_copy(turn, zl).start()
        else:
            own_y.start()

    add_first(3)
    add_first(2)
    add_last(1)
    add_last(0)
    add_first(1)
    add_first(0)
    from_z[z_mine] = small[0]
    for d in range(1, 8):
        z = lax.rem(z_mine + d, 8)
        there = from_z.at[z]
        remote(there, there, y_send.at[0], y_recv.at[z], z_line[0]).wait_recv()
    place = me.c * 4 + me.y
    result[place] = total_of([from_z[z] for z in range(8)]).astype(BF16)
    ends = y_lines + [sibling]

    def e_copy(i):
        return remote(result.at[place], result.at[place], e_send.at[i], e_recv.at[place], ends[i])

    for i in (2, 3, 0, 1, 4, 5, 6):
        e_copy(i).start()
    for d in range(1, 8):
        there = result.at[lax.rem(place + d, 8)]
        remote(there, there, e_send.at[0], e_recv.at[lax.rem(place + d, 8)], sibling).wait_recv()
    everything = result[...].reshape(ROWS, WIDE)
    latent_out[...] = everything[:, 0:D_LAT]
    rope_out[...] = everything[:, D_LAT:WIDE].astype(F32).T[0:D_ROPE].astype(BF16)
    stores[1].start()
    stores[2].start()

    @pl.when(me.c == 0)
    def _():
        for i in range(3):
            rows_copy(i).wait_send()

    @pl.when(me.c == 1)
    def _():
        for i in range(3):
            piece_copy(i).wait_send()
        for turn in range(4):
            for d in (1, 2, 3):
                f_copy(turn, d).wait_send()

    sent = [s_copy(turn) for turn in range(4)] + [t_copy(turn) for turn in range(4)]
    sent += [make(turn, d) for make in (l_copy, p_copy, g_copy) for turn in range(4) for d in (1, 2, 3)]
    sent += [y_copy(turn, zl) for turn in (1, 2, 3) for zl in (0, 1)] + [own_y]
    sent += [e_copy(i) for i in range(7)]
    for copy in sent:
        copy.wait_send()
    for store in stores:
        store.wait()


def copy_out(query_in, latent_in, rope_in, query_out, latent_out, rope_out, query, latent, rope, in_sem, out_sem):
    steps = [(query_in, query, query_out), (latent_in, latent, latent_out), (rope_in, rope, rope_out)]
    reads = [pltpu.make_async_copy(a, b, in_sem.at[i]) for i, (a, b, c) in enumerate(steps)]
    writes = [pltpu.make_async_copy(b, c, out_sem.at[i]) for i, (a, b, c) in enumerate(steps)]
    for read in reads:
        read.start()
    for read, write in zip(reads, writes):
        read.wait()
        write.start()
    for write in writes:
        write.wait()


VMEM = pl.BlockSpec(memory_space=pltpu.VMEM)
SMEM = pl.BlockSpec(memory_space=pltpu.SMEM)
ANY = pl.BlockSpec(memory_space=pl.ANY)
DMA = pltpu.SemaphoreType.DMA


OUTS = (
    jax.ShapeDtypeStruct((ROWS, MAPS * D_QK), BF16),
    jax.ShapeDtypeStruct((ROWS, D_LAT), BF16),
    jax.ShapeDtypeStruct((D_ROPE, ROWS), BF16),
)


def fused(*operands):
    piece = (PIECE, WIDE)
    outs = pl.pallas_call(
        fused_kernel,
        out_shape=OUTS,
        in_specs=[ANY] * 9,
        out_specs=(ANY, ANY, ANY),
        scratch_shapes=[pltpu.VMEM(out.shape, BF16) for out in OUTS]
        + [
            pltpu.SMEM((PAIRS_DEV,), F32),
            pltpu.SMEM((32,), jnp.int32),
            pltpu.VMEM((1, 512), F32),
            pltpu.VMEM((ROWS, MAPS * D_QK), BF16),
            pltpu.VMEM((D_ROPE, ROWS), BF16),
            pltpu.VMEM((8, PIECE, 128), BF16),
            pltpu.VMEM((D_LAT, 512), BF16),
            pltpu.VMEM((D_LAT, 512), BF16),
            pltpu.VMEM((ROWS, 512), BF16),
            pltpu.VMEM((CHUNKS, 4, 4) + piece, BF16),
            pltpu.VMEM((CHUNKS, CHUNK), jnp.int32),
            pltpu.VMEM((ROWS, CHUNK), jnp.int32),
            pltpu.VMEM((MAPS, ROWS, 256), BF16),
            pltpu.VMEM((CHUNKS, MAPS, CHUNK, 256), BF16),
            pltpu.VMEM((CHUNKS, PAIRS_DEV, CHUNK, PAIR_WIDTH), BF16),
            pltpu.VMEM((CHUNKS, MAPS, ROWS, CHUNK), F32),
            pltpu.VMEM((CHUNKS, MAPS, ROWS, CHUNK), BF16),
            pltpu.VMEM((MAPS, ROWS, 128), F32),
            pltpu.VMEM((CHUNKS, MAPS, ROWS, 128), F32),
            pltpu.VMEM((PAIRS_DEV, 2 * ROWS, PAIR_WIDTH), F32),
            pltpu.VMEM((MAPS, ROWS, 128), F32),
            pltpu.VMEM((PAIRS_DEV, ROWS, PAIR_WIDTH), BF16),
            pltpu.VMEM((MAPS, ROWS, 128), F32),
            pltpu.VMEM((MAPS, ROWS, 256), F32),
            pltpu.VMEM((CHUNKS, 4, 4) + piece, BF16),
            pltpu.VMEM((4, 4, 4) + piece, BF16),
            pltpu.VMEM((4, 3, 4) + piece, BF16),
            pltpu.VMEM((4, 4) + piece, BF16),
            pltpu.VMEM((4, 3) + piece, BF16),
            pltpu.VMEM((4,) + piece, BF16),
            pltpu.VMEM((8,) + piece, BF16),
            pltpu.VMEM((8,) + piece, BF16),
        ]
        + [DMA((n,)) for n in (9, 3, 12, 12, 3, 4, 12, 12, 4, 4, 4, 4, 12, 12, 12, 12, 8, 8, 7, 8)],
        compiler_params=pltpu.CompilerParams(
            collective_id=0, has_side_effects=True, vmem_limit_bytes=56 << 20
        ),
        name="fused",
    )(*operands)
    return pl.pallas_call(
        copy_out,
        out_shape=OUTS,
        in_specs=[ANY] * 3,
        out_specs=(ANY, ANY, ANY),
        scratch_shapes=[pltpu.VMEM(out.shape, BF16) for out in OUTS] + [DMA((3,)), DMA((3,))],
        name="copy_out",
    )(*outs)


def on_device(
    queries, latent, rope_key, key_weight, value_weight, lambda_pair, norm_gain, out_grad, block_order
):
    query_grad, latent_grad, rope_grad = fused(
        lambda_pair, block_order, norm_gain.reshape(1, -1), queries, latent.reshape(8, PIECE, D_LAT), rope_key.T,
        key_weight, value_weight, out_grad,
    )
    return (query_grad, latent_grad, rope_grad.T)


def solution(mesh):
    return jax.shard_map(
        on_device,
        mesh=mesh,
        in_specs=(
            P("ctx", "head"),
            P("ctx", None),
            P("ctx", None),
            P(None, "head"),
            P(None, "head"),
            P("head"),
            P("head"),
            P("ctx", "head"),
            P(),
        ),
        out_specs=(P("ctx", "head"), P("ctx", None), P("ctx", None)),
        check_vma=False,
    )
```

```python
import functools

import jax
import jax.numpy as jnp
from jax import lax
from jax.experimental import pallas as pl
from jax.experimental.pallas import tpu as pltpu
from jax.sharding import PartitionSpec as P

MESH = pl.DeviceIdType.MESH
D_LAT = 512
D_NOPE = 128
D_ROPE = 64
D_QK = D_NOPE + D_ROPE
PAIR_WIDTH = 256
ROWS = 128
WIDE = 640
HALF = 64
CHUNKS = 8
CHUNK = 256
PIECE = 16
MAPS = 4
PAIRS_DEV = 2
LOGIT_SCALE = D_QK**-0.5
EXPONENT = LOGIT_SCALE * 1.4426950408889634
EPS = 1e-6
F32 = jnp.float32
BF16 = jnp.bfloat16


class Place:
    def __init__(self):
        ctx, head = lax.axis_index("ctx"), lax.axis_index("head")
        self.x, self.zh = lax.rem(ctx, 4), lax.div(ctx, 4)
        self.y = lax.div(head, 4)
        self.zl = lax.rem(lax.div(head, 2), 2)
        self.c = lax.rem(head, 2)
        self.o = 1 - self.c
        self.first = self.y * self.o + self.x * self.c
        self.last = self.x * self.o + self.y * self.c

    def at(self, x=None, y=None, zh=None, zl=None, c=None):
        x = self.x if x is None else x
        y = self.y if y is None else y
        zh = self.zh if zh is None else zh
        zl = self.zl if zl is None else zl
        c = self.c if c is None else c
        return (zh * 4 + x, y * 4 + zl * 2 + c)

    def first_peer(self, d):
        return self.at(x=lax.rem(self.x + d * self.c, 4), y=lax.rem(self.y + d * self.o, 4))

    def last_peer(self, d):
        return self.at(x=lax.rem(self.x + d * self.o, 4), y=lax.rem(self.y + d * self.c, 4))

    def z_peer(self, d):
        z = lax.rem(self.zh * 2 + self.zl + d, 8)
        return self.at(zh=lax.div(z, 2), zl=lax.rem(z, 2))

    def sibling(self):
        return self.at(c=self.o)


def remote(src, dst, send, recv, device):
    return pltpu.make_async_remote_copy(
        src_ref=src, dst_ref=dst, send_sem=send, recv_sem=recv, device_id=device, device_id_type=MESH
    )


def greet(devices, count):
    barrier = pltpu.get_barrier_semaphore()
    for device in devices:
        pl.semaphore_signal(barrier, inc=1, device_id=device, device_id_type=MESH)
    pl.semaphore_wait(barrier, count)


NT = (((1,), (1,)), ((), ()))
TN = (((0,), (0,)), ((), ()))


def dot(a, b, dims=None):
    if dims is None:
        return jnp.dot(a, b, preferred_element_type=F32)
    return lax.dot_general(a, b, dims, preferred_element_type=F32)


def total_of(parts):
    total = parts[0].astype(F32)
    for part in parts[1:]:
        total = total + part.astype(F32)
    return total


def pick(step, table):
    value = jnp.int32(table[0])
    for i in range(1, len(table)):
        value = jnp.where(step == i, jnp.int32(table[i]), value)
    return value


BACK_SIDE = (1, 1, 0, 1, 0, 1, 0, 0)
BACK_TURN = (3, 2, 3, 1, 2, 0, 1, 0)
BACK_STEP = {(side, turn): i for i, (side, turn) in enumerate(zip(BACK_SIDE, BACK_TURN))}


def fused_kernel(
    lam_hbm, order_hbm, gain_hbm, queries_hbm, latent_hbm, rope_hbm, key_weight_hbm, value_weight_hbm, out_grad_hbm,
    query_hbm, result_hbm,
    query_grad, lam, block_order, gain, queries, rope_in, rope_rows, key_weight, value_weight, out_grad,
    keys, key_pos, query_pos, q_cat, q_nope, q_rope, k_cat, values, scores, d_scores, tops, tops_then, outs, totals, lowered, deltas, q_acc,
    part, from_s, from_l, middle, from_f, small, from_z, result,
    in_sem, out_sem, f_send, f_recv, z_send, z_recv, l_send, l_recv, s_send, s_recv,
    t_send, t_recv, p_send, p_recv, g_send, g_recv, y_send, y_recv, e_send, e_recv, r_send, r_recv,
):
    me = Place()
    ctx = me.zh * 4 + me.x
    base, other = me.c * 4, me.o * 4
    x_line = [me.at(x=lax.rem(me.x + d, 4)) for d in (1, 2, 3)]
    y_line = [me.at(y=lax.rem(me.y + d, 4)) for d in (1, 2, 3)]
    z_line = [me.z_peer(d) for d in range(1, 8)]
    firsts = {d: me.first_peer(d) for d in (1, 2, 3)}
    lasts = {d: me.last_peer(d) for d in (1, 2, 3)}
    sibling = me.sibling()
    barrier = pltpu.get_barrier_semaphore()
    for device in x_line + y_line + z_line + [sibling]:
        pl.semaphore_signal(barrier, inc=1, device_id=device, device_id_type=MESH)

    near = lax.rem(me.zh + 3 - 2 * me.zl, 4)
    z_order = [me.zh, near, lax.rem(me.zh + 1 + 2 * me.zl, 4), lax.rem(me.zh + 2, 4)]
    my_rows = keys.at[base + me.zh, me.last]
    my_piece = my_rows.at[me.first]
    loads = [
        pltpu.make_async_copy(order_hbm, block_order, in_sem.at[0]),
        pltpu.make_async_copy(lam_hbm, lam, in_sem.at[1]),
        pltpu.make_async_copy(rope_hbm, rope_in, in_sem.at[2]),
        pltpu.make_async_copy(queries_hbm, queries, in_sem.at[3]),
        pltpu.make_async_copy(key_weight_hbm, key_weight, in_sem.at[4]),
        pltpu.make_async_copy(value_weight_hbm, value_weight, in_sem.at[5]),
        pltpu.make_async_copy(out_grad_hbm, out_grad, in_sem.at[6]),
        pltpu.make_async_copy(gain_hbm, gain, in_sem.at[7]),
    ]
    whole_load = pltpu.make_async_copy(
        latent_hbm.at[pl.ds(0, 4)], my_rows.at[:, :, pl.ds(0, D_LAT)], in_sem.at[8]
    )
    piece_load = pltpu.make_async_copy(
        latent_hbm.at[4 + me.y], my_piece.at[:, pl.ds(0, D_LAT)], in_sem.at[8]
    )

    @pl.when(me.c == 0)
    def _():
        whole_load.start()

    @pl.when(me.c == 1)
    def _():
        piece_load.start()

    loads[2].start()
    loads[0].start()
    loads[1].start()
    for load in loads[3:]:
        load.start()

    loads[2].wait()
    rope_rows[:, :, 0:D_ROPE] = rope_in[...].astype(F32).T.astype(BF16).reshape(8, PIECE, D_ROPE)
    rope_rows[:, :, D_ROPE:128] = jnp.zeros((8, PIECE, 128 - D_ROPE), BF16)

    @pl.when(me.c == 0)
    def _():
        whole_load.wait()
        my_rows[:, :, D_LAT:WIDE] = rope_rows[0:4]

    @pl.when(me.c == 1)
    def _():
        piece_load.wait()
        my_piece[:, D_LAT:WIDE] = rope_rows[4 + me.y]

    pl.semaphore_wait(barrier, 14)

    z_to = [
        me.at(zh=near, zl=1 - me.zl),
        me.at(zh=near, zl=me.zl),
        me.at(zh=z_order[3], zl=1 - me.zl),
    ]

    def f_copy(turn, d):
        piece = keys.at[base + z_order[turn], me.last, me.first]
        i = turn * 3 + d - 1
        return remote(piece, piece, f_send.at[i], f_recv.at[i], firsts[d])

    def rows_copy(i):
        return remote(my_rows, my_rows, z_send.at[i], z_recv.at[me.zh], z_to[i])

    def piece_copy(i):
        return remote(my_piece, my_piece, z_send.at[i], z_recv.at[me.zh], z_to[i])

    def rows_wait(turn):
        rows = keys.at[base + z_order[turn], me.last]
        remote(rows, rows, z_send.at[0], z_recv.at[z_order[turn]], z_to[0]).wait_recv()

    def piece_wait(turn):
        piece = keys.at[base + z_order[turn], me.last, me.first]
        remote(piece, piece, z_send.at[0], z_recv.at[z_order[turn]], z_to[0]).wait_recv()

    def z_at(turn):
        return z_order[turn] if isinstance(turn, int) else pick(turn, z_order)

    def l_copy(turn, d):
        rows = keys.at[base + z_at(turn), me.last]
        i = turn * 3 + d - 1
        return remote(rows, rows, l_send.at[i], l_recv.at[i], lasts[d])

    def s_copy(turn):
        rows = keys.at[base + z_at(turn)]
        return remote(rows, rows, s_send.at[turn], s_recv.at[turn], sibling)

    def l_sends(turn):
        for d in (2, 1, 3):
            l_copy(turn, d).start()

    def f_sends(turn):
        for d in (2, 1, 3):
            f_copy(turn, d).start()

    def f_done(turn):
        for d in (1, 3, 2):
            f_copy(turn, d).wait_recv()
        l_sends(turn)

    @pl.when(me.c == 0)
    def _():
        for i in range(3):
            rows_copy(i).start()
        l_sends(0)

    @pl.when(me.c == 1)
    def _():
        f_sends(0)
        for i in (2, 1, 0):
            piece_copy(i).start()

    loads[0].wait()
    chunk = lax.broadcasted_iota(jnp.int32, (CHUNKS, CHUNK), 0)
    lane = lax.broadcasted_iota(jnp.int32, (CHUNKS, CHUNK), 1)
    side, k_z = chunk // 4, chunk % 4
    k_last, k_first, k_r = lane // 64, (lane // 16) % 4, lane % 16
    slot = 2 * (k_z * 4 + jnp.where(side == 0, k_last, k_first)) + side
    held = jnp.zeros((CHUNKS, CHUNK), jnp.int32)
    for i in range(32):
        held = jnp.where(slot == i, block_order[i], held)
    key_pos[...] = held * HALF + jnp.where(side == 0, k_first, k_last) * PIECE + k_r
    token = lax.broadcasted_iota(jnp.int32, (ROWS, CHUNK), 0)
    query_pos[...] = (
        jnp.where(token < HALF, block_order[2 * ctx], block_order[2 * ctx + 1]) * HALF + token % HALF
    )
    tops[...] = jnp.full(tops.shape, -1e30, F32)
    outs[...] = jnp.zeros(outs.shape, F32)
    totals[...] = jnp.zeros(totals.shape, F32)
    q_acc[...] = jnp.zeros(q_acc.shape, F32)

    for load in loads[1:2] + loads[3:4]:
        load.wait()
    for h in range(MAPS):
        q_cat[h] = jnp.concatenate(
            [queries[:, h * D_QK : (h + 1) * D_QK], jnp.zeros((ROWS, 256 - D_QK), BF16)], axis=1
        )
        rows, columns = pl.ds(h % 2 * ROWS, ROWS), h % 2 * D_NOPE
        q_nope[h // 2, rows, columns : columns + D_NOPE] = q_cat[h, :, 0:D_NOPE]
        q_nope[h // 2, rows, D_NOPE - columns : 2 * D_NOPE - columns] = jnp.zeros((ROWS, D_NOPE), BF16)
        q_rope[h * ROWS : (h + 1) * ROWS, :] = q_cat[h, :, D_NOPE:256]
    for load in loads[4:]:
        load.wait()

    @pl.when(me.c == 0)
    def _():
        for turn in (1, 2):
            rows_wait(turn)
            l_sends(turn)

    @pl.when(me.c == 1)
    def _():
        f_done(0)
        for turn in (1, 2, 3):
            piece_wait(turn)
            f_sends(turn)
        for turn in (1, 2):
            f_done(turn)

    def absorb(chunks):
        spans = [slice(n * CHUNK, (n + 1) * CHUNK) for n in range(len(chunks))]
        tokens = [keys[i].reshape(CHUNK, WIDE) for i in chunks]
        latent = jnp.concatenate([part[:, 0:D_LAT] for part in tokens], axis=0)
        nope = dot(latent, key_weight[...]).astype(BF16)
        value = dot(latent, value_weight[...]).astype(BF16)
        seen = [key_pos[pl.ds(i, 1), :] <= query_pos[...] for i in chunks]
        for i, span, part in zip(chunks, spans, tokens):
            for p in range(PAIRS_DEV):
                values[i, p] = value[span, p * PAIR_WIDTH : (p + 1) * PAIR_WIDTH]
            for h in range(MAPS):
                k_cat[i, h, :, 0:D_NOPE] = nope[span, h * D_NOPE : (h + 1) * D_NOPE]
                k_cat[i, h, :, D_NOPE:256] = part[:, D_LAT:WIDE]
        for p in range(PAIRS_DEV):
            both, shrinks = [], []
            for m in range(2):
                h = 2 * p + m
                tiles = [
                    jnp.where(mask, dot(q_cat[h], k_cat[i, h], NT), -jnp.inf) for i, mask in zip(chunks, seen)
                ]
                highest = functools.reduce(jnp.maximum, tiles)
                top = jnp.maximum(tops[h], jnp.max(highest, axis=1, keepdims=True))
                shrink = jnp.exp2((tops[h] - top) * EXPONENT)
                wide_top = jnp.concatenate([top, top], axis=1)
                weights = [jnp.exp2((tile - wide_top) * EXPONENT) for tile in tiles]
                tops[h] = top
                total = functools.reduce(jnp.add, weights)
                totals[h] = totals[h] * shrink + (total[:, 0:128] + total[:, 128:256])
                for i, weight in zip(chunks, weights):
                    tops_then[i, h] = top
                    scores[i, h] = weight
                both.append(jnp.concatenate([weight.astype(BF16) for weight in weights], axis=1))
                shrinks.append(jnp.concatenate([shrink, shrink], axis=1))
            outs[p] = outs[p] * jnp.concatenate(shrinks, axis=0) + dot(
                jnp.concatenate(both, axis=0), value[:, p * PAIR_WIDTH : (p + 1) * PAIR_WIDTH]
            )

    def own_ready(turn):
        for d in (1, 3, 2):
            l_copy(turn, d).wait_recv()
        s_copy(turn).start()

    own_ready(0)
    absorb([base + z_order[0]])

    @pl.when(me.c == 0)
    def _():
        rows_wait(3)

    @pl.when(me.c == 1)
    def _():
        for d in (1, 3, 2):
            f_copy(3, d).wait_recv()

    for d in (2, 1, 3):
        l_copy(1, d).wait_send()
    l_sends(3)

    def expand(turn, carry):
        own_ready(turn)
        s_copy(turn - 1).wait_recv()
        absorb([other + z_at(turn - 1), base + z_at(turn)])
        return carry

    lax.fori_loop(1, 4, expand, 0)
    s_copy(3).wait_recv()
    absorb([other + z_order[3]])

    for p in range(PAIRS_DEV):
        lam_p = lam[p]
        maps = []
        for m in range(2):
            h = 2 * p + m
            inverse = 1.0 / jnp.sum(totals[h], axis=1, keepdims=True)
            totals[h] = jnp.broadcast_to(inverse, (ROWS, 128))
            maps.append(outs[p, m * ROWS : (m + 1) * ROWS] * inverse)
        mixed = maps[0] - lam_p * maps[1]
        inv_root = lax.rsqrt(jnp.mean(mixed * mixed, axis=1, keepdims=True) + EPS)
        normed = mixed * inv_root
        scaled = out_grad[:, p * PAIR_WIDTH : (p + 1) * PAIR_WIDTH].astype(F32) * gain[
            :, p * PAIR_WIDTH : (p + 1) * PAIR_WIDTH
        ]
        d_mixed = (scaled - normed * jnp.mean(scaled * normed, axis=1, keepdims=True)) * inv_root
        lowered[p] = d_mixed.astype(BF16)
        deltas[2 * p] = jnp.broadcast_to(jnp.sum(d_mixed * maps[0], axis=1, keepdims=True), (ROWS, 128))
        deltas[2 * p + 1] = jnp.broadcast_to(
            -lam_p * jnp.sum(d_mixed * maps[1], axis=1, keepdims=True), (ROWS, 128)
        )

    def t_copy(turn):
        return remote(part.at[BACK_STEP[1, turn]], from_s.at[turn], t_send.at[turn], t_recv.at[turn], sibling)

    def p_copy(turn, d):
        rows = part.at[BACK_STEP[0, turn], lax.rem(me.last + d, 4)]
        i = turn * 3 + d - 1
        return remote(rows, from_l.at[turn, d - 1], p_send.at[i], p_recv.at[i], lasts[d])

    def g_copy(turn, d):
        piece = middle.at[turn, lax.rem(me.first + d, 4)]
        i = turn * 3 + d - 1
        return remote(piece, from_f.at[turn, d - 1], g_send.at[i], g_recv.at[i], firsts[d])

    def add_own(turn):
        t_copy(turn).wait_recv()
        there = part.at[BACK_STEP[0, turn]]
        there[...] = total_of([there[...], from_s[turn]]).astype(BF16)
        for d in (2, 1, 3):
            p_copy(turn, d).start()

    def add_last(turn):
        for d in (1, 3, 2):
            p_copy(turn, d).wait_recv()
        middle[turn] = total_of(
            [part[BACK_STEP[0, turn], me.last]] + [from_l[turn, d] for d in range(3)]
        ).astype(BF16)
        for d in (2, 1, 3):
            g_copy(turn, d).start()

    def chunk_grads(step):
        theirs = pick(step, BACK_SIDE)
        i = base * (1 - theirs) + other * theirs + pick(pick(step, BACK_TURN), z_order)
        d_nope = []
        d_value = []
        d_all = []
        for p in range(PAIRS_DEV):
            lam_p = lam[p]
            grad = lowered[p]
            through = dot(grad, values[i, p], NT)
            probs = []
            for m in range(2):
                h = 2 * p + m
                share = jnp.exp2((tops_then[i, h] - tops[h]) * EXPONENT) * (totals[h] * LOGIT_SCALE)
                probs.append(scores[i, h] * jnp.concatenate([share, share], axis=1))
            merged = probs[0] * (1 / LOGIT_SCALE) - probs[1] * (lam_p * (1 / LOGIT_SCALE))
            d_value.append(dot(merged.astype(BF16), grad, TN).astype(BF16))
            pair = []
            for m in range(2):
                h = 2 * p + m
                delta = jnp.concatenate([deltas[h], deltas[h]], axis=1)
                inner = through if m == 0 else -lam_p * through
                d_score = (probs[m] * (inner - delta)).astype(BF16)
                d_scores[i, h] = d_score
                pair.append(d_score)
            d_nope.append(dot(jnp.concatenate(pair, axis=0), q_nope[p], TN).astype(BF16))
            d_all.extend(pair)
        d_rope = dot(jnp.concatenate(d_all, axis=0), q_rope[...], TN)
        d_latent = dot(jnp.concatenate(d_nope, axis=1), key_weight[...], NT)
        d_latent = d_latent + dot(jnp.concatenate(d_value, axis=1), value_weight[...], NT)
        part[step, :, :, :, 0:D_LAT] = d_latent.astype(BF16).reshape(4, 4, PIECE, D_LAT)
        part[step, :, :, :, D_LAT:WIDE] = d_rope.astype(BF16).reshape(4, 4, PIECE, WIDE - D_LAT)

    def backward(pair, carry):
        chunk_grads(2 * pair)
        chunk_grads(2 * pair + 1)
        for turn in (3, 2, 1, 0):

            @pl.when(pair == BACK_STEP[1, turn] // 2)
            def _(turn=turn):
                t_copy(turn).start()

        for turn in (3, 2, 1, 0):

            @pl.when(pair == BACK_STEP[0, turn] // 2)
            def _(turn=turn):
                add_own(turn)

        return carry

    lax.fori_loop(0, CHUNKS // 2, backward, 0)
    add_last(3)
    add_last(2)

    def to_queries(i, carry):
        for h in range(MAPS):
            q_acc[h] += dot(d_scores[i, h], k_cat[i, h])
        return carry

    lax.fori_loop(0, CHUNKS, to_queries, 0)
    for h in range(MAPS):
        query_grad[:, h * D_QK : (h + 1) * D_QK] = q_acc[h, :, 0:D_QK].astype(BF16)

    stores = [
        pltpu.make_async_copy(query_grad, query_hbm, out_sem.at[0]),
        pltpu.make_async_copy(result, result_hbm, out_sem.at[1]),
    ]
    stores[0].start()
    z_mine = me.zh * 2 + me.zl

    def y_copy(turn, zl):
        i = turn * 2 + zl
        device = me.at(zh=z_order[turn], zl=zl)
        return remote(small.at[turn], from_z.at[z_mine], y_send.at[i], y_recv.at[z_mine], device)

    own_y = remote(
        small.at[0], from_z.at[z_mine], y_send.at[0], y_recv.at[z_mine], me.at(zl=1 - me.zl)
    )

    def add_first(turn):
        for d in (1, 3, 2):
            g_copy(turn, d).wait_recv()
        small[turn] = total_of(
            [middle[turn, me.first]] + [from_f[turn, d] for d in range(3)]
        ).astype(BF16)
        if turn:
            for zl in (0, 1):
                y_copy(turn, zl).start()
        else:
            own_y.start()

    @pl.when(me.c == 0)
    def _():
        for i in range(3):
            rows_copy(i).wait_send()

    @pl.when(me.c == 1)
    def _():
        for i in range(3):
            piece_copy(i).wait_send()
        for turn in range(4):
            for d in (1, 2, 3):
                f_copy(turn, d).wait_send()

    early = [s_copy(turn) for turn in range(4)] + [t_copy(turn) for turn in range(4)]
    early += [l_copy(turn, d) for turn in (0, 2, 3) for d in (1, 2, 3)]
    early += [p_copy(turn, d) for turn in (3, 2) for d in (1, 2, 3)]
    for copy in early:
        copy.wait_send()
    add_first(3)
    add_first(2)
    add_last(1)
    add_last(0)
    add_first(1)
    add_first(0)
    from_z[z_mine] = small[0]
    for d in range(1, 8):
        z = lax.rem(z_mine + d, 8)
        there = from_z.at[z]
        remote(there, there, y_send.at[0], y_recv.at[z], z_line[0]).wait_recv()
    place = me.c * 4 + me.y
    result[place] = total_of([from_z[z] for z in range(8)]).astype(BF16)

    def e_copy(d):
        piece = result.at[place]
        return remote(piece, piece, e_send.at[d - 1], e_recv.at[d - 1], y_line[d - 1])

    def r_copy(d):
        piece = result.at[me.c * 4 + lax.rem(me.y + 4 - d, 4)]
        return remote(piece, piece, r_send.at[d], r_recv.at[d], sibling)

    for d in (2, 1, 3):
        e_copy(d).start()
    r_copy(0).start()
    for d in (1, 3, 2):
        e_copy(d).wait_recv()
        r_copy(d).start()
    for d in range(4):
        r_copy(d).wait_recv()
    stores[1].start()
    sent = [p_copy(turn, d) for turn in (1, 0) for d in (1, 2, 3)]
    sent += [g_copy(turn, d) for turn in range(4) for d in (1, 2, 3)]
    sent += [y_copy(turn, zl) for turn in (1, 2, 3) for zl in (0, 1)] + [own_y]
    sent += [e_copy(d) for d in (1, 2, 3)] + [r_copy(d) for d in range(4)]
    for copy in sent:
        copy.wait_send()
    for store in stores:
        store.wait()


def copy_out(query_in, result_in, query_out, latent_out, rope_out, query, result, latent, rope, in_sem, out_sem):
    reads = [
        pltpu.make_async_copy(result_in, result, in_sem.at[0]),
        pltpu.make_async_copy(query_in, query, in_sem.at[1]),
    ]
    writes = [
        pltpu.make_async_copy(query, query_out, out_sem.at[0]),
        pltpu.make_async_copy(latent, latent_out, out_sem.at[1]),
        pltpu.make_async_copy(rope, rope_out, out_sem.at[2]),
    ]
    for read in reads:
        read.start()
    reads[0].wait()
    everything = result[...].reshape(ROWS, WIDE)
    rope[...] = everything[:, D_LAT:WIDE].astype(F32).T[0:D_ROPE].astype(BF16)
    writes[2].start()
    latent[...] = everything[:, 0:D_LAT]
    writes[1].start()
    reads[1].wait()
    writes[0].start()
    for write in writes:
        write.wait()


VMEM = pl.BlockSpec(memory_space=pltpu.VMEM)
SMEM = pl.BlockSpec(memory_space=pltpu.SMEM)
ANY = pl.BlockSpec(memory_space=pl.ANY)
DMA = pltpu.SemaphoreType.DMA


OUTS = (
    jax.ShapeDtypeStruct((ROWS, MAPS * D_QK), BF16),
    jax.ShapeDtypeStruct((ROWS, D_LAT), BF16),
    jax.ShapeDtypeStruct((D_ROPE, ROWS), BF16),
)


def fused(*operands):
    piece = (PIECE, WIDE)
    outs = pl.pallas_call(
        fused_kernel,
        out_shape=(OUTS[0], jax.ShapeDtypeStruct((8,) + piece, BF16)),
        in_specs=[ANY] * 9,
        out_specs=(ANY, ANY),
        scratch_shapes=[
            pltpu.VMEM((ROWS, MAPS * D_QK), BF16),
            pltpu.SMEM((PAIRS_DEV,), F32),
            pltpu.SMEM((32,), jnp.int32),
            pltpu.VMEM((1, 512), F32),
            pltpu.VMEM((ROWS, MAPS * D_QK), BF16),
            pltpu.VMEM((D_ROPE, ROWS), BF16),
            pltpu.VMEM((8, PIECE, 128), BF16),
            pltpu.VMEM((D_LAT, 512), BF16),
            pltpu.VMEM((D_LAT, 512), BF16),
            pltpu.VMEM((ROWS, 512), BF16),
            pltpu.VMEM((CHUNKS, 4, 4) + piece, BF16),
            pltpu.VMEM((CHUNKS, CHUNK), jnp.int32),
            pltpu.VMEM((ROWS, CHUNK), jnp.int32),
            pltpu.VMEM((MAPS, ROWS, 256), BF16),
            pltpu.VMEM((PAIRS_DEV, 2 * ROWS, 2 * D_NOPE), BF16),
            pltpu.VMEM((MAPS * ROWS, 128), BF16),
            pltpu.VMEM((CHUNKS, MAPS, CHUNK, 256), BF16),
            pltpu.VMEM((CHUNKS, PAIRS_DEV, CHUNK, PAIR_WIDTH), BF16),
            pltpu.VMEM((CHUNKS, MAPS, ROWS, CHUNK), F32),
            pltpu.VMEM((CHUNKS, MAPS, ROWS, CHUNK), BF16),
            pltpu.VMEM((MAPS, ROWS, 128), F32),
            pltpu.VMEM((CHUNKS, MAPS, ROWS, 128), F32),
            pltpu.VMEM((PAIRS_DEV, 2 * ROWS, PAIR_WIDTH), F32),
            pltpu.VMEM((MAPS, ROWS, 128), F32),
            pltpu.VMEM((PAIRS_DEV, ROWS, PAIR_WIDTH), BF16),
            pltpu.VMEM((MAPS, ROWS, 128), F32),
            pltpu.VMEM((MAPS, ROWS, 256), F32),
            pltpu.VMEM((CHUNKS, 4, 4) + piece, BF16),
            pltpu.VMEM((4, 4, 4) + piece, BF16),
            pltpu.VMEM((4, 3, 4) + piece, BF16),
            pltpu.VMEM((4, 4) + piece, BF16),
            pltpu.VMEM((4, 3) + piece, BF16),
            pltpu.VMEM((4,) + piece, BF16),
            pltpu.VMEM((8,) + piece, BF16),
            pltpu.VMEM((8,) + piece, BF16),
        ]
        + [DMA((n,)) for n in (9, 2, 12, 12, 3, 4, 12, 12, 4, 4, 4, 4, 12, 12, 12, 12, 8, 8, 3, 3, 4, 4)],
        compiler_params=pltpu.CompilerParams(
            collective_id=0, has_side_effects=True, vmem_limit_bytes=56 << 20
        ),
        name="fused",
    )(*operands)
    return pl.pallas_call(
        copy_out,
        out_shape=OUTS,
        in_specs=[ANY] * 2,
        out_specs=(ANY, ANY, ANY),
        scratch_shapes=[pltpu.VMEM(OUTS[0].shape, BF16), pltpu.VMEM((8,) + piece, BF16)]
        + [pltpu.VMEM(out.shape, BF16) for out in OUTS[1:]]
        + [DMA((2,)), DMA((3,))],
        name="copy_out",
    )(*outs)


def on_device(
    queries, latent, rope_key, key_weight, value_weight, lambda_pair, norm_gain, out_grad, block_order
):
    query_grad, latent_grad, rope_grad = fused(
        lambda_pair, block_order, norm_gain.reshape(1, -1), queries, latent.reshape(8, PIECE, D_LAT), rope_key.T,
        key_weight, value_weight, out_grad,
    )
    return (query_grad, latent_grad, rope_grad.T)


def solution(mesh):
    return jax.shard_map(
        on_device,
        mesh=mesh,
        in_specs=(
            P("ctx", "head"),
            P("ctx", None),
            P("ctx", None),
            P(None, "head"),
            P(None, "head"),
            P("head"),
            P("head"),
            P("ctx", "head"),
            P(),
        ),
        out_specs=(P("ctx", "head"), P("ctx", None), P("ctx", None)),
        check_vma=False,
    )
```

```python
import functools

import jax
import jax.numpy as jnp
from jax import lax
from jax.experimental import pallas as pl
from jax.experimental.pallas import tpu as pltpu
from jax.sharding import PartitionSpec as P

MESH = pl.DeviceIdType.MESH
D_LAT = 512
D_NOPE = 128
D_ROPE = 64
D_QK = D_NOPE + D_ROPE
PAIR_WIDTH = 256
ROWS = 128
WIDE = 640
HALF = 64
CHUNKS = 8
CHUNK = 256
PIECE = 16
MAPS = 4
PAIRS_DEV = 2
LOGIT_SCALE = D_QK**-0.5
EXPONENT = LOGIT_SCALE * 1.4426950408889634
EPS = 1e-6
F32 = jnp.float32
BF16 = jnp.bfloat16


class Place:
    def __init__(self):
        ctx, head = lax.axis_index("ctx"), lax.axis_index("head")
        self.x, self.zh = lax.rem(ctx, 4), lax.div(ctx, 4)
        self.y = lax.div(head, 4)
        self.zl = lax.rem(lax.div(head, 2), 2)
        self.c = lax.rem(head, 2)
        self.o = 1 - self.c
        self.first = self.y * self.o + self.x * self.c
        self.last = self.x * self.o + self.y * self.c

    def at(self, x=None, y=None, zh=None, zl=None, c=None):
        x = self.x if x is None else x
        y = self.y if y is None else y
        zh = self.zh if zh is None else zh
        zl = self.zl if zl is None else zl
        c = self.c if c is None else c
        return (zh * 4 + x, y * 4 + zl * 2 + c)

    def first_peer(self, d):
        return self.at(x=lax.rem(self.x + d * self.c, 4), y=lax.rem(self.y + d * self.o, 4))

    def last_peer(self, d):
        return self.at(x=lax.rem(self.x + d * self.o, 4), y=lax.rem(self.y + d * self.c, 4))

    def z_peer(self, d):
        z = lax.rem(self.zh * 2 + self.zl + d, 8)
        return self.at(zh=lax.div(z, 2), zl=lax.rem(z, 2))

    def sibling(self):
        return self.at(c=self.o)


def remote(src, dst, send, recv, device):
    return pltpu.make_async_remote_copy(
        src_ref=src, dst_ref=dst, send_sem=send, recv_sem=recv, device_id=device, device_id_type=MESH
    )


def greet(devices, count):
    barrier = pltpu.get_barrier_semaphore()
    for device in devices:
        pl.semaphore_signal(barrier, inc=1, device_id=device, device_id_type=MESH)
    pl.semaphore_wait(barrier, count)


NT = (((1,), (1,)), ((), ()))
TN = (((0,), (0,)), ((), ()))


def dot(a, b, dims=None):
    if dims is None:
        return jnp.dot(a, b, preferred_element_type=F32)
    return lax.dot_general(a, b, dims, preferred_element_type=F32)


def total_of(parts):
    total = parts[0].astype(F32)
    for part in parts[1:]:
        total = total + part.astype(F32)
    return total


def pick(step, table):
    value = jnp.int32(table[0])
    for i in range(1, len(table)):
        value = jnp.where(step == i, jnp.int32(table[i]), value)
    return value


BACK_SIDE = (1, 1, 0, 1, 0, 1, 0, 0)
BACK_TURN = (3, 2, 3, 1, 2, 0, 1, 0)
BACK_STEP = {(side, turn): i for i, (side, turn) in enumerate(zip(BACK_SIDE, BACK_TURN))}


def fused_kernel(
    lam_hbm, order_hbm, gain_hbm, queries_hbm, latent_hbm, rope_hbm, key_weight_hbm, value_weight_hbm, out_grad_hbm,
    query_grad, result,
    lam, block_order, gain, queries, rope_in, rope_rows, key_weight, value_weight, out_grad,
    keys, key_pos, query_pos, q_cat, q_nope, q_rope, k_cat, values, scores, d_scores, tops, tops_then, outs, totals, lowered, deltas, q_acc,
    part, from_s, from_l, middle, from_f, small, from_z,
    in_sem, f_send, f_recv, z_send, z_recv, l_send, l_recv, s_send, s_recv,
    t_send, t_recv, p_send, p_recv, g_send, g_recv, y_send, y_recv, e_send, e_recv, r_send, r_recv,
):
    me = Place()
    ctx = me.zh * 4 + me.x
    base, other = me.c * 4, me.o * 4
    x_line = [me.at(x=lax.rem(me.x + d, 4)) for d in (1, 2, 3)]
    y_line = [me.at(y=lax.rem(me.y + d, 4)) for d in (1, 2, 3)]
    z_line = [me.z_peer(d) for d in range(1, 8)]
    firsts = {d: me.first_peer(d) for d in (1, 2, 3)}
    lasts = {d: me.last_peer(d) for d in (1, 2, 3)}
    sibling = me.sibling()
    near = lax.rem(me.zh + 3 - 2 * me.zl, 4)
    z_order = [me.zh, near, lax.rem(me.zh + 1 + 2 * me.zl, 4), lax.rem(me.zh + 2, 4)]
    my_rows = keys.at[base + me.zh, me.last]
    my_piece = my_rows.at[me.first]
    loads = [
        pltpu.make_async_copy(order_hbm, block_order, in_sem.at[0]),
        pltpu.make_async_copy(lam_hbm, lam, in_sem.at[1]),
        pltpu.make_async_copy(rope_hbm, rope_in, in_sem.at[2]),
        pltpu.make_async_copy(queries_hbm, queries, in_sem.at[3]),
        pltpu.make_async_copy(key_weight_hbm, key_weight, in_sem.at[4]),
        pltpu.make_async_copy(value_weight_hbm, value_weight, in_sem.at[5]),
        pltpu.make_async_copy(out_grad_hbm, out_grad, in_sem.at[6]),
        pltpu.make_async_copy(gain_hbm, gain, in_sem.at[7]),
    ]
    whole_load = pltpu.make_async_copy(
        latent_hbm.at[pl.ds(0, 4)], my_rows.at[:, :, pl.ds(0, D_LAT)], in_sem.at[8]
    )
    piece_load = pltpu.make_async_copy(
        latent_hbm.at[4 + me.y], my_piece.at[:, pl.ds(0, D_LAT)], in_sem.at[8]
    )

    @pl.when(me.c == 0)
    def _():
        whole_load.start()

    @pl.when(me.c == 1)
    def _():
        piece_load.start()

    loads[2].start()
    barrier = pltpu.get_barrier_semaphore()
    greeted = [z_line[i] for i in (3, 2, 4, 1, 5)] + [x_line[1], y_line[1], z_line[0], z_line[6]]
    for device in greeted + [x_line[0], x_line[2], y_line[0], y_line[2], sibling]:
        pl.semaphore_signal(barrier, inc=1, device_id=device, device_id_type=MESH)
    loads[0].start()
    loads[1].start()
    for load in loads[3:]:
        load.start()

    loads[2].wait()
    rope_rows[:, :, 0:D_ROPE] = rope_in[...].astype(F32).T.astype(BF16).reshape(8, PIECE, D_ROPE)
    rope_rows[:, :, D_ROPE:128] = jnp.zeros((8, PIECE, 128 - D_ROPE), BF16)

    @pl.when(me.c == 0)
    def _():
        whole_load.wait()
        my_rows[:, :, D_LAT:WIDE] = rope_rows[0:4]

    @pl.when(me.c == 1)
    def _():
        piece_load.wait()
        my_piece[:, D_LAT:WIDE] = rope_rows[4 + me.y]

    pl.semaphore_wait(barrier, 14)

    z_to = [
        me.at(zh=near, zl=1 - me.zl),
        me.at(zh=near, zl=me.zl),
        me.at(zh=z_order[3], zl=1 - me.zl),
    ]

    def f_copy(turn, d):
        piece = keys.at[base + z_order[turn], me.last, me.first]
        i = turn * 3 + d - 1
        return remote(piece, piece, f_send.at[i], f_recv.at[i], firsts[d])

    def rows_copy(i):
        return remote(my_rows, my_rows, z_send.at[i], z_recv.at[me.zh], z_to[i])

    def piece_copy(i):
        return remote(my_piece, my_piece, z_send.at[i], z_recv.at[me.zh], z_to[i])

    def rows_wait(turn):
        rows = keys.at[base + z_order[turn], me.last]
        remote(rows, rows, z_send.at[0], z_recv.at[z_order[turn]], z_to[0]).wait_recv()

    def piece_wait(turn):
        piece = keys.at[base + z_order[turn], me.last, me.first]
        remote(piece, piece, z_send.at[0], z_recv.at[z_order[turn]], z_to[0]).wait_recv()

    def z_at(turn):
        return z_order[turn] if isinstance(turn, int) else pick(turn, z_order)

    def l_copy(turn, d):
        rows = keys.at[base + z_at(turn), me.last]
        i = turn * 3 + d - 1
        return remote(rows, rows, l_send.at[i], l_recv.at[i], lasts[d])

    def s_copy(turn):
        rows = keys.at[base + z_at(turn)]
        return remote(rows, rows, s_send.at[turn], s_recv.at[turn], sibling)

    def l_sends(turn):
        for d in (2, 1, 3):
            l_copy(turn, d).start()

    def f_sends(turn):
        for d in (2, 1, 3):
            f_copy(turn, d).start()

    def f_done(turn):
        for d in (1, 3, 2):
            f_copy(turn, d).wait_recv()
        l_sends(turn)

    @pl.when(me.c == 0)
    def _():
        for i in range(3):
            rows_copy(i).start()
        l_sends(0)

    @pl.when(me.c == 1)
    def _():
        f_sends(0)
        for i in (2, 1, 0):
            piece_copy(i).start()

    loads[0].wait()
    chunk = lax.broadcasted_iota(jnp.int32, (CHUNKS, CHUNK), 0)
    lane = lax.broadcasted_iota(jnp.int32, (CHUNKS, CHUNK), 1)
    side, k_z = chunk // 4, chunk % 4
    k_last, k_first, k_r = lane // 64, (lane // 16) % 4, lane % 16
    slot = 2 * (k_z * 4 + jnp.where(side == 0, k_last, k_first)) + side
    held = jnp.zeros((CHUNKS, CHUNK), jnp.int32)
    for i in range(32):
        held = jnp.where(slot == i, block_order[i], held)
    key_pos[...] = held * HALF + jnp.where(side == 0, k_first, k_last) * PIECE + k_r
    token = lax.broadcasted_iota(jnp.int32, (ROWS, CHUNK), 0)
    query_pos[...] = (
        jnp.where(token < HALF, block_order[2 * ctx], block_order[2 * ctx + 1]) * HALF + token % HALF
    )
    tops[...] = jnp.full(tops.shape, -1e30, F32)
    outs[...] = jnp.zeros(outs.shape, F32)
    totals[...] = jnp.zeros(totals.shape, F32)
    q_acc[...] = jnp.zeros(q_acc.shape, F32)

    for load in loads[1:2] + loads[3:4]:
        load.wait()
    for h in range(MAPS):
        q_cat[h] = jnp.concatenate(
            [queries[:, h * D_QK : (h + 1) * D_QK], jnp.zeros((ROWS, 256 - D_QK), BF16)], axis=1
        )
        rows, columns = pl.ds(h % 2 * ROWS, ROWS), h % 2 * D_NOPE
        q_nope[h // 2, rows, columns : columns + D_NOPE] = q_cat[h, :, 0:D_NOPE]
        q_nope[h // 2, rows, D_NOPE - columns : 2 * D_NOPE - columns] = jnp.zeros((ROWS, D_NOPE), BF16)
        q_rope[h * ROWS : (h + 1) * ROWS, :] = q_cat[h, :, D_NOPE:256]
    for load in loads[4:]:
        load.wait()

    @pl.when(me.c == 0)
    def _():
        for turn in (1, 2):
            rows_wait(turn)
            l_sends(turn)

    @pl.when(me.c == 1)
    def _():
        f_done(0)
        for turn in (1, 2, 3):
            piece_wait(turn)
            f_sends(turn)
        for turn in (1, 2):
            f_done(turn)

    def absorb(chunks):
        spans = [slice(n * CHUNK, (n + 1) * CHUNK) for n in range(len(chunks))]
        tokens = [keys[i].reshape(CHUNK, WIDE) for i in chunks]
        latent = jnp.concatenate([part[:, 0:D_LAT] for part in tokens], axis=0)
        nope = dot(latent, key_weight[...]).astype(BF16)
        value = dot(latent, value_weight[...]).astype(BF16)
        seen = [key_pos[pl.ds(i, 1), :] <= query_pos[...] for i in chunks]
        for i, span, part in zip(chunks, spans, tokens):
            for p in range(PAIRS_DEV):
                values[i, p] = value[span, p * PAIR_WIDTH : (p + 1) * PAIR_WIDTH]
            for h in range(MAPS):
                k_cat[i, h, :, 0:D_NOPE] = nope[span, h * D_NOPE : (h + 1) * D_NOPE]
                k_cat[i, h, :, D_NOPE:256] = part[:, D_LAT:WIDE]
        for p in range(PAIRS_DEV):
            both, shrinks = [], []
            for m in range(2):
                h = 2 * p + m
                tiles = [
                    jnp.where(mask, dot(q_cat[h], k_cat[i, h], NT), -jnp.inf) for i, mask in zip(chunks, seen)
                ]
                highest = functools.reduce(jnp.maximum, tiles)
                top = jnp.maximum(tops[h], jnp.max(highest, axis=1, keepdims=True))
                shrink = jnp.exp2((tops[h] - top) * EXPONENT)
                wide_top = jnp.concatenate([top, top], axis=1)
                weights = [jnp.exp2((tile - wide_top) * EXPONENT) for tile in tiles]
                tops[h] = top
                total = functools.reduce(jnp.add, weights)
                totals[h] = totals[h] * shrink + (total[:, 0:128] + total[:, 128:256])
                for i, weight in zip(chunks, weights):
                    tops_then[i, h] = top
                    scores[i, h] = weight
                both.append(jnp.concatenate([weight.astype(BF16) for weight in weights], axis=1))
                shrinks.append(jnp.concatenate([shrink, shrink], axis=1))
            outs[p] = outs[p] * jnp.concatenate(shrinks, axis=0) + dot(
                jnp.concatenate(both, axis=0), value[:, p * PAIR_WIDTH : (p + 1) * PAIR_WIDTH]
            )

    def own_ready(turn):
        for d in (1, 3, 2):
            l_copy(turn, d).wait_recv()
        s_copy(turn).start()

    own_ready(0)
    absorb([base + z_order[0]])

    @pl.when(me.c == 0)
    def _():
        rows_wait(3)

    @pl.when(me.c == 1)
    def _():
        for d in (1, 3, 2):
            f_copy(3, d).wait_recv()

    for d in (2, 1, 3):
        l_copy(1, d).wait_send()
    l_sends(3)

    def expand(turn, carry):
        own_ready(turn)
        s_copy(turn - 1).wait_recv()
        absorb([other + z_at(turn - 1), base + z_at(turn)])
        return carry

    lax.fori_loop(1, 4, expand, 0)
    s_copy(3).wait_recv()
    absorb([other + z_order[3]])

    for p in range(PAIRS_DEV):
        lam_p = lam[p]
        maps = []
        for m in range(2):
            h = 2 * p + m
            inverse = 1.0 / jnp.sum(totals[h], axis=1, keepdims=True)
            totals[h] = jnp.broadcast_to(inverse, (ROWS, 128))
            maps.append(outs[p, m * ROWS : (m + 1) * ROWS] * inverse)
        mixed = maps[0] - lam_p * maps[1]
        inv_root = lax.rsqrt(jnp.mean(mixed * mixed, axis=1, keepdims=True) + EPS)
        normed = mixed * inv_root
        scaled = out_grad[:, p * PAIR_WIDTH : (p + 1) * PAIR_WIDTH].astype(F32) * gain[
            :, p * PAIR_WIDTH : (p + 1) * PAIR_WIDTH
        ]
        d_mixed = (scaled - normed * jnp.mean(scaled * normed, axis=1, keepdims=True)) * inv_root
        lowered[p] = d_mixed.astype(BF16)
        deltas[2 * p] = jnp.broadcast_to(jnp.sum(d_mixed * maps[0], axis=1, keepdims=True), (ROWS, 128))
        deltas[2 * p + 1] = jnp.broadcast_to(
            -lam_p * jnp.sum(d_mixed * maps[1], axis=1, keepdims=True), (ROWS, 128)
        )

    def t_copy(turn):
        return remote(part.at[BACK_STEP[1, turn]], from_s.at[turn], t_send.at[turn], t_recv.at[turn], sibling)

    def p_copy(turn, d):
        rows = part.at[BACK_STEP[0, turn], lax.rem(me.last + d, 4)]
        i = turn * 3 + d - 1
        return remote(rows, from_l.at[turn, d - 1], p_send.at[i], p_recv.at[i], lasts[d])

    def g_copy(turn, d):
        piece = middle.at[turn, lax.rem(me.first + d, 4)]
        i = turn * 3 + d - 1
        return remote(piece, from_f.at[turn, d - 1], g_send.at[i], g_recv.at[i], firsts[d])

    def add_own(turn):
        t_copy(turn).wait_recv()
        there = part.at[BACK_STEP[0, turn]]
        there[...] += from_s[turn]
        for d in (2, 1, 3):
            p_copy(turn, d).start()

    def add_last(turn):
        for d in (1, 3, 2):
            p_copy(turn, d).wait_recv()
        middle[turn] = total_of(
            [part[BACK_STEP[0, turn], me.last]] + [from_l[turn, d] for d in range(3)]
        ).astype(BF16)
        for d in (2, 1, 3):
            g_copy(turn, d).start()

    def chunk_grads(step):
        theirs = pick(step, BACK_SIDE)
        i = base * (1 - theirs) + other * theirs + pick(pick(step, BACK_TURN), z_order)
        d_nope = []
        d_value = []
        d_all = []
        for p in range(PAIRS_DEV):
            lam_p = lam[p]
            grad = lowered[p]
            through = dot(grad, values[i, p], NT)
            probs = []
            for m in range(2):
                h = 2 * p + m
                share = jnp.exp2((tops_then[i, h] - tops[h]) * EXPONENT) * (totals[h] * LOGIT_SCALE)
                probs.append(scores[i, h] * jnp.concatenate([share, share], axis=1))
            merged = probs[0] * (1 / LOGIT_SCALE) - probs[1] * (lam_p * (1 / LOGIT_SCALE))
            d_value.append(dot(merged.astype(BF16), grad, TN).astype(BF16))
            pair = []
            for m in range(2):
                h = 2 * p + m
                delta = jnp.concatenate([deltas[h], deltas[h]], axis=1)
                inner = through if m == 0 else -lam_p * through
                d_score = (probs[m] * (inner - delta)).astype(BF16)
                d_scores[i, h] = d_score
                pair.append(d_score)
            d_nope.append(dot(jnp.concatenate(pair, axis=0), q_nope[p], TN).astype(BF16))
            d_all.extend(pair)
        d_rope = dot(jnp.concatenate(d_all, axis=0), q_rope[...], TN)
        d_latent = dot(jnp.concatenate(d_nope, axis=1), key_weight[...], NT)
        d_latent = d_latent + dot(jnp.concatenate(d_value, axis=1), value_weight[...], NT)
        part[step, :, :, :, 0:D_LAT] = d_latent.astype(BF16).reshape(4, 4, PIECE, D_LAT)
        part[step, :, :, :, D_LAT:WIDE] = d_rope.astype(BF16).reshape(4, 4, PIECE, WIDE - D_LAT)

    def backward(pair, carry):
        chunk_grads(2 * pair)
        chunk_grads(2 * pair + 1)
        for turn in (3, 2, 1, 0):

            @pl.when(pair == BACK_STEP[1, turn] // 2)
            def _(turn=turn):
                t_copy(turn).start()

        for turn in (3, 2, 1, 0):

            @pl.when(pair == BACK_STEP[0, turn] // 2)
            def _(turn=turn):
                add_own(turn)

        return carry

    lax.fori_loop(0, CHUNKS // 2, backward, 0)
    add_last(3)
    add_last(2)

    def to_queries(i, carry):
        for h in range(MAPS):
            q_acc[h] += dot(d_scores[i, h], k_cat[i, h])
        return carry

    lax.fori_loop(0, CHUNKS, to_queries, 0)
    for h in range(MAPS):
        query_grad[:, h * D_QK : (h + 1) * D_QK] = q_acc[h, :, 0:D_QK].astype(BF16)

    z_mine = me.zh * 2 + me.zl

    def y_copy(turn, zl):
        i = turn * 2 + zl
        device = me.at(zh=z_order[turn], zl=zl)
        return remote(small.at[turn], from_z.at[z_mine], y_send.at[i], y_recv.at[z_mine], device)

    own_y = remote(
        small.at[0], from_z.at[z_mine], y_send.at[0], y_recv.at[z_mine], me.at(zl=1 - me.zl)
    )

    def add_first(turn):
        for d in (1, 3, 2):
            g_copy(turn, d).wait_recv()
        small[turn] = total_of(
            [middle[turn, me.first]] + [from_f[turn, d] for d in range(3)]
        ).astype(BF16)
        if turn:
            for zl in (0, 1):
                y_copy(turn, zl).start()
        else:
            own_y.start()

    @pl.when(me.c == 0)
    def _():
        for i in range(3):
            rows_copy(i).wait_send()

    @pl.when(me.c == 1)
    def _():
        for i in range(3):
            piece_copy(i).wait_send()
        for turn in range(4):
            for d in (1, 2, 3):
                f_copy(turn, d).wait_send()

    early = [s_copy(turn) for turn in range(4)] + [t_copy(turn) for turn in range(4)]
    early += [l_copy(turn, d) for turn in (0, 2, 3) for d in (1, 2, 3)]
    early += [p_copy(turn, d) for turn in (3, 2) for d in (1, 2, 3)]
    for copy in early:
        copy.wait_send()
    add_first(3)
    add_first(2)
    add_last(1)
    add_last(0)
    add_first(1)
    add_first(0)
    from_z[z_mine] = small[0]
    for d in range(1, 8):
        z = lax.rem(z_mine + d, 8)
        there = from_z.at[z]
        remote(there, there, y_send.at[0], y_recv.at[z], z_line[0]).wait_recv()
    place = me.c * 4 + me.y
    result[place] = total_of([from_z[z] for z in range(8)]).astype(BF16)

    def e_copy(d):
        piece = result.at[place]
        return remote(piece, piece, e_send.at[d - 1], e_recv.at[d - 1], y_line[d - 1])

    def r_copy(d):
        piece = result.at[me.c * 4 + lax.rem(me.y + 4 - d, 4)]
        return remote(piece, piece, r_send.at[d], r_recv.at[d], sibling)

    for d in (2, 1, 3):
        e_copy(d).start()
    r_copy(0).start()
    for d in (1, 3, 2):
        e_copy(d).wait_recv()
        r_copy(d).start()
    for d in range(4):
        r_copy(d).wait_recv()
    sent = [p_copy(turn, d) for turn in (1, 0) for d in (1, 2, 3)]
    sent += [g_copy(turn, d) for turn in range(4) for d in (1, 2, 3)]
    sent += [y_copy(turn, zl) for turn in (1, 2, 3) for zl in (0, 1)] + [own_y]
    sent += [e_copy(d) for d in (1, 2, 3)] + [r_copy(d) for d in range(4)]
    for copy in sent:
        copy.wait_send()


def copy_out(query, result, query_out, latent_out, rope_out, latent, rope, sem):
    writes = [
        pltpu.make_async_copy(query, query_out, sem.at[0]),
        pltpu.make_async_copy(latent, latent_out, sem.at[1]),
        pltpu.make_async_copy(rope, rope_out, sem.at[2]),
    ]
    writes[0].start()
    everything = result[...].reshape(ROWS, WIDE)
    rope[...] = everything[:, D_LAT:WIDE].astype(F32).T[0:D_ROPE].astype(BF16)
    writes[2].start()
    latent[...] = everything[:, 0:D_LAT]
    writes[1].start()
    for write in writes:
        write.wait()


VMEM = pl.BlockSpec(memory_space=pltpu.VMEM)
SMEM = pl.BlockSpec(memory_space=pltpu.SMEM)
ANY = pl.BlockSpec(memory_space=pl.ANY)
HBM = pl.BlockSpec(memory_space=pltpu.HBM)
DMA = pltpu.SemaphoreType.DMA


OUTS = (
    jax.ShapeDtypeStruct((ROWS, MAPS * D_QK), BF16),
    jax.ShapeDtypeStruct((ROWS, D_LAT), BF16),
    jax.ShapeDtypeStruct((D_ROPE, ROWS), BF16),
)


def fused(*operands):
    piece = (PIECE, WIDE)
    outs = pl.pallas_call(
        fused_kernel,
        out_shape=(pltpu.VMEM(OUTS[0].shape, BF16), pltpu.VMEM((8,) + piece, BF16)),
        in_specs=[HBM] * 9,
        out_specs=(VMEM, VMEM),
        scratch_shapes=[
            pltpu.SMEM((PAIRS_DEV,), F32),
            pltpu.SMEM((32,), jnp.int32),
            pltpu.VMEM((1, 512), F32),
            pltpu.VMEM((ROWS, MAPS * D_QK), BF16),
            pltpu.VMEM((D_ROPE, ROWS), BF16),
            pltpu.VMEM((8, PIECE, 128), BF16),
            pltpu.VMEM((D_LAT, 512), BF16),
            pltpu.VMEM((D_LAT, 512), BF16),
            pltpu.VMEM((ROWS, 512), BF16),
            pltpu.VMEM((CHUNKS, 4, 4) + piece, BF16),
            pltpu.VMEM((CHUNKS, CHUNK), jnp.int32),
            pltpu.VMEM((ROWS, CHUNK), jnp.int32),
            pltpu.VMEM((MAPS, ROWS, 256), BF16),
            pltpu.VMEM((PAIRS_DEV, 2 * ROWS, 2 * D_NOPE), BF16),
            pltpu.VMEM((MAPS * ROWS, 128), BF16),
            pltpu.VMEM((CHUNKS, MAPS, CHUNK, 256), BF16),
            pltpu.VMEM((CHUNKS, PAIRS_DEV, CHUNK, PAIR_WIDTH), BF16),
            pltpu.VMEM((CHUNKS, MAPS, ROWS, CHUNK), F32),
            pltpu.VMEM((CHUNKS, MAPS, ROWS, CHUNK), BF16),
            pltpu.VMEM((MAPS, ROWS, 128), F32),
            pltpu.VMEM((CHUNKS, MAPS, ROWS, 128), F32),
            pltpu.VMEM((PAIRS_DEV, 2 * ROWS, PAIR_WIDTH), F32),
            pltpu.VMEM((MAPS, ROWS, 128), F32),
            pltpu.VMEM((PAIRS_DEV, ROWS, PAIR_WIDTH), BF16),
            pltpu.VMEM((MAPS, ROWS, 128), F32),
            pltpu.VMEM((MAPS, ROWS, 256), F32),
            pltpu.VMEM((CHUNKS, 4, 4) + piece, BF16),
            pltpu.VMEM((4, 4, 4) + piece, BF16),
            pltpu.VMEM((4, 3, 4) + piece, BF16),
            pltpu.VMEM((4, 4) + piece, BF16),
            pltpu.VMEM((4, 3) + piece, BF16),
            pltpu.VMEM((4,) + piece, BF16),
            pltpu.VMEM((8,) + piece, BF16),
        ]
        + [DMA((n,)) for n in (9, 12, 12, 3, 4, 12, 12, 4, 4, 4, 4, 12, 12, 12, 12, 8, 8, 3, 3, 4, 4)],
        compiler_params=pltpu.CompilerParams(
            collective_id=0, has_side_effects=True, vmem_limit_bytes=56 << 20
        ),
        name="fused",
    )(*(pltpu.with_memory_space_constraint(operand, pltpu.HBM) for operand in operands))
    return pl.pallas_call(
        copy_out,
        out_shape=OUTS,
        in_specs=[VMEM] * 2,
        out_specs=(HBM, HBM, HBM),
        scratch_shapes=[pltpu.VMEM(out.shape, BF16) for out in OUTS[1:]] + [DMA((3,))],
        name="copy_out",
    )(*(pltpu.with_memory_space_constraint(out, pltpu.VMEM) for out in outs))


def on_device(
    queries, latent, rope_key, key_weight, value_weight, lambda_pair, norm_gain, out_grad, block_order
):
    query_grad, latent_grad, rope_grad = fused(
        lambda_pair, block_order, norm_gain.reshape(1, -1), queries, latent.reshape(8, PIECE, D_LAT), rope_key.T,
        key_weight, value_weight, out_grad,
    )
    return (query_grad, latent_grad, rope_grad.T)


def solution(mesh):
    return jax.shard_map(
        on_device,
        mesh=mesh,
        in_specs=(
            P("ctx", "head"),
            P("ctx", None),
            P("ctx", None),
            P(None, "head"),
            P(None, "head"),
            P("head"),
            P("head"),
            P("ctx", "head"),
            P(),
        ),
        out_specs=(P("ctx", "head"), P("ctx", None), P("ctx", None)),
        check_vma=False,
    )
```

```python
import functools

import jax
import jax.numpy as jnp
from jax import lax
from jax.experimental import pallas as pl
from jax.experimental.pallas import tpu as pltpu
from jax.sharding import PartitionSpec as P

MESH = pl.DeviceIdType.MESH
D_LAT = 512
D_NOPE = 128
D_ROPE = 64
D_QK = D_NOPE + D_ROPE
PAIR_WIDTH = 256
ROWS = 128
WIDE = 640
HALF = 64
CHUNKS = 8
CHUNK = 256
PIECE = 16
MAPS = 4
PAIRS_DEV = 2
LOGIT_SCALE = D_QK**-0.5
EXPONENT = LOGIT_SCALE * 1.4426950408889634
EPS = 1e-6
F32 = jnp.float32
BF16 = jnp.bfloat16


class Place:
    def __init__(self):
        ctx, head = lax.axis_index("ctx"), lax.axis_index("head")
        self.x, self.zh = lax.rem(ctx, 4), lax.div(ctx, 4)
        self.y = lax.div(head, 4)
        self.zl = lax.rem(lax.div(head, 2), 2)
        self.c = lax.rem(head, 2)
        self.o = 1 - self.c
        self.first = self.y * self.o + self.x * self.c
        self.last = self.x * self.o + self.y * self.c

    def at(self, x=None, y=None, zh=None, zl=None, c=None):
        x = self.x if x is None else x
        y = self.y if y is None else y
        zh = self.zh if zh is None else zh
        zl = self.zl if zl is None else zl
        c = self.c if c is None else c
        return (zh * 4 + x, y * 4 + zl * 2 + c)

    def first_peer(self, d):
        return self.at(x=lax.rem(self.x + d * self.c, 4), y=lax.rem(self.y + d * self.o, 4))

    def last_peer(self, d):
        return self.at(x=lax.rem(self.x + d * self.o, 4), y=lax.rem(self.y + d * self.c, 4))

    def z_peer(self, d):
        z = lax.rem(self.zh * 2 + self.zl + d, 8)
        return self.at(zh=lax.div(z, 2), zl=lax.rem(z, 2))

    def sibling(self):
        return self.at(c=self.o)


def remote(src, dst, send, recv, device):
    return pltpu.make_async_remote_copy(
        src_ref=src, dst_ref=dst, send_sem=send, recv_sem=recv, device_id=device, device_id_type=MESH
    )


def greet(devices, count):
    barrier = pltpu.get_barrier_semaphore()
    for device in devices:
        pl.semaphore_signal(barrier, inc=1, device_id=device, device_id_type=MESH)
    pl.semaphore_wait(barrier, count)


NT = (((1,), (1,)), ((), ()))
TN = (((0,), (0,)), ((), ()))


def dot(a, b, dims=None):
    if dims is None:
        return jnp.dot(a, b, preferred_element_type=F32)
    return lax.dot_general(a, b, dims, preferred_element_type=F32)


def total_of(parts):
    total = parts[0].astype(F32)
    for part in parts[1:]:
        total = total + part.astype(F32)
    return total


def pick(step, table):
    value = jnp.int32(table[0])
    for i in range(1, len(table)):
        value = jnp.where(step == i, jnp.int32(table[i]), value)
    return value


BACK_SIDE = (1, 1, 0, 1, 0, 1, 0, 0)
BACK_TURN = (3, 2, 3, 1, 2, 0, 1, 0)
BACK_STEP = {(side, turn): i for i, (side, turn) in enumerate(zip(BACK_SIDE, BACK_TURN))}


def fused_kernel(
    lam_hbm, order_hbm, gain_hbm, queries_hbm, latent_hbm, rope_hbm, key_weight_hbm, value_weight_hbm, out_grad_hbm,
    query_grad, result,
    lam, block_order, gain, queries, rope_in, rope_rows, key_weight, value_weight, out_grad,
    keys, key_pos, query_pos, q_cat, q_nope, q_rope, k_cat, values, scores, d_scores, tops, tops_then, outs, totals, lowered, deltas, q_acc,
    part, from_s, from_l, middle, from_f, small, from_z, from_far,
    in_sem, f_send, f_recv, z_send, z_recv, l_send, l_recv, s_send, s_recv,
    t_send, t_recv, p_send, p_recv, g_send, g_recv, y_send, y_recv, e_send, e_recv, r_send, r_recv,
):
    me = Place()
    ctx = me.zh * 4 + me.x
    base, other = me.c * 4, me.o * 4
    x_line = [me.at(x=lax.rem(me.x + d, 4)) for d in (1, 2, 3)]
    y_line = [me.at(y=lax.rem(me.y + d, 4)) for d in (1, 2, 3)]
    z_line = [me.z_peer(d) for d in range(1, 8)]
    firsts = {d: me.first_peer(d) for d in (1, 2, 3)}
    lasts = {d: me.last_peer(d) for d in (1, 2, 3)}
    sibling = me.sibling()
    near = lax.rem(me.zh + 3 - 2 * me.zl, 4)
    z_order = [me.zh, near, lax.rem(me.zh + 1 + 2 * me.zl, 4), lax.rem(me.zh + 2, 4)]
    my_rows = keys.at[base + me.zh, me.last]
    my_piece = my_rows.at[me.first]
    loads = [
        pltpu.make_async_copy(order_hbm, block_order, in_sem.at[0]),
        pltpu.make_async_copy(lam_hbm, lam, in_sem.at[1]),
        pltpu.make_async_copy(rope_hbm, rope_in, in_sem.at[2]),
        pltpu.make_async_copy(queries_hbm, queries, in_sem.at[3]),
        pltpu.make_async_copy(key_weight_hbm, key_weight, in_sem.at[4]),
        pltpu.make_async_copy(value_weight_hbm, value_weight, in_sem.at[5]),
        pltpu.make_async_copy(out_grad_hbm, out_grad, in_sem.at[6]),
        pltpu.make_async_copy(gain_hbm, gain, in_sem.at[7]),
    ]
    whole_load = pltpu.make_async_copy(
        latent_hbm.at[pl.ds(0, 4)], my_rows.at[:, :, pl.ds(0, D_LAT)], in_sem.at[8]
    )
    piece_load = pltpu.make_async_copy(
        latent_hbm.at[4 + me.y], my_piece.at[:, pl.ds(0, D_LAT)], in_sem.at[8]
    )

    @pl.when(me.c == 0)
    def _():
        whole_load.start()

    @pl.when(me.c == 1)
    def _():
        piece_load.start()

    loads[2].start()
    barrier = pltpu.get_barrier_semaphore()
    greeted = [z_line[i] for i in (2, 4, 1, 5)] + [x_line[1], y_line[1], z_line[0], z_line[6]]
    for device in greeted + [x_line[0], x_line[2], y_line[0], y_line[2], sibling]:
        pl.semaphore_signal(barrier, inc=1, device_id=device, device_id_type=MESH)
    loads[0].start()
    loads[1].start()
    for load in loads[3:]:
        load.start()

    loads[2].wait()
    rope_rows[:, :, 0:D_ROPE] = rope_in[...].astype(F32).T.astype(BF16).reshape(8, PIECE, D_ROPE)
    rope_rows[:, :, D_ROPE:128] = jnp.zeros((8, PIECE, 128 - D_ROPE), BF16)

    @pl.when(me.c == 0)
    def _():
        whole_load.wait()
        my_rows[:, :, D_LAT:WIDE] = rope_rows[0:4]

    @pl.when(me.c == 1)
    def _():
        piece_load.wait()
        my_piece[:, D_LAT:WIDE] = rope_rows[4 + me.y]

    pl.semaphore_wait(barrier, 13)

    z_to = [
        me.at(zh=near, zl=1 - me.zl),
        me.at(zh=near, zl=me.zl),
        me.at(zh=z_order[3], zl=1 - me.zl),
    ]

    def f_copy(turn, d):
        piece = keys.at[base + z_order[turn], me.last, me.first]
        i = turn * 3 + d - 1
        return remote(piece, piece, f_send.at[i], f_recv.at[i], firsts[d])

    def rows_copy(i):
        return remote(my_rows, my_rows, z_send.at[i], z_recv.at[me.zh], z_to[i])

    def piece_copy(i):
        return remote(my_piece, my_piece, z_send.at[i], z_recv.at[me.zh], z_to[i])

    def rows_wait(turn):
        rows = keys.at[base + z_order[turn], me.last]
        remote(rows, rows, z_send.at[0], z_recv.at[z_order[turn]], z_to[0]).wait_recv()

    def piece_wait(turn):
        piece = keys.at[base + z_order[turn], me.last, me.first]
        remote(piece, piece, z_send.at[0], z_recv.at[z_order[turn]], z_to[0]).wait_recv()

    def z_at(turn):
        return z_order[turn] if isinstance(turn, int) else pick(turn, z_order)

    def l_copy(turn, d):
        rows = keys.at[base + z_at(turn), me.last]
        i = turn * 3 + d - 1
        return remote(rows, rows, l_send.at[i], l_recv.at[i], lasts[d])

    def s_copy(turn):
        rows = keys.at[base + z_at(turn)]
        return remote(rows, rows, s_send.at[turn], s_recv.at[turn], sibling)

    def l_sends(turn):
        for d in (2, 1, 3):
            l_copy(turn, d).start()

    def f_sends(turn):
        for d in (2, 1, 3):
            f_copy(turn, d).start()

    def f_done(turn):
        for d in (1, 3, 2):
            f_copy(turn, d).wait_recv()
        l_sends(turn)

    @pl.when(me.c == 0)
    def _():
        for i in range(3):
            rows_copy(i).start()
        l_sends(0)

    @pl.when(me.c == 1)
    def _():
        f_sends(0)
        for i in (2, 1, 0):
            piece_copy(i).start()

    loads[0].wait()
    chunk = lax.broadcasted_iota(jnp.int32, (CHUNKS, CHUNK), 0)
    lane = lax.broadcasted_iota(jnp.int32, (CHUNKS, CHUNK), 1)
    side, k_z = chunk // 4, chunk % 4
    k_last, k_first, k_r = lane // 64, (lane // 16) % 4, lane % 16
    slot = 2 * (k_z * 4 + jnp.where(side == 0, k_last, k_first)) + side
    held = jnp.zeros((CHUNKS, CHUNK), jnp.int32)
    for i in range(32):
        held = jnp.where(slot == i, block_order[i], held)
    key_pos[...] = held * HALF + jnp.where(side == 0, k_first, k_last) * PIECE + k_r
    token = lax.broadcasted_iota(jnp.int32, (ROWS, CHUNK), 0)
    query_pos[...] = (
        jnp.where(token < HALF, block_order[2 * ctx], block_order[2 * ctx + 1]) * HALF + token % HALF
    )
    tops[...] = jnp.full(tops.shape, -1e30, F32)
    outs[...] = jnp.zeros(outs.shape, F32)
    totals[...] = jnp.zeros(totals.shape, F32)
    q_acc[...] = jnp.zeros(q_acc.shape, F32)

    for load in loads[1:2] + loads[3:4]:
        load.wait()
    for h in range(MAPS):
        q_cat[h] = jnp.concatenate(
            [queries[:, h * D_QK : (h + 1) * D_QK], jnp.zeros((ROWS, 256 - D_QK), BF16)], axis=1
        )
        rows, columns = pl.ds(h % 2 * ROWS, ROWS), h % 2 * D_NOPE
        q_nope[h // 2, rows, columns : columns + D_NOPE] = q_cat[h, :, 0:D_NOPE]
        q_nope[h // 2, rows, D_NOPE - columns : 2 * D_NOPE - columns] = jnp.zeros((ROWS, D_NOPE), BF16)
        q_rope[h * ROWS : (h + 1) * ROWS, :] = q_cat[h, :, D_NOPE:256]
    for load in loads[4:]:
        load.wait()

    @pl.when(me.c == 0)
    def _():
        for turn in (1, 2):
            rows_wait(turn)
            l_sends(turn)

    @pl.when(me.c == 1)
    def _():
        f_done(0)
        for turn in (1, 2, 3):
            piece_wait(turn)
            f_sends(turn)
        for turn in (1, 2):
            f_done(turn)

    def absorb(chunks):
        spans = [slice(n * CHUNK, (n + 1) * CHUNK) for n in range(len(chunks))]
        tokens = [keys[i].reshape(CHUNK, WIDE) for i in chunks]
        latent = jnp.concatenate([part[:, 0:D_LAT] for part in tokens], axis=0)
        nope = dot(latent, key_weight[...]).astype(BF16)
        value = dot(latent, value_weight[...]).astype(BF16)
        seen = [key_pos[pl.ds(i, 1), :] <= query_pos[...] for i in chunks]
        for i, span, part in zip(chunks, spans, tokens):
            for p in range(PAIRS_DEV):
                values[i, p] = value[span, p * PAIR_WIDTH : (p + 1) * PAIR_WIDTH]
            for h in range(MAPS):
                k_cat[i, h, :, 0:D_NOPE] = nope[span, h * D_NOPE : (h + 1) * D_NOPE]
                k_cat[i, h, :, D_NOPE:256] = part[:, D_LAT:WIDE]
        for p in range(PAIRS_DEV):
            both, shrinks = [], []
            for m in range(2):
                h = 2 * p + m
                tiles = [
                    jnp.where(mask, dot(q_cat[h], k_cat[i, h], NT), -jnp.inf) for i, mask in zip(chunks, seen)
                ]
                highest = functools.reduce(jnp.maximum, tiles)
                top = jnp.maximum(tops[h], jnp.max(highest, axis=1, keepdims=True))
                shrink = jnp.exp2((tops[h] - top) * EXPONENT)
                wide_top = jnp.concatenate([top, top], axis=1)
                weights = [jnp.exp2((tile - wide_top) * EXPONENT) for tile in tiles]
                tops[h] = top
                total = functools.reduce(jnp.add, weights)
                totals[h] = totals[h] * shrink + (total[:, 0:128] + total[:, 128:256])
                for i, weight in zip(chunks, weights):
                    tops_then[i, h] = top
                    scores[i, h] = weight
                both.append(jnp.concatenate([weight.astype(BF16) for weight in weights], axis=1))
                shrinks.append(jnp.concatenate([shrink, shrink], axis=1))
            outs[p] = outs[p] * jnp.concatenate(shrinks, axis=0) + dot(
                jnp.concatenate(both, axis=0), value[:, p * PAIR_WIDTH : (p + 1) * PAIR_WIDTH]
            )

    def own_ready(turn):
        for d in (1, 3, 2):
            l_copy(turn, d).wait_recv()
        s_copy(turn).start()

    @pl.when(me.c == 0)
    def _():
        rows_wait(3)

    @pl.when(me.c == 1)
    def _():
        for d in (1, 3, 2):
            f_copy(3, d).wait_recv()

    l_sends(3)

    own_ready(0)
    absorb([base + z_order[0]])

    def expand(turn, carry):
        own_ready(turn)
        s_copy(turn - 1).wait_recv()
        absorb([other + z_at(turn - 1), base + z_at(turn)])
        return carry

    lax.fori_loop(1, 4, expand, 0)
    s_copy(3).wait_recv()
    absorb([other + z_order[3]])

    for p in range(PAIRS_DEV):
        lam_p = lam[p]
        maps = []
        for m in range(2):
            h = 2 * p + m
            inverse = 1.0 / jnp.sum(totals[h], axis=1, keepdims=True)
            totals[h] = jnp.broadcast_to(inverse, (ROWS, 128))
            maps.append(outs[p, m * ROWS : (m + 1) * ROWS] * inverse)
        mixed = maps[0] - lam_p * maps[1]
        inv_root = lax.rsqrt(jnp.mean(mixed * mixed, axis=1, keepdims=True) + EPS)
        normed = mixed * inv_root
        scaled = out_grad[:, p * PAIR_WIDTH : (p + 1) * PAIR_WIDTH].astype(F32) * gain[
            :, p * PAIR_WIDTH : (p + 1) * PAIR_WIDTH
        ]
        d_mixed = (scaled - normed * jnp.mean(scaled * normed, axis=1, keepdims=True)) * inv_root
        lowered[p] = d_mixed.astype(BF16)
        deltas[2 * p] = jnp.broadcast_to(jnp.sum(d_mixed * maps[0], axis=1, keepdims=True), (ROWS, 128))
        deltas[2 * p + 1] = jnp.broadcast_to(
            -lam_p * jnp.sum(d_mixed * maps[1], axis=1, keepdims=True), (ROWS, 128)
        )

    def t_copy(turn):
        return remote(part.at[BACK_STEP[1, turn]], from_s.at[turn], t_send.at[turn], t_recv.at[turn], sibling)

    def p_copy(turn, d):
        rows = part.at[BACK_STEP[0, turn], lax.rem(me.last + d, 4)]
        i = turn * 3 + d - 1
        return remote(rows, from_l.at[turn, d - 1], p_send.at[i], p_recv.at[i], lasts[d])

    def g_copy(turn, d):
        piece = middle.at[turn, lax.rem(me.first + d, 4)]
        i = turn * 3 + d - 1
        return remote(piece, from_f.at[turn, d - 1], g_send.at[i], g_recv.at[i], firsts[d])

    def add_own(turn):
        t_copy(turn).wait_recv()
        there = part.at[BACK_STEP[0, turn]]
        there[...] += from_s[turn]
        for d in (2, 1, 3):
            p_copy(turn, d).start()

    def add_last(turn):
        for d in (1, 3, 2):
            p_copy(turn, d).wait_recv()
        middle[turn] = total_of(
            [part[BACK_STEP[0, turn], me.last]] + [from_l[turn, d] for d in range(3)]
        ).astype(BF16)
        for d in (2, 1, 3):
            g_copy(turn, d).start()

    def chunk_grads(step):
        theirs = pick(step, BACK_SIDE)
        i = base * (1 - theirs) + other * theirs + pick(pick(step, BACK_TURN), z_order)
        d_nope = []
        d_value = []
        d_all = []
        for p in range(PAIRS_DEV):
            lam_p = lam[p]
            grad = lowered[p]
            through = dot(grad, values[i, p], NT)
            probs = []
            for m in range(2):
                h = 2 * p + m
                share = jnp.exp2((tops_then[i, h] - tops[h]) * EXPONENT) * (totals[h] * LOGIT_SCALE)
                probs.append(scores[i, h] * jnp.concatenate([share, share], axis=1))
            merged = probs[0] * (1 / LOGIT_SCALE) - probs[1] * (lam_p * (1 / LOGIT_SCALE))
            d_value.append(dot(merged.astype(BF16), grad, TN).astype(BF16))
            pair = []
            for m in range(2):
                h = 2 * p + m
                delta = jnp.concatenate([deltas[h], deltas[h]], axis=1)
                inner = through if m == 0 else -lam_p * through
                d_score = (probs[m] * (inner - delta)).astype(BF16)
                d_scores[i, h] = d_score
                pair.append(d_score)
            d_nope.append(dot(jnp.concatenate(pair, axis=0), q_nope[p], TN).astype(BF16))
            d_all.extend(pair)
        d_rope = dot(jnp.concatenate(d_all, axis=0), q_rope[...], TN)
        d_latent = dot(jnp.concatenate(d_nope, axis=1), key_weight[...], NT)
        d_latent = d_latent + dot(jnp.concatenate(d_value, axis=1), value_weight[...], NT)
        part[step, :, :, :, 0:D_LAT] = d_latent.astype(BF16).reshape(4, 4, PIECE, D_LAT)
        part[step, :, :, :, D_LAT:WIDE] = d_rope.astype(BF16).reshape(4, 4, PIECE, WIDE - D_LAT)

    def backward(pair, carry):
        chunk_grads(2 * pair)
        chunk_grads(2 * pair + 1)
        for turn in (3, 2, 1, 0):

            @pl.when(pair == BACK_STEP[1, turn] // 2)
            def _(turn=turn):
                t_copy(turn).start()

        for turn in (3, 2):

            @pl.when(pair == BACK_STEP[0, turn] // 2)
            def _(turn=turn):
                add_own(turn)

        return carry

    lax.fori_loop(0, 3, backward, 0)

    def backward_last(step, carry):
        chunk_grads(step)

        @pl.when(step == 6)
        def _():
            add_own(1)

        return carry

    lax.fori_loop(6, 8, backward_last, 0)
    add_own(0)
    add_last(3)
    add_last(2)

    def to_queries(i, carry):
        for h in range(MAPS):
            q_acc[h] += dot(d_scores[i, h], k_cat[i, h])
        return carry

    lax.fori_loop(0, CHUNKS, to_queries, 0)
    for h in range(MAPS):
        query_grad[:, h * D_QK : (h + 1) * D_QK] = q_acc[h, :, 0:D_QK].astype(BF16)

    z_mine = me.zh * 2 + me.zl

    def y_copy(turn, zl):
        i = turn * 2 + zl
        device = me.at(zh=z_order[turn], zl=zl)
        return remote(small.at[turn], from_z.at[z_mine], y_send.at[i], y_recv.at[z_mine], device)

    far_y = remote(
        small.at[3], from_far, y_send.at[6], y_recv.at[8], me.at(zh=z_order[3], zl=1 - me.zl)
    )
    own_y = remote(
        from_z.at[z_mine], from_z.at[z_mine], y_send.at[0], y_recv.at[z_mine], me.at(zl=1 - me.zl)
    )

    def add_first(turn):
        for d in (1, 3, 2):
            g_copy(turn, d).wait_recv()
        small[turn] = total_of(
            [middle[turn, me.first]] + [from_f[turn, d] for d in range(3)]
        ).astype(BF16)
        if turn == 3:
            far_y.start()
        elif turn:
            for zl in (0, 1):
                y_copy(turn, zl).start()
        else:
            far_y.wait_recv()
            from_z[z_mine] = total_of([small[0], from_far[...]]).astype(BF16)
            own_y.start()

    @pl.when(me.c == 0)
    def _():
        for i in range(3):
            rows_copy(i).wait_send()

    @pl.when(me.c == 1)
    def _():
        for i in range(3):
            piece_copy(i).wait_send()
        for turn in range(4):
            for d in (1, 2, 3):
                f_copy(turn, d).wait_send()

    early = [s_copy(turn) for turn in range(4)] + [t_copy(turn) for turn in range(4)]
    early += [l_copy(turn, d) for turn in range(4) for d in (1, 2, 3)]
    early += [p_copy(turn, d) for turn in (3, 2) for d in (1, 2, 3)]
    for copy in early:
        copy.wait_send()
    add_first(3)
    add_first(2)
    add_last(1)
    add_last(0)
    add_first(1)
    add_first(0)
    told = [lax.rem(me.zh + k, 4) * 2 + zl for k in (0, 1, 3) for zl in (0, 1)]
    remote(small.at[0], from_z.at[0], y_send.at[0], y_recv.at[lax.rem(z_mine + 1 - 2 * me.zl + 8, 8)], z_line[0]).wait_recv()
    for z in told[2:]:
        remote(small.at[0], from_z.at[0], y_send.at[0], y_recv.at[z], z_line[0]).wait_recv()
    place = me.c * 4 + me.y
    result[place] = total_of([from_z[z] for z in told]).astype(BF16)

    def e_copy(d):
        piece = result.at[place]
        return remote(piece, piece, e_send.at[d - 1], e_recv.at[d - 1], y_line[d - 1])

    def r_copy(d):
        piece = result.at[me.c * 4 + lax.rem(me.y + 4 - d, 4)]
        return remote(piece, piece, r_send.at[d], r_recv.at[d], sibling)

    for d in (2, 1, 3):
        e_copy(d).start()
    r_copy(0).start()
    sent = [p_copy(turn, d) for turn in (1, 0) for d in (1, 2, 3)]
    sent += [g_copy(turn, d) for turn in range(4) for d in (1, 2, 3)]
    sent += [y_copy(turn, zl) for turn in (1, 2) for zl in (0, 1)] + [far_y, own_y]
    for copy in sent:
        copy.wait_send()
    for d in (1, 3, 2):
        e_copy(d).wait_recv()
        r_copy(d).start()
    for d in range(4):
        r_copy(d).wait_recv()
    for copy in [e_copy(d) for d in (1, 2, 3)] + [r_copy(d) for d in range(4)]:
        copy.wait_send()


def copy_out(query, result, query_out, latent_out, rope_out, latent, rope, sem):
    writes = [
        pltpu.make_async_copy(query, query_out, sem.at[0]),
        pltpu.make_async_copy(latent, latent_out, sem.at[1]),
        pltpu.make_async_copy(rope, rope_out, sem.at[2]),
    ]
    writes[0].start()
    everything = result[...].reshape(ROWS, WIDE)
    rope[...] = everything[:, D_LAT:WIDE].astype(F32).T[0:D_ROPE].astype(BF16)
    writes[2].start()
    latent[...] = everything[:, 0:D_LAT]
    writes[1].start()
    for write in writes:
        write.wait()


VMEM = pl.BlockSpec(memory_space=pltpu.VMEM)
SMEM = pl.BlockSpec(memory_space=pltpu.SMEM)
ANY = pl.BlockSpec(memory_space=pl.ANY)
HBM = pl.BlockSpec(memory_space=pltpu.HBM)
DMA = pltpu.SemaphoreType.DMA


OUTS = (
    jax.ShapeDtypeStruct((ROWS, MAPS * D_QK), BF16),
    jax.ShapeDtypeStruct((ROWS, D_LAT), BF16),
    jax.ShapeDtypeStruct((D_ROPE, ROWS), BF16),
)


def fused(*operands):
    piece = (PIECE, WIDE)
    outs = pl.pallas_call(
        fused_kernel,
        out_shape=(pltpu.VMEM(OUTS[0].shape, BF16), pltpu.VMEM((8,) + piece, BF16)),
        in_specs=[HBM] * 9,
        out_specs=(VMEM, VMEM),
        scratch_shapes=[
            pltpu.SMEM((PAIRS_DEV,), F32),
            pltpu.SMEM((32,), jnp.int32),
            pltpu.VMEM((1, 512), F32),
            pltpu.VMEM((ROWS, MAPS * D_QK), BF16),
            pltpu.VMEM((D_ROPE, ROWS), BF16),
            pltpu.VMEM((8, PIECE, 128), BF16),
            pltpu.VMEM((D_LAT, 512), BF16),
            pltpu.VMEM((D_LAT, 512), BF16),
            pltpu.VMEM((ROWS, 512), BF16),
            pltpu.VMEM((CHUNKS, 4, 4) + piece, BF16),
            pltpu.VMEM((CHUNKS, CHUNK), jnp.int32),
            pltpu.VMEM((ROWS, CHUNK), jnp.int32),
            pltpu.VMEM((MAPS, ROWS, 256), BF16),
            pltpu.VMEM((PAIRS_DEV, 2 * ROWS, 2 * D_NOPE), BF16),
            pltpu.VMEM((MAPS * ROWS, 128), BF16),
            pltpu.VMEM((CHUNKS, MAPS, CHUNK, 256), BF16),
            pltpu.VMEM((CHUNKS, PAIRS_DEV, CHUNK, PAIR_WIDTH), BF16),
            pltpu.VMEM((CHUNKS, MAPS, ROWS, CHUNK), F32),
            pltpu.VMEM((CHUNKS, MAPS, ROWS, CHUNK), BF16),
            pltpu.VMEM((MAPS, ROWS, 128), F32),
            pltpu.VMEM((CHUNKS, MAPS, ROWS, 128), F32),
            pltpu.VMEM((PAIRS_DEV, 2 * ROWS, PAIR_WIDTH), F32),
            pltpu.VMEM((MAPS, ROWS, 128), F32),
            pltpu.VMEM((PAIRS_DEV, ROWS, PAIR_WIDTH), BF16),
            pltpu.VMEM((MAPS, ROWS, 128), F32),
            pltpu.VMEM((MAPS, ROWS, 256), F32),
            pltpu.VMEM((CHUNKS, 4, 4) + piece, BF16),
            pltpu.VMEM((4, 4, 4) + piece, BF16),
            pltpu.VMEM((4, 3, 4) + piece, BF16),
            pltpu.VMEM((4, 4) + piece, BF16),
            pltpu.VMEM((4, 3) + piece, BF16),
            pltpu.VMEM((4,) + piece, BF16),
            pltpu.VMEM((8,) + piece, BF16),
            pltpu.VMEM(piece, BF16),
        ]
        + [DMA((n,)) for n in (9, 12, 12, 3, 4, 12, 12, 4, 4, 4, 4, 12, 12, 12, 12, 8, 9, 3, 3, 4, 4)],
        compiler_params=pltpu.CompilerParams(
            collective_id=0, has_side_effects=True, vmem_limit_bytes=56 << 20
        ),
        name="fused",
    )(*(pltpu.with_memory_space_constraint(operand, pltpu.HBM) for operand in operands))
    return pl.pallas_call(
        copy_out,
        out_shape=OUTS,
        in_specs=[VMEM] * 2,
        out_specs=(HBM, HBM, HBM),
        scratch_shapes=[pltpu.VMEM(out.shape, BF16) for out in OUTS[1:]] + [DMA((3,))],
        name="copy_out",
    )(*(pltpu.with_memory_space_constraint(out, pltpu.VMEM) for out in outs))


def on_device(
    queries, latent, rope_key, key_weight, value_weight, lambda_pair, norm_gain, out_grad, block_order
):
    query_grad, latent_grad, rope_grad = fused(
        lambda_pair, block_order, norm_gain.reshape(1, -1), queries, latent.reshape(8, PIECE, D_LAT), rope_key.T,
        key_weight, value_weight, out_grad,
    )
    return (query_grad, latent_grad, rope_grad.T)


def solution(mesh):
    return jax.shard_map(
        on_device,
        mesh=mesh,
        in_specs=(
            P("ctx", "head"),
            P("ctx", None),
            P("ctx", None),
            P(None, "head"),
            P(None, "head"),
            P("head"),
            P("head"),
            P("ctx", "head"),
            P(),
        ),
        out_specs=(P("ctx", "head"), P("ctx", None), P("ctx", None)),
        check_vma=False,
    )
```

```python
import functools

import jax
import jax.numpy as jnp
from jax import lax
from jax.experimental import pallas as pl
from jax.experimental.pallas import tpu as pltpu
from jax.sharding import PartitionSpec as P

MESH = pl.DeviceIdType.MESH
D_LAT = 512
D_NOPE = 128
D_ROPE = 64
D_QK = D_NOPE + D_ROPE
PAIR_WIDTH = 256
ROWS = 128
WIDE = 640
HALF = 64
CHUNKS = 8
CHUNK = 256
PIECE = 16
MAPS = 4
PAIRS_DEV = 2
LOGIT_SCALE = D_QK**-0.5
EXPONENT = LOGIT_SCALE * 1.4426950408889634
EPS = 1e-6
F32 = jnp.float32
BF16 = jnp.bfloat16


class Place:
    def __init__(self):
        ctx, head = lax.axis_index("ctx"), lax.axis_index("head")
        self.x, self.zh = lax.rem(ctx, 4), lax.div(ctx, 4)
        self.y = lax.div(head, 4)
        self.zl = lax.rem(lax.div(head, 2), 2)
        self.c = lax.rem(head, 2)
        self.o = 1 - self.c
        self.first = self.y * self.o + self.x * self.c
        self.last = self.x * self.o + self.y * self.c

    def at(self, x=None, y=None, zh=None, zl=None, c=None):
        x = self.x if x is None else x
        y = self.y if y is None else y
        zh = self.zh if zh is None else zh
        zl = self.zl if zl is None else zl
        c = self.c if c is None else c
        return (zh * 4 + x, y * 4 + zl * 2 + c)

    def first_peer(self, d):
        return self.at(x=lax.rem(self.x + d * self.c, 4), y=lax.rem(self.y + d * self.o, 4))

    def last_peer(self, d):
        return self.at(x=lax.rem(self.x + d * self.o, 4), y=lax.rem(self.y + d * self.c, 4))

    def z_peer(self, d):
        z = lax.rem(self.zh * 2 + self.zl + d, 8)
        return self.at(zh=lax.div(z, 2), zl=lax.rem(z, 2))

    def sibling(self):
        return self.at(c=self.o)


def remote(src, dst, send, recv, device):
    return pltpu.make_async_remote_copy(
        src_ref=src, dst_ref=dst, send_sem=send, recv_sem=recv, device_id=device, device_id_type=MESH
    )


def greet(devices, count):
    barrier = pltpu.get_barrier_semaphore()
    for device in devices:
        pl.semaphore_signal(barrier, inc=1, device_id=device, device_id_type=MESH)
    pl.semaphore_wait(barrier, count)


NT = (((1,), (1,)), ((), ()))
TN = (((0,), (0,)), ((), ()))


def dot(a, b, dims=None):
    if dims is None:
        return jnp.dot(a, b, preferred_element_type=F32)
    return lax.dot_general(a, b, dims, preferred_element_type=F32)


def total_of(parts):
    total = parts[0].astype(F32)
    for part in parts[1:]:
        total = total + part.astype(F32)
    return total


def pick(step, table):
    value = jnp.int32(table[0])
    for i in range(1, len(table)):
        value = jnp.where(step == i, jnp.int32(table[i]), value)
    return value


BACK_SIDE = (1, 1, 0, 1, 0, 1, 0, 0)
BACK_TURN = (3, 2, 3, 1, 2, 0, 1, 0)
BACK_STEP = {(side, turn): i for i, (side, turn) in enumerate(zip(BACK_SIDE, BACK_TURN))}


def fused_kernel(
    lam_hbm, order_hbm, gain_hbm, queries_hbm, latent_hbm, rope_hbm, key_weight_hbm, value_weight_hbm, out_grad_hbm,
    query_grad, result,
    lam, block_order, gain, queries, rope_in, rope_rows, key_weight, value_weight, out_grad,
    keys, key_pos, query_pos, q_cat, q_nope, q_rope, k_cat, values, scores, d_scores, tops, tops_then, outs, totals, lowered, deltas, q_acc,
    part, from_s, from_l, middle, from_f, small, from_z, from_far,
    in_sem, f_send, f_recv, z_send, z_recv, l_send, l_recv, s_send, s_recv,
    t_send, t_recv, p_send, p_recv, g_send, g_recv, y_send, y_recv, e_send, e_recv, r_send, r_recv,
):
    me = Place()
    ctx = me.zh * 4 + me.x
    base, other = me.c * 4, me.o * 4
    x_line = [me.at(x=lax.rem(me.x + d, 4)) for d in (1, 2, 3)]
    y_line = [me.at(y=lax.rem(me.y + d, 4)) for d in (1, 2, 3)]
    y_over = me.at(y=lax.rem(me.y + 2, 4), c=me.o)
    z_line = [me.z_peer(d) for d in range(1, 8)]
    firsts = {d: me.first_peer(d) for d in (1, 2, 3)}
    lasts = {d: me.last_peer(d) for d in (1, 2, 3)}
    sibling = me.sibling()
    near = lax.rem(me.zh + 3 - 2 * me.zl, 4)
    z_order = [me.zh, near, lax.rem(me.zh + 1 + 2 * me.zl, 4), lax.rem(me.zh + 2, 4)]
    my_rows = keys.at[base + me.zh, me.last]
    my_piece = my_rows.at[me.first]
    loads = [
        pltpu.make_async_copy(order_hbm, block_order, in_sem.at[0]),
        pltpu.make_async_copy(lam_hbm, lam, in_sem.at[1]),
        pltpu.make_async_copy(rope_hbm, rope_in, in_sem.at[2]),
        pltpu.make_async_copy(queries_hbm, queries, in_sem.at[3]),
        pltpu.make_async_copy(key_weight_hbm, key_weight, in_sem.at[4]),
        pltpu.make_async_copy(value_weight_hbm, value_weight, in_sem.at[5]),
        pltpu.make_async_copy(out_grad_hbm, out_grad, in_sem.at[6]),
        pltpu.make_async_copy(gain_hbm, gain, in_sem.at[7]),
    ]
    whole_load = pltpu.make_async_copy(
        latent_hbm.at[pl.ds(0, 4)], my_rows.at[:, :, pl.ds(0, D_LAT)], in_sem.at[8]
    )
    piece_load = pltpu.make_async_copy(
        latent_hbm.at[4 + me.y], my_piece.at[:, pl.ds(0, D_LAT)], in_sem.at[8]
    )

    @pl.when(me.c == 0)
    def _():
        whole_load.start()

    @pl.when(me.c == 1)
    def _():
        piece_load.start()

    loads[2].start()
    barrier = pltpu.get_barrier_semaphore()
    greeted = [z_line[i] for i in (2, 4, 1, 5)] + [x_line[1], y_line[1], y_over, z_line[0], z_line[6]]
    for device in greeted + [x_line[0], x_line[2], y_line[0], y_line[2], sibling]:
        pl.semaphore_signal(barrier, inc=1, device_id=device, device_id_type=MESH)
    loads[0].start()
    loads[1].start()
    for load in loads[3:]:
        load.start()

    loads[2].wait()
    rope_rows[:, :, 0:D_ROPE] = rope_in[...].astype(F32).T.astype(BF16).reshape(8, PIECE, D_ROPE)
    rope_rows[:, :, D_ROPE:128] = jnp.zeros((8, PIECE, 128 - D_ROPE), BF16)

    @pl.when(me.c == 0)
    def _():
        whole_load.wait()
        my_rows[:, :, D_LAT:WIDE] = rope_rows[0:4]

    @pl.when(me.c == 1)
    def _():
        piece_load.wait()
        my_piece[:, D_LAT:WIDE] = rope_rows[4 + me.y]

    pl.semaphore_wait(barrier, 14)

    z_to = [
        me.at(zh=near, zl=1 - me.zl),
        me.at(zh=near, zl=me.zl),
        me.at(zh=z_order[3], zl=1 - me.zl),
    ]

    def f_copy(turn, d):
        piece = keys.at[base + z_order[turn], me.last, me.first]
        i = turn * 3 + d - 1
        return remote(piece, piece, f_send.at[i], f_recv.at[i], firsts[d])

    def rows_copy(i):
        return remote(my_rows, my_rows, z_send.at[i], z_recv.at[me.zh], z_to[i])

    def piece_copy(i):
        return remote(my_piece, my_piece, z_send.at[i], z_recv.at[me.zh], z_to[i])

    def rows_wait(turn):
        rows = keys.at[base + z_order[turn], me.last]
        remote(rows, rows, z_send.at[0], z_recv.at[z_order[turn]], z_to[0]).wait_recv()

    def piece_wait(turn):
        piece = keys.at[base + z_order[turn], me.last, me.first]
        remote(piece, piece, z_send.at[0], z_recv.at[z_order[turn]], z_to[0]).wait_recv()

    def z_at(turn):
        return z_order[turn] if isinstance(turn, int) else pick(turn, z_order)

    def l_copy(turn, d):
        rows = keys.at[base + z_at(turn), me.last]
        i = turn * 3 + d - 1
        return remote(rows, rows, l_send.at[i], l_recv.at[i], lasts[d])

    def s_copy(turn):
        rows = keys.at[base + z_at(turn)]
        return remote(rows, rows, s_send.at[turn], s_recv.at[turn], sibling)

    def l_sends(turn):
        for d in (2, 1, 3):
            l_copy(turn, d).start()

    def f_sends(turn):
        for d in (2, 1, 3):
            f_copy(turn, d).start()

    def f_done(turn):
        for d in (1, 3, 2):
            f_copy(turn, d).wait_recv()
        l_sends(turn)

    @pl.when(me.c == 0)
    def _():
        for i in range(2):
            rows_copy(i).start()
        l_sends(0)

    @pl.when(me.c == 1)
    def _():
        f_sends(0)
        for i in (2, 1, 0):
            piece_copy(i).start()

    loads[0].wait()
    chunk = lax.broadcasted_iota(jnp.int32, (CHUNKS, CHUNK), 0)
    lane = lax.broadcasted_iota(jnp.int32, (CHUNKS, CHUNK), 1)
    side, k_z = chunk // 4, chunk % 4
    k_last, k_first, k_r = lane // 64, (lane // 16) % 4, lane % 16
    slot = 2 * (k_z * 4 + jnp.where(side == 0, k_last, k_first)) + side
    held = jnp.zeros((CHUNKS, CHUNK), jnp.int32)
    for i in range(32):
        held = jnp.where(slot == i, block_order[i], held)
    key_pos[...] = held * HALF + jnp.where(side == 0, k_first, k_last) * PIECE + k_r
    token = lax.broadcasted_iota(jnp.int32, (ROWS, CHUNK), 0)
    query_pos[...] = (
        jnp.where(token < HALF, block_order[2 * ctx], block_order[2 * ctx + 1]) * HALF + token % HALF
    )
    tops[...] = jnp.full(tops.shape, -1e30, F32)
    outs[...] = jnp.zeros(outs.shape, F32)
    totals[...] = jnp.zeros(totals.shape, F32)
    q_acc[...] = jnp.zeros(q_acc.shape, F32)

    for load in loads[1:2] + loads[3:4]:
        load.wait()
    for h in range(MAPS):
        q_cat[h] = jnp.concatenate(
            [queries[:, h * D_QK : (h + 1) * D_QK], jnp.zeros((ROWS, 256 - D_QK), BF16)], axis=1
        )
        rows, columns = pl.ds(h % 2 * ROWS, ROWS), h % 2 * D_NOPE
        q_nope[h // 2, rows, columns : columns + D_NOPE] = q_cat[h, :, 0:D_NOPE]
        q_nope[h // 2, rows, D_NOPE - columns : 2 * D_NOPE - columns] = jnp.zeros((ROWS, D_NOPE), BF16)
        q_rope[h * ROWS : (h + 1) * ROWS, :] = q_cat[h, :, D_NOPE:256]
    for load in loads[4:]:
        load.wait()

    @pl.when(me.c == 0)
    def _():
        for i in range(2):
            rows_copy(i).wait_send()
        rows_copy(2).start()
        for turn in (1, 2):
            rows_wait(turn)
            l_sends(turn)

    @pl.when(me.c == 1)
    def _():
        f_done(0)
        for turn in (1, 2, 3):
            piece_wait(turn)
            f_sends(turn)
        for turn in (1, 2):
            f_done(turn)

    def absorb(chunks):
        spans = [slice(n * CHUNK, (n + 1) * CHUNK) for n in range(len(chunks))]
        tokens = [keys[i].reshape(CHUNK, WIDE) for i in chunks]
        latent = jnp.concatenate([part[:, 0:D_LAT] for part in tokens], axis=0)
        nope = dot(latent, key_weight[...]).astype(BF16)
        value = dot(latent, value_weight[...]).astype(BF16)
        seen = [key_pos[pl.ds(i, 1), :] <= query_pos[...] for i in chunks]
        for i, span, part in zip(chunks, spans, tokens):
            for p in range(PAIRS_DEV):
                values[i, p] = value[span, p * PAIR_WIDTH : (p + 1) * PAIR_WIDTH]
            for h in range(MAPS):
                k_cat[i, h, :, 0:D_NOPE] = nope[span, h * D_NOPE : (h + 1) * D_NOPE]
                k_cat[i, h, :, D_NOPE:256] = part[:, D_LAT:WIDE]
        for p in range(PAIRS_DEV):
            both, shrinks = [], []
            for m in range(2):
                h = 2 * p + m
                tiles = [
                    jnp.where(mask, dot(q_cat[h], k_cat[i, h], NT), -jnp.inf) for i, mask in zip(chunks, seen)
                ]
                highest = functools.reduce(jnp.maximum, tiles)
                top = jnp.maximum(tops[h], jnp.max(highest, axis=1, keepdims=True))
                shrink = jnp.exp2((tops[h] - top) * EXPONENT)
                wide_top = jnp.concatenate([top, top], axis=1)
                weights = [jnp.exp2((tile - wide_top) * EXPONENT) for tile in tiles]
                tops[h] = top
                total = functools.reduce(jnp.add, weights)
                totals[h] = totals[h] * shrink + (total[:, 0:128] + total[:, 128:256])
                for i, weight in zip(chunks, weights):
                    tops_then[i, h] = top
                    scores[i, h] = weight
                both.append(jnp.concatenate([weight.astype(BF16) for weight in weights], axis=1))
                shrinks.append(jnp.concatenate([shrink, shrink], axis=1))
            outs[p] = outs[p] * jnp.concatenate(shrinks, axis=0) + dot(
                jnp.concatenate(both, axis=0), value[:, p * PAIR_WIDTH : (p + 1) * PAIR_WIDTH]
            )

    def own_ready(turn):
        for d in (1, 3, 2):
            l_copy(turn, d).wait_recv()
        s_copy(turn).start()

    @pl.when(me.c == 0)
    def _():
        rows_wait(3)

    @pl.when(me.c == 1)
    def _():
        for d in (1, 3, 2):
            f_copy(3, d).wait_recv()

    l_sends(3)

    own_ready(0)
    absorb([base + z_order[0]])

    def expand(turn, carry):
        own_ready(turn)
        s_copy(turn - 1).wait_recv()
        absorb([other + z_at(turn - 1), base + z_at(turn)])
        return carry

    lax.fori_loop(1, 4, expand, 0)
    s_copy(3).wait_recv()
    absorb([other + z_order[3]])

    for p in range(PAIRS_DEV):
        lam_p = lam[p]
        maps = []
        for m in range(2):
            h = 2 * p + m
            inverse = 1.0 / jnp.sum(totals[h], axis=1, keepdims=True)
            totals[h] = jnp.broadcast_to(inverse, (ROWS, 128))
            maps.append(outs[p, m * ROWS : (m + 1) * ROWS] * inverse)
        mixed = maps[0] - lam_p * maps[1]
        inv_root = lax.rsqrt(jnp.mean(mixed * mixed, axis=1, keepdims=True) + EPS)
        normed = mixed * inv_root
        scaled = out_grad[:, p * PAIR_WIDTH : (p + 1) * PAIR_WIDTH].astype(F32) * gain[
            :, p * PAIR_WIDTH : (p + 1) * PAIR_WIDTH
        ]
        d_mixed = (scaled - normed * jnp.mean(scaled * normed, axis=1, keepdims=True)) * inv_root
        lowered[p] = d_mixed.astype(BF16)
        deltas[2 * p] = jnp.broadcast_to(jnp.sum(d_mixed * maps[0], axis=1, keepdims=True), (ROWS, 128))
        deltas[2 * p + 1] = jnp.broadcast_to(
            -lam_p * jnp.sum(d_mixed * maps[1], axis=1, keepdims=True), (ROWS, 128)
        )

    def t_copy(turn):
        return remote(part.at[BACK_STEP[1, turn]], from_s.at[turn], t_send.at[turn], t_recv.at[turn], sibling)

    def p_copy(turn, d):
        rows = part.at[BACK_STEP[0, turn], lax.rem(me.last + d, 4)]
        i = turn * 3 + d - 1
        return remote(rows, from_l.at[turn, d - 1], p_send.at[i], p_recv.at[i], lasts[d])

    def g_copy(turn, d):
        piece = middle.at[turn, lax.rem(me.first + d, 4)]
        i = turn * 3 + d - 1
        return remote(piece, from_f.at[turn, d - 1], g_send.at[i], g_recv.at[i], firsts[d])

    def add_own(turn):
        t_copy(turn).wait_recv()
        there = part.at[BACK_STEP[0, turn]]
        there[...] += from_s[turn]
        for d in (2, 1, 3):
            p_copy(turn, d).start()

    def add_last(turn):
        for d in (1, 3, 2):
            p_copy(turn, d).wait_recv()
        middle[turn] = total_of(
            [part[BACK_STEP[0, turn], me.last]] + [from_l[turn, d] for d in range(3)]
        ).astype(BF16)
        for d in (2, 1, 3):
            g_copy(turn, d).start()

    def chunk_grads(step):
        theirs = pick(step, BACK_SIDE)
        i = base * (1 - theirs) + other * theirs + pick(pick(step, BACK_TURN), z_order)
        d_nope = []
        d_value = []
        d_all = []
        for p in range(PAIRS_DEV):
            lam_p = lam[p]
            grad = lowered[p]
            through = dot(grad, values[i, p], NT)
            probs = []
            for m in range(2):
                h = 2 * p + m
                share = jnp.exp2((tops_then[i, h] - tops[h]) * EXPONENT) * (totals[h] * LOGIT_SCALE)
                probs.append(scores[i, h] * jnp.concatenate([share, share], axis=1))
            merged = probs[0] * (1 / LOGIT_SCALE) - probs[1] * (lam_p * (1 / LOGIT_SCALE))
            d_value.append(dot(merged.astype(BF16), grad, TN).astype(BF16))
            pair = []
            for m in range(2):
                h = 2 * p + m
                delta = jnp.concatenate([deltas[h], deltas[h]], axis=1)
                inner = through if m == 0 else -lam_p * through
                d_score = (probs[m] * (inner - delta)).astype(BF16)
                d_scores[i, h] = d_score
                pair.append(d_score)
            d_nope.append(dot(jnp.concatenate(pair, axis=0), q_nope[p], TN).astype(BF16))
            d_all.extend(pair)
        d_rope = dot(jnp.concatenate(d_all, axis=0), q_rope[...], TN)
        d_latent = dot(jnp.concatenate(d_nope, axis=1), key_weight[...], NT)
        d_latent = d_latent + dot(jnp.concatenate(d_value, axis=1), value_weight[...], NT)
        part[step, :, :, :, 0:D_LAT] = d_latent.astype(BF16).reshape(4, 4, PIECE, D_LAT)
        part[step, :, :, :, D_LAT:WIDE] = d_rope.astype(BF16).reshape(4, 4, PIECE, WIDE - D_LAT)

    def backward(pair, carry):
        chunk_grads(2 * pair)
        chunk_grads(2 * pair + 1)
        for turn in (3, 2, 1, 0):

            @pl.when(pair == BACK_STEP[1, turn] // 2)
            def _(turn=turn):
                t_copy(turn).start()

        for turn in (3, 2):

            @pl.when(pair == BACK_STEP[0, turn] // 2)
            def _(turn=turn):
                add_own(turn)

        return carry

    lax.fori_loop(0, 3, backward, 0)

    def backward_last(step, carry):
        chunk_grads(step)

        @pl.when(step == 6)
        def _():
            add_own(1)

        return carry

    lax.fori_loop(6, 8, backward_last, 0)
    add_own(0)

    def to_queries(i, carry):
        for h in range(MAPS):
            q_acc[h] += dot(d_scores[i, h], k_cat[i, h])
        return carry

    lax.fori_loop(0, CHUNKS, to_queries, 0)
    for h in range(MAPS):
        query_grad[:, h * D_QK : (h + 1) * D_QK] = q_acc[h, :, 0:D_QK].astype(BF16)

    z_mine = me.zh * 2 + me.zl

    def y_copy(turn, zl):
        i = turn * 2 + zl
        device = me.at(zh=z_order[turn], zl=zl)
        return remote(small.at[turn], from_z.at[z_mine], y_send.at[i], y_recv.at[z_mine], device)

    far_y = remote(
        small.at[3], from_far, y_send.at[6], y_recv.at[8], me.at(zh=z_order[3], zl=1 - me.zl)
    )
    own_y = remote(
        from_z.at[z_mine], from_z.at[z_mine], y_send.at[0], y_recv.at[z_mine], me.at(zl=1 - me.zl)
    )

    def add_first(turn):
        for d in (1, 3, 2):
            g_copy(turn, d).wait_recv()
        small[turn] = total_of(
            [middle[turn, me.first]] + [from_f[turn, d] for d in range(3)]
        ).astype(BF16)
        if turn == 3:
            far_y.start()
        elif turn:
            for zl in (0, 1):
                y_copy(turn, zl).start()
        else:
            far_y.wait_recv()
            from_z[z_mine] = total_of([small[0], from_far[...]]).astype(BF16)
            own_y.start()

    add_last(3)
    add_last(2)

    @pl.when(me.c == 0)
    def _():
        rows_copy(2).wait_send()

    @pl.when(me.c == 1)
    def _():
        for i in range(3):
            piece_copy(i).wait_send()
        for turn in range(4):
            for d in (1, 2, 3):
                f_copy(turn, d).wait_send()

    early = [s_copy(turn) for turn in range(4)] + [t_copy(turn) for turn in range(4)]
    early += [l_copy(turn, d) for turn in range(4) for d in (1, 2, 3)]
    early += [p_copy(turn, d) for turn in (3, 2) for d in (1, 2, 3)]
    for copy in early:
        copy.wait_send()
    add_last(1)
    add_first(3)
    add_last(0)
    add_first(2)
    add_first(1)
    add_first(0)
    told = [lax.rem(me.zh + k, 4) * 2 + zl for k in (0, 1, 3) for zl in (0, 1)]
    remote(small.at[0], from_z.at[0], y_send.at[0], y_recv.at[lax.rem(z_mine + 1 - 2 * me.zl + 8, 8)], z_line[0]).wait_recv()
    for z in told[2:]:
        remote(small.at[0], from_z.at[0], y_send.at[0], y_recv.at[z], z_line[0]).wait_recv()
    place = me.c * 4 + me.y
    result[place] = total_of([from_z[z] for z in told]).astype(BF16)

    def e_copy(d):
        piece = result.at[place]
        return remote(piece, piece, e_send.at[d - 1], e_recv.at[d - 1], (y_line + [y_over])[d - 1])

    def r_copy(d):
        piece = result.at[me.c * 4 + lax.rem(me.y + 4 - d, 4)]
        return remote(piece, piece, r_send.at[d], r_recv.at[d], sibling)

    for d in (4, 2, 1, 3):
        e_copy(d).start()
    r_copy(0).start()
    sent = [p_copy(turn, d) for turn in (1, 0) for d in (1, 2, 3)]
    sent += [g_copy(turn, d) for turn in range(4) for d in (1, 2, 3)]
    sent += [y_copy(turn, zl) for turn in (1, 2) for zl in (0, 1)] + [far_y, own_y]
    for copy in sent:
        copy.wait_send()
    for d in (1, 3):
        e_copy(d).wait_recv()
        r_copy(d).start()
    for d in (2, 4):
        e_copy(d).wait_recv()
    for d in (0, 1, 3):
        r_copy(d).wait_recv()
    for copy in [e_copy(d) for d in (1, 2, 3, 4)] + [r_copy(d) for d in (0, 1, 3)]:
        copy.wait_send()


def copy_out(query, result, query_out, latent_out, rope_out, latent, rope, sem):
    writes = [
        pltpu.make_async_copy(query, query_out, sem.at[0]),
        pltpu.make_async_copy(latent, latent_out, sem.at[1]),
        pltpu.make_async_copy(rope, rope_out, sem.at[2]),
    ]
    writes[0].start()
    everything = result[...].reshape(ROWS, WIDE)
    rope[...] = everything[:, D_LAT:WIDE].astype(F32).T[0:D_ROPE].astype(BF16)
    writes[2].start()
    latent[...] = everything[:, 0:D_LAT]
    writes[1].start()
    for write in writes:
        write.wait()


VMEM = pl.BlockSpec(memory_space=pltpu.VMEM)
SMEM = pl.BlockSpec(memory_space=pltpu.SMEM)
ANY = pl.BlockSpec(memory_space=pl.ANY)
HBM = pl.BlockSpec(memory_space=pltpu.HBM)
DMA = pltpu.SemaphoreType.DMA


OUTS = (
    jax.ShapeDtypeStruct((ROWS, MAPS * D_QK), BF16),
    jax.ShapeDtypeStruct((ROWS, D_LAT), BF16),
    jax.ShapeDtypeStruct((D_ROPE, ROWS), BF16),
)


def fused(*operands):
    piece = (PIECE, WIDE)
    outs = pl.pallas_call(
        fused_kernel,
        out_shape=(pltpu.VMEM(OUTS[0].shape, BF16), pltpu.VMEM((8,) + piece, BF16)),
        in_specs=[HBM] * 9,
        out_specs=(VMEM, VMEM),
        scratch_shapes=[
            pltpu.SMEM((PAIRS_DEV,), F32),
            pltpu.SMEM((32,), jnp.int32),
            pltpu.VMEM((1, 512), F32),
            pltpu.VMEM((ROWS, MAPS * D_QK), BF16),
            pltpu.VMEM((D_ROPE, ROWS), BF16),
            pltpu.VMEM((8, PIECE, 128), BF16),
            pltpu.VMEM((D_LAT, 512), BF16),
            pltpu.VMEM((D_LAT, 512), BF16),
            pltpu.VMEM((ROWS, 512), BF16),
            pltpu.VMEM((CHUNKS, 4, 4) + piece, BF16),
            pltpu.VMEM((CHUNKS, CHUNK), jnp.int32),
            pltpu.VMEM((ROWS, CHUNK), jnp.int32),
            pltpu.VMEM((MAPS, ROWS, 256), BF16),
            pltpu.VMEM((PAIRS_DEV, 2 * ROWS, 2 * D_NOPE), BF16),
            pltpu.VMEM((MAPS * ROWS, 128), BF16),
            pltpu.VMEM((CHUNKS, MAPS, CHUNK, 256), BF16),
            pltpu.VMEM((CHUNKS, PAIRS_DEV, CHUNK, PAIR_WIDTH), BF16),
            pltpu.VMEM((CHUNKS, MAPS, ROWS, CHUNK), F32),
            pltpu.VMEM((CHUNKS, MAPS, ROWS, CHUNK), BF16),
            pltpu.VMEM((MAPS, ROWS, 128), F32),
            pltpu.VMEM((CHUNKS, MAPS, ROWS, 128), F32),
            pltpu.VMEM((PAIRS_DEV, 2 * ROWS, PAIR_WIDTH), F32),
            pltpu.VMEM((MAPS, ROWS, 128), F32),
            pltpu.VMEM((PAIRS_DEV, ROWS, PAIR_WIDTH), BF16),
            pltpu.VMEM((MAPS, ROWS, 128), F32),
            pltpu.VMEM((MAPS, ROWS, 256), F32),
            pltpu.VMEM((CHUNKS, 4, 4) + piece, BF16),
            pltpu.VMEM((4, 4, 4) + piece, BF16),
            pltpu.VMEM((4, 3, 4) + piece, BF16),
            pltpu.VMEM((4, 4) + piece, BF16),
            pltpu.VMEM((4, 3) + piece, BF16),
            pltpu.VMEM((4,) + piece, BF16),
            pltpu.VMEM((8,) + piece, BF16),
            pltpu.VMEM(piece, BF16),
        ]
        + [DMA((n,)) for n in (9, 12, 12, 3, 4, 12, 12, 4, 4, 4, 4, 12, 12, 12, 12, 8, 9, 4, 4, 4, 4)],
        compiler_params=pltpu.CompilerParams(
            collective_id=0, has_side_effects=True, vmem_limit_bytes=56 << 20
        ),
        name="fused",
    )(*(pltpu.with_memory_space_constraint(operand, pltpu.HBM) for operand in operands))
    return pl.pallas_call(
        copy_out,
        out_shape=OUTS,
        in_specs=[VMEM] * 2,
        out_specs=(HBM, HBM, HBM),
        scratch_shapes=[pltpu.VMEM(out.shape, BF16) for out in OUTS[1:]] + [DMA((3,))],
        name="copy_out",
    )(*(pltpu.with_memory_space_constraint(out, pltpu.VMEM) for out in outs))


def on_device(
    queries, latent, rope_key, key_weight, value_weight, lambda_pair, norm_gain, out_grad, block_order
):
    query_grad, latent_grad, rope_grad = fused(
        lambda_pair, block_order, norm_gain.reshape(1, -1), queries, latent.reshape(8, PIECE, D_LAT), rope_key.T,
        key_weight, value_weight, out_grad,
    )
    return (query_grad, latent_grad, rope_grad.T)


def solution(mesh):
    return jax.shard_map(
        on_device,
        mesh=mesh,
        in_specs=(
            P("ctx", "head"),
            P("ctx", None),
            P("ctx", None),
            P(None, "head"),
            P(None, "head"),
            P("head"),
            P("head"),
            P("ctx", "head"),
            P(),
        ),
        out_specs=(P("ctx", "head"), P("ctx", None), P("ctx", None)),
        check_vma=False,
    )
```

```python
import functools

import jax
import jax.numpy as jnp
from jax import lax
from jax.experimental import pallas as pl
from jax.experimental.pallas import tpu as pltpu
from jax.sharding import PartitionSpec as P

MESH = pl.DeviceIdType.MESH
D_LAT = 512
D_NOPE = 128
D_ROPE = 64
D_QK = D_NOPE + D_ROPE
PAIR_WIDTH = 256
ROWS = 128
WIDE = 640
HALF = 64
CHUNKS = 8
CHUNK = 256
PIECE = 16
MAPS = 4
PAIRS_DEV = 2
LOGIT_SCALE = D_QK**-0.5
EXPONENT = LOGIT_SCALE * 1.4426950408889634
EPS = 1e-6
F32 = jnp.float32
BF16 = jnp.bfloat16


class Place:
    def __init__(self):
        ctx, head = lax.axis_index("ctx"), lax.axis_index("head")
        self.x, self.zh = lax.rem(ctx, 4), lax.div(ctx, 4)
        self.y = lax.div(head, 4)
        self.zl = lax.rem(lax.div(head, 2), 2)
        self.c = lax.rem(head, 2)
        self.o = 1 - self.c
        self.first = self.y * self.o + self.x * self.c
        self.last = self.x * self.o + self.y * self.c

    def at(self, x=None, y=None, zh=None, zl=None, c=None):
        x = self.x if x is None else x
        y = self.y if y is None else y
        zh = self.zh if zh is None else zh
        zl = self.zl if zl is None else zl
        c = self.c if c is None else c
        return (zh * 4 + x, y * 4 + zl * 2 + c)

    def first_peer(self, d):
        return self.at(x=lax.rem(self.x + d * self.c, 4), y=lax.rem(self.y + d * self.o, 4))

    def last_peer(self, d):
        return self.at(x=lax.rem(self.x + d * self.o, 4), y=lax.rem(self.y + d * self.c, 4))

    def z_peer(self, d):
        z = lax.rem(self.zh * 2 + self.zl + d, 8)
        return self.at(zh=lax.div(z, 2), zl=lax.rem(z, 2))

    def sibling(self):
        return self.at(c=self.o)


def remote(src, dst, send, recv, device):
    return pltpu.make_async_remote_copy(
        src_ref=src, dst_ref=dst, send_sem=send, recv_sem=recv, device_id=device, device_id_type=MESH
    )


def greet(devices, count):
    barrier = pltpu.get_barrier_semaphore()
    for device in devices:
        pl.semaphore_signal(barrier, inc=1, device_id=device, device_id_type=MESH)
    pl.semaphore_wait(barrier, count)


NT = (((1,), (1,)), ((), ()))
TN = (((0,), (0,)), ((), ()))


def dot(a, b, dims=None):
    if dims is None:
        return jnp.dot(a, b, preferred_element_type=F32)
    return lax.dot_general(a, b, dims, preferred_element_type=F32)


def total_of(parts):
    total = parts[0].astype(F32)
    for part in parts[1:]:
        total = total + part.astype(F32)
    return total


def pick(step, table):
    value = jnp.int32(table[0])
    for i in range(1, len(table)):
        value = jnp.where(step == i, jnp.int32(table[i]), value)
    return value


BACK_SIDE = (1, 1, 0, 1, 0, 1, 0, 0)
BACK_TURN = (3, 2, 3, 1, 2, 0, 1, 0)
BACK_STEP = {(side, turn): i for i, (side, turn) in enumerate(zip(BACK_SIDE, BACK_TURN))}


def fused_kernel(
    lam_hbm, order_hbm, gain_hbm, queries_hbm, latent_hbm, rope_hbm, key_weight_hbm, value_weight_hbm, out_grad_hbm,
    query_grad, result,
    lam, block_order, gain, queries, rope_in, rope_rows, key_weight, value_weight, out_grad,
    keys, key_pos, query_pos, q_cat, q_nope, q_rope, k_cat, values, scores, d_scores, tops, tops_then, outs, totals, lowered, deltas, q_acc,
    part, from_s, from_l, middle, from_f, small, from_z, from_far,
    in_sem, f_send, f_recv, z_send, z_recv, l_send, l_recv, s_send, s_recv,
    t_send, t_recv, p_send, p_recv, g_send, g_recv, y_send, y_recv, e_send, e_recv, r_send, r_recv,
):
    me = Place()
    ctx = me.zh * 4 + me.x
    base, other = me.c * 4, me.o * 4
    x_line = [me.at(x=lax.rem(me.x + d, 4)) for d in (1, 2, 3)]
    y_line = [me.at(y=lax.rem(me.y + d, 4)) for d in (1, 2, 3)]
    y_over = me.at(y=lax.rem(me.y + 2, 4), c=me.o)
    z_line = [me.z_peer(d) for d in range(1, 8)]
    firsts = {d: me.first_peer(d) for d in (1, 2, 3)}
    lasts = {d: me.last_peer(d) for d in (1, 2, 3)}
    sibling = me.sibling()
    near = lax.rem(me.zh + 3 - 2 * me.zl, 4)
    z_order = [me.zh, near, lax.rem(me.zh + 1 + 2 * me.zl, 4), lax.rem(me.zh + 2, 4)]
    my_rows = keys.at[base + me.zh, me.last]
    my_piece = my_rows.at[me.first]
    loads = [
        pltpu.make_async_copy(order_hbm, block_order, in_sem.at[0]),
        pltpu.make_async_copy(lam_hbm, lam, in_sem.at[1]),
        pltpu.make_async_copy(rope_hbm, rope_in, in_sem.at[2]),
        pltpu.make_async_copy(queries_hbm, queries, in_sem.at[3]),
        pltpu.make_async_copy(key_weight_hbm, key_weight, in_sem.at[4]),
        pltpu.make_async_copy(value_weight_hbm, value_weight, in_sem.at[5]),
        pltpu.make_async_copy(out_grad_hbm, out_grad, in_sem.at[6]),
        pltpu.make_async_copy(gain_hbm, gain, in_sem.at[7]),
    ]
    whole_load = pltpu.make_async_copy(
        latent_hbm.at[pl.ds(0, 4)], my_rows.at[:, :, pl.ds(0, D_LAT)], in_sem.at[8]
    )
    piece_load = pltpu.make_async_copy(
        latent_hbm.at[4 + me.y], my_piece.at[:, pl.ds(0, D_LAT)], in_sem.at[8]
    )

    @pl.when(me.c == 0)
    def _():
        whole_load.start()

    @pl.when(me.c == 1)
    def _():
        piece_load.start()

    loads[2].start()
    barrier = pltpu.get_barrier_semaphore()
    greeted = [z_line[i] for i in (2, 4, 1, 5)] + [x_line[1], y_line[1], y_over, z_line[0], z_line[6]]
    for device in greeted + [x_line[0], x_line[2], y_line[0], y_line[2], sibling]:
        pl.semaphore_signal(barrier, inc=1, device_id=device, device_id_type=MESH)
    loads[0].start()
    loads[1].start()
    for load in loads[3:]:
        load.start()

    loads[2].wait()
    rope_rows[:, :, 0:D_ROPE] = rope_in[...].astype(F32).T.astype(BF16).reshape(8, PIECE, D_ROPE)
    rope_rows[:, :, D_ROPE:128] = jnp.zeros((8, PIECE, 128 - D_ROPE), BF16)

    @pl.when(me.c == 0)
    def _():
        whole_load.wait()
        my_rows[:, :, D_LAT:WIDE] = rope_rows[0:4]

    @pl.when(me.c == 1)
    def _():
        piece_load.wait()
        my_piece[:, D_LAT:WIDE] = rope_rows[4 + me.y]

    pl.semaphore_wait(barrier, 14)

    z_to = [
        me.at(zh=near, zl=1 - me.zl),
        me.at(zh=near, zl=me.zl),
        me.at(zh=z_order[3], zl=1 - me.zl),
    ]

    def f_copy(turn, d):
        piece = keys.at[base + z_order[turn], me.last, me.first]
        i = turn * 3 + d - 1
        return remote(piece, piece, f_send.at[i], f_recv.at[i], firsts[d])

    def rows_copy(i):
        return remote(my_rows, my_rows, z_send.at[i], z_recv.at[me.zh], z_to[i])

    def piece_copy(i):
        return remote(my_piece, my_piece, z_send.at[i], z_recv.at[me.zh], z_to[i])

    def rows_wait(turn):
        rows = keys.at[base + z_order[turn], me.last]
        remote(rows, rows, z_send.at[0], z_recv.at[z_order[turn]], z_to[0]).wait_recv()

    def piece_wait(turn):
        piece = keys.at[base + z_order[turn], me.last, me.first]
        remote(piece, piece, z_send.at[0], z_recv.at[z_order[turn]], z_to[0]).wait_recv()

    def z_at(turn):
        return z_order[turn] if isinstance(turn, int) else pick(turn, z_order)

    def l_copy(turn, d):
        rows = keys.at[base + z_at(turn), me.last]
        i = turn * 3 + d - 1
        return remote(rows, rows, l_send.at[i], l_recv.at[i], lasts[d])

    def s_copy(turn):
        rows = keys.at[base + z_at(turn)]
        return remote(rows, rows, s_send.at[turn], s_recv.at[turn], sibling)

    def l_sends(turn):
        for d in (2, 1, 3):
            l_copy(turn, d).start()

    def f_sends(turn):
        for d in (2, 1, 3):
            f_copy(turn, d).start()

    def f_done(turn):
        for d in (1, 3, 2):
            f_copy(turn, d).wait_recv()
        l_sends(turn)

    @pl.when(me.c == 0)
    def _():
        for i in range(2):
            rows_copy(i).start()
        l_sends(0)

    @pl.when(me.c == 1)
    def _():
        f_sends(0)
        for i in (2, 1, 0):
            piece_copy(i).start()

    loads[0].wait()
    chunk = lax.broadcasted_iota(jnp.int32, (CHUNKS, CHUNK), 0)
    lane = lax.broadcasted_iota(jnp.int32, (CHUNKS, CHUNK), 1)
    side, k_z = chunk // 4, chunk % 4
    k_last, k_first, k_r = lane // 64, (lane // 16) % 4, lane % 16
    slot = 2 * (k_z * 4 + jnp.where(side == 0, k_last, k_first)) + side
    held = jnp.zeros((CHUNKS, CHUNK), jnp.int32)
    for i in range(32):
        held = jnp.where(slot == i, block_order[i], held)
    key_pos[...] = held * HALF + jnp.where(side == 0, k_first, k_last) * PIECE + k_r
    token = lax.broadcasted_iota(jnp.int32, (ROWS, CHUNK), 0)
    query_pos[...] = (
        jnp.where(token < HALF, block_order[2 * ctx], block_order[2 * ctx + 1]) * HALF + token % HALF
    )
    tops[...] = jnp.full(tops.shape, -1e30, F32)
    outs[...] = jnp.zeros(outs.shape, F32)
    totals[...] = jnp.zeros(totals.shape, F32)
    q_acc[...] = jnp.zeros(q_acc.shape, F32)

    for load in loads[1:2] + loads[3:4]:
        load.wait()
    for h in range(MAPS):
        q_cat[h] = jnp.concatenate(
            [queries[:, h * D_QK : (h + 1) * D_QK], jnp.zeros((ROWS, 256 - D_QK), BF16)], axis=1
        )
        rows, columns = pl.ds(h % 2 * ROWS, ROWS), h % 2 * D_NOPE
        q_nope[h // 2, rows, columns : columns + D_NOPE] = q_cat[h, :, 0:D_NOPE]
        q_nope[h // 2, rows, D_NOPE - columns : 2 * D_NOPE - columns] = jnp.zeros((ROWS, D_NOPE), BF16)
        q_rope[h * ROWS : (h + 1) * ROWS, :] = q_cat[h, :, D_NOPE:256]
    for load in loads[4:]:
        load.wait()

    @pl.when(me.c == 0)
    def _():
        for i in range(2):
            rows_copy(i).wait_send()
        rows_copy(2).start()
        for turn in (1, 2):
            rows_wait(turn)
            l_sends(turn)

    @pl.when(me.c == 1)
    def _():
        f_done(0)
        for turn in (1, 2, 3):
            piece_wait(turn)
            f_sends(turn)
        for turn in (1, 2):
            f_done(turn)

    def absorb(chunks):
        spans = [slice(n * CHUNK, (n + 1) * CHUNK) for n in range(len(chunks))]
        tokens = [keys[i].reshape(CHUNK, WIDE) for i in chunks]
        latent = jnp.concatenate([part[:, 0:D_LAT] for part in tokens], axis=0)
        nope = dot(latent, key_weight[...]).astype(BF16)
        value = dot(latent, value_weight[...]).astype(BF16)
        seen = [key_pos[pl.ds(i, 1), :] <= query_pos[...] for i in chunks]
        for i, span, part in zip(chunks, spans, tokens):
            for p in range(PAIRS_DEV):
                values[i, p] = value[span, p * PAIR_WIDTH : (p + 1) * PAIR_WIDTH]
            for h in range(MAPS):
                k_cat[i, h, :, 0:D_NOPE] = nope[span, h * D_NOPE : (h + 1) * D_NOPE]
                k_cat[i, h, :, D_NOPE:256] = part[:, D_LAT:WIDE]
        for p in range(PAIRS_DEV):
            both, shrinks = [], []
            for m in range(2):
                h = 2 * p + m
                tiles = [
                    jnp.where(mask, dot(q_cat[h], k_cat[i, h], NT), -jnp.inf) for i, mask in zip(chunks, seen)
                ]
                highest = functools.reduce(jnp.maximum, tiles)
                top = jnp.maximum(tops[h], jnp.max(highest, axis=1, keepdims=True))
                shrink = jnp.exp2((tops[h] - top) * EXPONENT)
                wide_top = jnp.concatenate([top, top], axis=1)
                weights = [jnp.exp2((tile - wide_top) * EXPONENT) for tile in tiles]
                tops[h] = top
                total = functools.reduce(jnp.add, weights)
                totals[h] = totals[h] * shrink + (total[:, 0:128] + total[:, 128:256])
                for i, weight in zip(chunks, weights):
                    tops_then[i, h] = top
                    scores[i, h] = weight
                both.append(jnp.concatenate([weight.astype(BF16) for weight in weights], axis=1))
                shrinks.append(jnp.concatenate([shrink, shrink], axis=1))
            outs[p] = outs[p] * jnp.concatenate(shrinks, axis=0) + dot(
                jnp.concatenate(both, axis=0), value[:, p * PAIR_WIDTH : (p + 1) * PAIR_WIDTH]
            )

    def own_ready(turn):
        for d in (1, 3, 2):
            l_copy(turn, d).wait_recv()
        s_copy(turn).start()

    @pl.when(me.c == 0)
    def _():
        rows_wait(3)

    @pl.when(me.c == 1)
    def _():
        for d in (1, 3, 2):
            f_copy(3, d).wait_recv()

    l_sends(3)

    own_ready(0)
    absorb([base + z_order[0]])

    def expand(turn, carry):
        own_ready(turn)
        s_copy(turn - 1).wait_recv()
        absorb([other + z_at(turn - 1), base + z_at(turn)])
        return carry

    lax.fori_loop(1, 4, expand, 0)
    s_copy(3).wait_recv()
    absorb([other + z_order[3]])

    for p in range(PAIRS_DEV):
        lam_p = lam[p]
        maps = []
        for m in range(2):
            h = 2 * p + m
            inverse = 1.0 / jnp.sum(totals[h], axis=1, keepdims=True)
            totals[h] = jnp.broadcast_to(inverse, (ROWS, 128))
            maps.append(outs[p, m * ROWS : (m + 1) * ROWS] * inverse)
        mixed = maps[0] - lam_p * maps[1]
        inv_root = lax.rsqrt(jnp.mean(mixed * mixed, axis=1, keepdims=True) + EPS)
        normed = mixed * inv_root
        scaled = out_grad[:, p * PAIR_WIDTH : (p + 1) * PAIR_WIDTH].astype(F32) * gain[
            :, p * PAIR_WIDTH : (p + 1) * PAIR_WIDTH
        ]
        d_mixed = (scaled - normed * jnp.mean(scaled * normed, axis=1, keepdims=True)) * inv_root
        lowered[p] = d_mixed.astype(BF16)
        deltas[2 * p] = jnp.broadcast_to(jnp.sum(d_mixed * maps[0], axis=1, keepdims=True), (ROWS, 128))
        deltas[2 * p + 1] = jnp.broadcast_to(
            -lam_p * jnp.sum(d_mixed * maps[1], axis=1, keepdims=True), (ROWS, 128)
        )

    def t_copy(turn):
        return remote(part.at[BACK_STEP[1, turn]], from_s.at[turn], t_send.at[turn], t_recv.at[turn], sibling)

    def p_copy(turn, d):
        rows = part.at[BACK_STEP[0, turn], lax.rem(me.last + d, 4)]
        i = turn * 3 + d - 1
        return remote(rows, from_l.at[turn, d - 1], p_send.at[i], p_recv.at[i], lasts[d])

    def g_copy(turn, d):
        piece = middle.at[turn, lax.rem(me.first + d, 4)]
        i = turn * 3 + d - 1
        return remote(piece, from_f.at[turn, d - 1], g_send.at[i], g_recv.at[i], firsts[d])

    def add_own(turn):
        t_copy(turn).wait_recv()
        there = part.at[BACK_STEP[0, turn]]
        there[...] += from_s[turn]
        for d in (2, 1, 3):
            p_copy(turn, d).start()

    def add_last(turn):
        for d in (1, 3, 2):
            p_copy(turn, d).wait_recv()
        middle[turn] = total_of(
            [part[BACK_STEP[0, turn], me.last]] + [from_l[turn, d] for d in range(3)]
        ).astype(BF16)
        for d in (2, 1, 3):
            g_copy(turn, d).start()

    def chunk_grads(step):
        theirs = pick(step, BACK_SIDE)
        i = base * (1 - theirs) + other * theirs + pick(pick(step, BACK_TURN), z_order)
        d_nope = []
        d_value = []
        d_all = []
        for p in range(PAIRS_DEV):
            lam_p = lam[p]
            grad = lowered[p]
            through = dot(grad, values[i, p], NT)
            probs = []
            for m in range(2):
                h = 2 * p + m
                share = jnp.exp2((tops_then[i, h] - tops[h]) * EXPONENT) * (totals[h] * LOGIT_SCALE)
                probs.append(scores[i, h] * jnp.concatenate([share, share], axis=1))
            merged = probs[0] * (1 / LOGIT_SCALE) - probs[1] * (lam_p * (1 / LOGIT_SCALE))
            d_value.append(dot(merged.astype(BF16), grad, TN).astype(BF16))
            pair = []
            for m in range(2):
                h = 2 * p + m
                delta = jnp.concatenate([deltas[h], deltas[h]], axis=1)
                inner = through if m == 0 else -lam_p * through
                d_score = (probs[m] * (inner - delta)).astype(BF16)
                d_scores[i, h] = d_score
                pair.append(d_score)
            d_nope.append(dot(jnp.concatenate(pair, axis=0), q_nope[p], TN).astype(BF16))
            d_all.extend(pair)
        d_rope = dot(jnp.concatenate(d_all, axis=0), q_rope[...], TN)
        d_latent = dot(jnp.concatenate(d_nope, axis=1), key_weight[...], NT)
        d_latent = d_latent + dot(jnp.concatenate(d_value, axis=1), value_weight[...], NT)
        part[step, :, :, :, 0:D_LAT] = d_latent.astype(BF16).reshape(4, 4, PIECE, D_LAT)
        part[step, :, :, :, D_LAT:WIDE] = d_rope.astype(BF16).reshape(4, 4, PIECE, WIDE - D_LAT)

    def backward(pair, carry):
        chunk_grads(2 * pair)
        chunk_grads(2 * pair + 1)
        for turn in (3, 2, 1, 0):

            @pl.when(pair == BACK_STEP[1, turn] // 2)
            def _(turn=turn):
                t_copy(turn).start()

        for turn in (3, 2):

            @pl.when(pair == BACK_STEP[0, turn] // 2)
            def _(turn=turn):
                add_own(turn)

        return carry

    lax.fori_loop(0, 3, backward, 0)

    def backward_last(step, carry):
        chunk_grads(step)

        @pl.when(step == 6)
        def _():
            add_own(1)

        return carry

    lax.fori_loop(6, 8, backward_last, 0)
    add_own(0)

    def to_queries(i, carry):
        for h in range(MAPS):
            q_acc[h] += dot(d_scores[i, h], k_cat[i, h])
        return carry

    lax.fori_loop(0, CHUNKS, to_queries, 0)
    for h in range(MAPS):
        query_grad[:, h * D_QK : (h + 1) * D_QK] = q_acc[h, :, 0:D_QK].astype(BF16)

    z_mine = me.zh * 2 + me.zl

    def y_copy(turn, zl):
        i = turn * 2 + zl
        device = me.at(zh=z_order[turn], zl=zl)
        return remote(small.at[turn], from_z.at[z_mine], y_send.at[i], y_recv.at[z_mine], device)

    far_y = remote(
        small.at[3], from_far, y_send.at[6], y_recv.at[8], me.at(zh=z_order[3], zl=1 - me.zl)
    )
    mid_y = remote(
        small.at[2], from_z.at[z_mine], y_send.at[4], y_recv.at[z_mine], me.at(zh=z_order[2])
    )
    z_mid = near * 2 + me.zl
    own_y = remote(
        from_z.at[z_mine], from_z.at[z_mine], y_send.at[0], y_recv.at[z_mine], me.at(zl=1 - me.zl)
    )

    def add_first(turn):
        for d in (1, 3, 2):
            g_copy(turn, d).wait_recv()
        small[turn] = total_of(
            [middle[turn, me.first]] + [from_f[turn, d] for d in range(3)]
        ).astype(BF16)
        if turn == 3:
            far_y.start()
        elif turn == 2:
            mid_y.start()
        elif turn:
            for zl in (0, 1):
                y_copy(turn, zl).start()
        else:
            far_y.wait_recv()
            remote(small.at[0], from_z.at[0], y_send.at[0], y_recv.at[z_mid], z_line[0]).wait_recv()
            from_z[z_mine] = total_of([small[0], from_far[...], from_z[z_mid]]).astype(BF16)
            own_y.start()

    add_last(3)
    add_last(2)

    @pl.when(me.c == 0)
    def _():
        rows_copy(2).wait_send()

    @pl.when(me.c == 1)
    def _():
        for i in range(3):
            piece_copy(i).wait_send()
        for turn in range(4):
            for d in (1, 2, 3):
                f_copy(turn, d).wait_send()

    early = [s_copy(turn) for turn in range(4)] + [t_copy(turn) for turn in range(4)]
    early += [l_copy(turn, d) for turn in range(4) for d in (1, 2, 3)]
    early += [p_copy(turn, d) for turn in (3, 2) for d in (1, 2, 3)]
    for copy in early:
        copy.wait_send()
    add_last(1)
    add_first(3)
    add_last(0)
    add_first(2)
    add_first(1)
    add_first(0)
    told = [lax.rem(me.zh + k, 4) * 2 + zl for k, zl in ((0, 0), (0, 1), (1, 0), (3, 1))]
    remote(small.at[0], from_z.at[0], y_send.at[0], y_recv.at[lax.rem(z_mine + 1 - 2 * me.zl + 8, 8)], z_line[0]).wait_recv()
    for z in told[2:]:
        remote(small.at[0], from_z.at[0], y_send.at[0], y_recv.at[z], z_line[0]).wait_recv()
    place = me.c * 4 + me.y
    result[place] = total_of([from_z[z] for z in told]).astype(BF16)

    def e_copy(d):
        piece = result.at[place]
        return remote(piece, piece, e_send.at[d - 1], e_recv.at[d - 1], (y_line + [y_over])[d - 1])

    def r_copy(d):
        piece = result.at[me.c * 4 + lax.rem(me.y + 4 - d, 4)]
        return remote(piece, piece, r_send.at[d], r_recv.at[d], sibling)

    for d in (4, 2, 1, 3):
        e_copy(d).start()
    r_copy(0).start()
    sent = [p_copy(turn, d) for turn in (1, 0) for d in (1, 2, 3)]
    sent += [g_copy(turn, d) for turn in range(4) for d in (1, 2, 3)]
    sent += [y_copy(1, zl) for zl in (0, 1)] + [mid_y, far_y, own_y]
    for copy in sent:
        copy.wait_send()
    for d in (1, 3):
        e_copy(d).wait_recv()
        r_copy(d).start()
    for d in (2, 4):
        e_copy(d).wait_recv()
    for d in (0, 1, 3):
        r_copy(d).wait_recv()
    for copy in [e_copy(d) for d in (1, 2, 3, 4)] + [r_copy(d) for d in (0, 1, 3)]:
        copy.wait_send()


def copy_out(query, result, query_out, latent_out, rope_out, latent, rope, sem):
    writes = [
        pltpu.make_async_copy(query, query_out, sem.at[0]),
        pltpu.make_async_copy(latent, latent_out, sem.at[1]),
        pltpu.make_async_copy(rope, rope_out, sem.at[2]),
    ]
    writes[0].start()
    everything = result[...].reshape(ROWS, WIDE)
    rope[...] = everything[:, D_LAT:WIDE].astype(F32).T[0:D_ROPE].astype(BF16)
    writes[2].start()
    latent[...] = everything[:, 0:D_LAT]
    writes[1].start()
    for write in writes:
        write.wait()


VMEM = pl.BlockSpec(memory_space=pltpu.VMEM)
SMEM = pl.BlockSpec(memory_space=pltpu.SMEM)
ANY = pl.BlockSpec(memory_space=pl.ANY)
HBM = pl.BlockSpec(memory_space=pltpu.HBM)
DMA = pltpu.SemaphoreType.DMA


OUTS = (
    jax.ShapeDtypeStruct((ROWS, MAPS * D_QK), BF16),
    jax.ShapeDtypeStruct((ROWS, D_LAT), BF16),
    jax.ShapeDtypeStruct((D_ROPE, ROWS), BF16),
)


def fused(*operands):
    piece = (PIECE, WIDE)
    outs = pl.pallas_call(
        fused_kernel,
        out_shape=(pltpu.VMEM(OUTS[0].shape, BF16), pltpu.VMEM((8,) + piece, BF16)),
        in_specs=[HBM] * 9,
        out_specs=(VMEM, VMEM),
        scratch_shapes=[
            pltpu.SMEM((PAIRS_DEV,), F32),
            pltpu.SMEM((32,), jnp.int32),
            pltpu.VMEM((1, 512), F32),
            pltpu.VMEM((ROWS, MAPS * D_QK), BF16),
            pltpu.VMEM((D_ROPE, ROWS), BF16),
            pltpu.VMEM((8, PIECE, 128), BF16),
            pltpu.VMEM((D_LAT, 512), BF16),
            pltpu.VMEM((D_LAT, 512), BF16),
            pltpu.VMEM((ROWS, 512), BF16),
            pltpu.VMEM((CHUNKS, 4, 4) + piece, BF16),
            pltpu.VMEM((CHUNKS, CHUNK), jnp.int32),
            pltpu.VMEM((ROWS, CHUNK), jnp.int32),
            pltpu.VMEM((MAPS, ROWS, 256), BF16),
            pltpu.VMEM((PAIRS_DEV, 2 * ROWS, 2 * D_NOPE), BF16),
            pltpu.VMEM((MAPS * ROWS, 128), BF16),
            pltpu.VMEM((CHUNKS, MAPS, CHUNK, 256), BF16),
            pltpu.VMEM((CHUNKS, PAIRS_DEV, CHUNK, PAIR_WIDTH), BF16),
            pltpu.VMEM((CHUNKS, MAPS, ROWS, CHUNK), F32),
            pltpu.VMEM((CHUNKS, MAPS, ROWS, CHUNK), BF16),
            pltpu.VMEM((MAPS, ROWS, 128), F32),
            pltpu.VMEM((CHUNKS, MAPS, ROWS, 128), F32),
            pltpu.VMEM((PAIRS_DEV, 2 * ROWS, PAIR_WIDTH), F32),
            pltpu.VMEM((MAPS, ROWS, 128), F32),
            pltpu.VMEM((PAIRS_DEV, ROWS, PAIR_WIDTH), BF16),
            pltpu.VMEM((MAPS, ROWS, 128), F32),
            pltpu.VMEM((MAPS, ROWS, 256), F32),
            pltpu.VMEM((CHUNKS, 4, 4) + piece, BF16),
            pltpu.VMEM((4, 4, 4) + piece, BF16),
            pltpu.VMEM((4, 3, 4) + piece, BF16),
            pltpu.VMEM((4, 4) + piece, BF16),
            pltpu.VMEM((4, 3) + piece, BF16),
            pltpu.VMEM((4,) + piece, BF16),
            pltpu.VMEM((8,) + piece, BF16),
            pltpu.VMEM(piece, BF16),
        ]
        + [DMA((n,)) for n in (9, 12, 12, 3, 4, 12, 12, 4, 4, 4, 4, 12, 12, 12, 12, 8, 9, 4, 4, 4, 4)],
        compiler_params=pltpu.CompilerParams(
            collective_id=0, has_side_effects=True, vmem_limit_bytes=56 << 20
        ),
        name="fused",
    )(*(pltpu.with_memory_space_constraint(operand, pltpu.HBM) for operand in operands))
    return pl.pallas_call(
        copy_out,
        out_shape=OUTS,
        in_specs=[VMEM] * 2,
        out_specs=(HBM, HBM, HBM),
        scratch_shapes=[pltpu.VMEM(out.shape, BF16) for out in OUTS[1:]] + [DMA((3,))],
        name="copy_out",
    )(*(pltpu.with_memory_space_constraint(out, pltpu.VMEM) for out in outs))


def on_device(
    queries, latent, rope_key, key_weight, value_weight, lambda_pair, norm_gain, out_grad, block_order
):
    query_grad, latent_grad, rope_grad = fused(
        lambda_pair, block_order, norm_gain.reshape(1, -1), queries, latent.reshape(8, PIECE, D_LAT), rope_key.T,
        key_weight, value_weight, out_grad,
    )
    return (query_grad, latent_grad, rope_grad.T)


def solution(mesh):
    return jax.shard_map(
        on_device,
        mesh=mesh,
        in_specs=(
            P("ctx", "head"),
            P("ctx", None),
            P("ctx", None),
            P(None, "head"),
            P(None, "head"),
            P("head"),
            P("head"),
            P("ctx", "head"),
            P(),
        ),
        out_specs=(P("ctx", "head"), P("ctx", None), P("ctx", None)),
        check_vma=False,
    )
```
